32 devices in a mesh: dp: 16 (over z, x, core), mp: 2 (over y).
Axes of the slice: x: 2, y: 2, z: 4, core: 2. Of those that a mesh axis runs over, the one named last changes fastest.
Arguments:
- enc_in: bfloat16 [32, 128, 768], P('dp'), may hold values from -6 to 6
- dec_in: bfloat16 [32, 64, 768], P('dp'), may hold values from -6 to 6
- cotangent: bfloat16 [32, 64, 768], P('dp'), may hold values from -6 to 6
- patch_counts: int32 [32], P('dp'), may hold values from 32 to 128, as said below
- table_lengths: int32 [32], P('dp'), may hold values from 40 to 64, as said below
- enc_qkv: bfloat16 [3, 768, 768], P(None, None, 'mp'), may hold values from -0.21875 to 0.21875
- enc_attn_out: bfloat16 [768, 768], P('mp'), may hold values from -1.25 to 1.25
- enc_mlp_in: bfloat16 [2, 768, 2048], P(None, None, 'mp'), may hold values from -0.21875 to 0.21875
- enc_mlp_out: bfloat16 [2048, 768], P('mp'), may hold values from -0.125 to 0.125
- enc_gains: float32 [3, 768], replicated, may hold values from 0.5 to 1.5
- dec_self_qkv: bfloat16 [3, 768, 768], P(None, None, 'mp'), may hold values from -0.21875 to 0.21875
- dec_self_out: bfloat16 [768, 768], P('mp'), may hold values from -1.25 to 1.25
- dec_cross_qkv: bfloat16 [3, 768, 768], P(None, None, 'mp'), may hold values from -0.21875 to 0.21875
- dec_cross_out: bfloat16 [768, 768], P('mp'), may hold values from -1.25 to 1.25
- dec_mlp_in: bfloat16 [2, 768, 2048], P(None, None, 'mp'), may hold values from -0.21875 to 0.21875
- dec_mlp_out: bfloat16 [2048, 768], P('mp'), may hold values from -0.125 to 0.125
- dec_gains: float32 [3, 768], replicated, may hold values from 0.5 to 1.5
Outputs:
- dec_out: bfloat16 [32, 64, 768], P('dp')
- enc_in_grad: bfloat16 [32, 128, 768], P('dp')
- dec_in_grad: bfloat16 [32, 64, 768], P('dp')
- enc_qkv_grad: float32 [3, 768, 768], P(None, 'dp', 'mp')
- enc_attn_out_grad: float32 [768, 768], P('mp', 'dp')
- enc_mlp_in_grad: float32 [2, 768, 2048], P(None, 'dp', 'mp')
- enc_mlp_out_grad: float32 [2048, 768], P('mp', 'dp')
- enc_gains_grad: float32 [3, 768], P(None, 'dp')
- dec_self_qkv_grad: float32 [3, 768, 768], P(None, 'dp', 'mp')
- dec_self_out_grad: float32 [768, 768], P('mp', 'dp')
- dec_cross_qkv_grad: float32 [3, 768, 768], P(None, 'dp', 'mp')
- dec_cross_out_grad: float32 [768, 768], P('mp', 'dp')
- dec_mlp_in_grad: float32 [2, 768, 2048], P(None, 'dp', 'mp')
- dec_mlp_out_grad: float32 [2048, 768], P('mp', 'dp')
- dec_gains_grad: float32 [3, 768], P(None, 'dp')
The draws below stay inside these ranges and needn't reach their ends.
Inputs may be any that keep to these rules, and one draw needn't show every extreme that they name: `patch_counts`: rows at or past a plot's count are padding that no query reads as a key; some plot has exactly 128 and another exactly 32. `table_lengths`: rows at or past a plot's length are padding that no query reads as a key; some plot has exactly 64 and another exactly 40.
All inputs are finite; a program needn't handle non-finite values.
Results may differ from the reference program's by a relative error of at most 0.02.
Values sent between devices are 32-bit elements; how exact they have to be, the bound alone decides.
No kernel may reach another device: no remote copies, remote signals or barrier semaphores. Data moves between devices by JAX's collectives and lax.ppermute only.
A program may use at most 192 MiB of HBM per device.

```python
import jax
import jax.numpy as jnp
from jax import lax

D = 768
HEADS = 12
HEAD_DIM = 64
FF = 2048
ENC = 128
DEC = 64
MIN_TABLE = 40
PLOTS = 32


def pick_places(key):
    first = jax.random.randint(jax.random.fold_in(key, 11), (), 0, PLOTS)
    second = (first + 1 + jax.random.randint(jax.random.fold_in(key, 12), (), 0, PLOTS - 1)) % PLOTS
    return (first, second)


def draw_patch_counts(key, part):
    key = jax.random.fold_in(key, 3)
    least = ENC // 4
    counts = least + jax.random.randint(jax.random.fold_in(key, 1), (PLOTS,), 0, ENC - least + 1)
    first, second = pick_places(key)
    counts = counts.at[first].set(ENC).at[second].set(least)
    return counts.astype(jnp.int32)


def draw_table_lengths(key, part):
    key = jax.random.fold_in(key, 5)
    draws = jax.random.randint(jax.random.fold_in(key, 1), (3, PLOTS), 0, DEC - MIN_TABLE + 1)
    lengths = MIN_TABLE + jnp.min(draws, 0)
    first, second = pick_places(key)
    lengths = lengths.at[first].set(DEC).at[second].set(MIN_TABLE)
    return lengths.astype(jnp.int32)


def raised(values, own_key, source, target, blocks, factor):
    owner, partner = [(jnp.arange(values.shape[dim]) // (values.shape[dim] // blocks)).reshape([-1 if axis == dim else 1 for axis in range(values.ndim)]) for dim in (source, target)]
    chosen = jax.random.permutation(own_key, blocks)[partner]
    strong = (owner == chosen) | (owner == (partner + blocks // 2) % blocks)
    return jnp.where(strong, factor * values, values)


def steps_of(own_key, extent, shards, low, largest):
    loudness = 1.0
    for dim, shards_of in shards:
        steps = jax.random.uniform(jax.random.fold_in(jax.random.fold_in(own_key, 6), dim), (shards_of,), jnp.float32, low / len(shards), largest / len(shards))
        loudness = loudness * jnp.repeat(jnp.exp(steps), extent[dim] // shards_of).reshape((-1,) + (1,) * (len(extent) - 1 - dim))
    return loudness


def gaussian(stream_key, dims, spread, limit, cuts=(), dtype=jnp.bfloat16):
    drawn = jax.random.normal(stream_key, dims, jnp.float32) * spread
    if len(cuts) > 0:
        drawn = steps_of(stream_key, dims, cuts, -0.22, 0.18) * drawn
    return jnp.clip(drawn, min=-limit, max=limit).astype(dtype)


def gaussian_with(key, extent, scale, most, split, heavy, kind=jnp.bfloat16):
    drawn = scale * jax.random.normal(key, extent, jnp.float32)
    if split:
        drawn = drawn * steps_of(key, extent, split, -0.22, 0.18)
    return jnp.clip(raised(drawn, jax.random.fold_in(key, 3), *heavy), -most, most).astype(kind)


def setup_inputs(seed: int = 0) -> dict:
    key_of = jax.random.split(jax.random.key(seed), 18)
    return {
        "enc_in": gaussian(key_of[0], (PLOTS, ENC, D), 1.0, 6.0, ((0, 16),)),
        "dec_in": gaussian(key_of[1], (PLOTS, DEC, D), 1.0, 6.0, ((0, 16),)),
        "cotangent": gaussian_with(key_of[2], (PLOTS, DEC, D), 1.0, 6.0, ((0, 16),), (0, 2, 16, 2.0)),
        "patch_counts": draw_patch_counts(jax.random.fold_in(key_of[17], 71), 0),
        "table_lengths": draw_table_lengths(jax.random.fold_in(key_of[17], 71), 0),
        "enc_qkv": gaussian(key_of[5], (3, D, D), D ** -0.5, 0.21875, ((2, 2),)),
        "enc_attn_out": gaussian(key_of[6], (D, D), (D // 32) ** -0.5, 1.25, ((0, 2),)),
        "enc_mlp_in": gaussian(key_of[7], (2, D, FF), D ** -0.5, 0.21875, ((2, 2),)),
        "enc_mlp_out": gaussian(key_of[8], (FF, D), FF ** -0.5, 0.125, ((0, 2),)),
        "enc_gains": jnp.clip(1.0 + 0.1 * jax.random.normal(key_of[9], (3, D), jnp.float32), 0.5, 1.5),
        "dec_self_qkv": gaussian(key_of[10], (3, D, D), D ** -0.5, 0.21875, ((2, 2),)),
        "dec_self_out": gaussian(key_of[11], (D, D), (D // 32) ** -0.5, 1.25, ((0, 2),)),
        "dec_cross_qkv": gaussian(key_of[12], (3, D, D), D ** -0.5, 0.21875, ((2, 2),)),
        "dec_cross_out": gaussian(key_of[13], (D, D), (D // 32) ** -0.5, 1.25, ((0, 2),)),
        "dec_mlp_in": gaussian(key_of[14], (2, D, FF), D ** -0.5, 0.21875, ((2, 2),)),
        "dec_mlp_out": gaussian(key_of[15], (FF, D), FF ** -0.5, 0.125, ((0, 2),)),
        "dec_gains": jnp.clip(1.0 + 0.1 * jax.random.normal(key_of[16], (3, D), jnp.float32), 0.5, 1.5),
    }


EPSILON = 1e-06
NEG_LARGE = -1e+30

@jax.custom_vjp
def low(v):
    return lax.optimization_barrier(v.astype(jnp.bfloat16)).astype(jnp.float32)

@jax.custom_vjp
def low_back(v):
    return v

def low_keep(v):
    return (low(v), None)

def low_pass(kept, grad):
    return (grad,)

def back_keep(v):
    return (v, None)

def back_low(kept, grad):
    return (low(grad),)
low.defvjp(low_keep, low_pass)
low_back.defvjp(back_keep, back_low)

def matmul(left, right):
    return jnp.dot(left, right, precision=lax.Precision.HIGHEST, preferred_element_type=jnp.float32)

def norm_rows(hidden, gain):
    return hidden * lax.rsqrt(lax.optimization_barrier(jnp.mean(hidden * hidden, -1, keepdims=True)) + EPSILON) * gain

def sub_attention(normed_q, normed_kv, stacked, out_weight, allowed):
    seq_q = normed_q.shape[0]
    seq_k = normed_kv.shape[0]
    query = low(low_back(matmul(normed_q, stacked[0]))).reshape(seq_q, HEADS, HEAD_DIM)
    keys = low(low_back(matmul(normed_kv, stacked[1]))).reshape(seq_k, HEADS, HEAD_DIM)
    values = low(low_back(matmul(normed_kv, stacked[2]))).reshape(seq_k, HEADS, HEAD_DIM)
    raw_scores = low_back(jnp.einsum('qhd,khd->hqk', query, keys, precision=lax.Precision.HIGHEST) * HEAD_DIM ** (-0.5))
    scores = jnp.where(allowed[None], raw_scores, NEG_LARGE)
    soft = jax.nn.softmax(scores, axis=-1)
    attended = jnp.einsum('hqk,khd->qhd', low(soft), values, precision=lax.Precision.HIGHEST).reshape(seq_q, HEADS * HEAD_DIM)
    attended = low(low_back(attended))
    return low_back(matmul(attended, out_weight))

def sub_mlp(normed, inner, outer):
    gate_pre = low_back(matmul(normed, inner[0]))
    up_pre = low_back(matmul(normed, inner[1]))
    hidden_low = low(jax.nn.gelu(gate_pre, approximate=True) * up_pre)
    return low_back(matmul(hidden_low, outer))

def layer_pair(weights, enc_rows, dec_rows, patches, table):
    enc_qkv, enc_attn_out, enc_mlp_in, enc_mlp_out, enc_gains, dec_self_qkv, dec_self_out, dec_cross_qkv, dec_cross_out, dec_mlp_in, dec_mlp_out, dec_gains = weights
    enc_pos = jnp.arange(ENC)
    dec_pos = jnp.arange(DEC)
    enc_allowed = jnp.broadcast_to(enc_pos[None, :] < patches, (ENC, ENC))
    self_allowed = (dec_pos[None, :] <= dec_pos[:, None]) & (dec_pos[None, :] < table)
    cross_allowed = jnp.broadcast_to(enc_pos[None, :] < patches, (DEC, ENC))
    normed = low(norm_rows(enc_rows, enc_gains[0]))
    state = enc_rows + sub_attention(normed, normed, enc_qkv, enc_attn_out, enc_allowed)
    normed = low(norm_rows(state, enc_gains[1]))
    state = state + sub_mlp(normed, enc_mlp_in, enc_mlp_out)
    memory = low(norm_rows(state, enc_gains[2]))
    normed = low(norm_rows(dec_rows, dec_gains[0]))
    stream = dec_rows + sub_attention(normed, normed, dec_self_qkv, dec_self_out, self_allowed)
    normed = low(norm_rows(stream, dec_gains[1]))
    stream = stream + sub_attention(normed, memory, dec_cross_qkv, dec_cross_out, cross_allowed)
    normed = low(norm_rows(stream, dec_gains[2]))
    return stream + sub_mlp(normed, dec_mlp_in, dec_mlp_out)

def reference(enc_in, dec_in, cotangent, patch_counts, table_lengths, enc_qkv, enc_attn_out, enc_mlp_in, enc_mlp_out, enc_gains, dec_self_qkv, dec_self_out, dec_cross_qkv, dec_cross_out, dec_mlp_in, dec_mlp_out, dec_gains):
    weights = tuple((w.astype(jnp.float32) for w in (enc_qkv, enc_attn_out, enc_mlp_in, enc_mlp_out, enc_gains, dec_self_qkv, dec_self_out, dec_cross_qkv, dec_cross_out, dec_mlp_in, dec_mlp_out, dec_gains)))

    def one_plot(totals, item):
        enc_rows, dec_rows, grad_rows, patches, table = item

        def forward(params, enc_part, dec_part):
            return layer_pair(params, enc_part, dec_part, patches, table)
        output, pull = jax.vjp(forward, weights, enc_rows.astype(jnp.float32), dec_rows.astype(jnp.float32))
        grad_weights, grad_enc, grad_dec = pull(grad_rows.astype(jnp.float32))
        totals = jax.tree.map(jnp.add, totals, grad_weights)
        return (totals, (output.astype(jnp.bfloat16), grad_enc.astype(jnp.bfloat16), grad_dec.astype(jnp.bfloat16)))
    zeros = jax.tree.map(jnp.zeros_like, weights)
    grads, (outputs, enc_grads, dec_grads) = lax.scan(one_plot, zeros, (enc_in, dec_in, cotangent, patch_counts, table_lengths))
    return (outputs, enc_grads, dec_grads) + tuple(grads)
```

```python
import jax
import jax.numpy as jnp
from jax import lax
from jax.sharding import PartitionSpec as P

HEAD_DIM = 64


EPSILON = 1e-06
NEG_LARGE = -1e30


def project(left, right):
    return jnp.dot(left, right, preferred_element_type=jnp.float32)


def project_back(left, right):
    return jnp.einsum("sd,ed->se", left, right, preferred_element_type=jnp.float32)


def outer_sum(left, right):
    return jnp.einsum("sd,se->de", left, right, preferred_element_type=jnp.float32)


def norm_rows(hidden, gain):
    scaling = lax.rsqrt(jnp.mean(hidden * hidden, -1, keepdims=True) + EPSILON)
    return (hidden * scaling * gain, scaling)


def norm_back(grad, hidden, scaling, gain):
    normed = hidden * scaling
    grad_hat = grad * gain
    grad_in = scaling * (grad_hat - normed * jnp.mean(grad_hat * normed, -1, keepdims=True))
    return (grad_in, jnp.sum(grad * normed, 0))


def heads_of(tensor):
    return tensor.reshape(tensor.shape[0], -1, HEAD_DIM)


def scores_of(query, keys, allowed):
    raw_scores = jnp.einsum(
        "qhd,khd->hqk", heads_of(query), heads_of(keys), preferred_element_type=jnp.float32
    ) * HEAD_DIM ** (-0.5)
    return jnp.where(allowed[None], raw_scores, NEG_LARGE)


def attend_fwd(query, keys, values, allowed):
    scores = scores_of(query, keys, allowed)
    row_max = jnp.max(scores, -1, keepdims=True)
    expon = jnp.exp(scores - row_max)
    row_sum = jnp.sum(expon, -1, keepdims=True)
    soft_low = (expon / row_sum).astype(jnp.bfloat16)
    mixed_heads = jnp.einsum(
        "hqk,khd->qhd", soft_low, heads_of(values), preferred_element_type=jnp.float32
    )
    return (mixed_heads.reshape(query.shape[0], -1), row_max + jnp.log(row_sum))


def attend_back(query, keys, values, allowed, log_sum, grad_out):
    scores = scores_of(query, keys, allowed)
    soft = jnp.exp(scores - log_sum)
    grad_heads = heads_of(grad_out)
    grad_values = jnp.einsum(
        "hqk,qhd->khd", soft.astype(jnp.bfloat16), grad_heads, preferred_element_type=jnp.float32
    )
    grad_soft = jnp.einsum(
        "qhd,khd->hqk", grad_heads, heads_of(values), preferred_element_type=jnp.float32
    )
    grad_scores = (soft * (grad_soft - jnp.sum(soft * grad_soft, -1, keepdims=True))).astype(
        jnp.bfloat16
    )
    factor = HEAD_DIM ** (-0.5)
    grad_query = (
        jnp.einsum("hqk,khd->qhd", grad_scores, heads_of(keys), preferred_element_type=jnp.float32)
        * factor
    )
    grad_keys = (
        jnp.einsum("hqk,qhd->khd", grad_scores, heads_of(query), preferred_element_type=jnp.float32)
        * factor
    )
    grad_query = grad_query.reshape(query.shape[0], -1).astype(jnp.bfloat16)
    grad_keys = grad_keys.reshape(keys.shape[0], -1).astype(jnp.bfloat16)
    grad_values = grad_values.reshape(keys.shape[0], -1).astype(jnp.bfloat16)
    return (grad_query, grad_keys, grad_values)


def attention_fwd(normed_q, normed_kv, stacked, allowed):
    query = project(normed_q, stacked[0]).astype(jnp.bfloat16)
    keys = project(normed_kv, stacked[1]).astype(jnp.bfloat16)
    values = project(normed_kv, stacked[2]).astype(jnp.bfloat16)
    attended, log_sum = attend_fwd(query, keys, values, allowed)
    attended = attended.astype(jnp.bfloat16)
    return (attended, (query, keys, values, log_sum, attended))


def attention_back(grad, normed_q, normed_kv, stacked, out_weight, saved, allowed):
    query, keys, values, log_sum, attended = saved
    grad_low = grad.astype(jnp.bfloat16)
    grad_out_weight = outer_sum(attended, grad_low)
    grad_attended = project_back(grad_low, out_weight).astype(jnp.bfloat16)
    grad_query, grad_keys, grad_values = attend_back(
        query, keys, values, allowed, log_sum, grad_attended
    )
    grad_stack = jnp.stack(
        [
            outer_sum(normed_q, grad_query),
            outer_sum(normed_kv, grad_keys),
            outer_sum(normed_kv, grad_values),
        ]
    )
    from_query = project_back(grad_query, stacked[0])
    from_memory = project_back(grad_keys, stacked[1]) + project_back(grad_values, stacked[2])
    return (grad_stack, grad_out_weight, from_query, from_memory)


def gated(gate_pre, up_pre):
    return jax.nn.gelu(gate_pre, approximate=True) * up_pre


def mlp_fwd(normed, inner):
    gate_pre = project(normed, inner[0])
    up_pre = project(normed, inner[1])
    hidden_low = gated(gate_pre, up_pre).astype(jnp.bfloat16)
    return (hidden_low, (gate_pre, up_pre, hidden_low))


def mlp_back(grad, normed, inner, outer, saved):
    gate_pre, up_pre, hidden_low = saved
    grad_low = grad.astype(jnp.bfloat16)
    grad_outer = outer_sum(hidden_low, grad_low)
    grad_hidden = project_back(grad_low, outer)
    unused, pull = jax.vjp(gated, gate_pre, up_pre)
    grad_gate, grad_up = pull(grad_hidden)
    grad_gate = grad_gate.astype(jnp.bfloat16)
    grad_up = grad_up.astype(jnp.bfloat16)
    grad_inner = jnp.stack([outer_sum(normed, grad_gate), outer_sum(normed, grad_up)])
    grad_normed = project_back(grad_gate, inner[0]) + project_back(grad_up, inner[1])
    return (grad_inner, grad_outer, grad_normed)


def pair_sum(partial_sum):
    shards = lax.axis_size("mp")
    if shards == 2:
        return partial_sum + lax.ppermute(partial_sum, "mp", [(0, 1), (1, 0)])
    return lax.psum(partial_sum, "mp")


branch_sum = pair_sum
input_sum = pair_sum


def scatter_sum(grads, cut_dims):
    shards = lax.axis_size("dp")
    me = lax.axis_index("dp")
    bits = shards.bit_length() - 1
    rows = []
    for grad, cut in zip(grads, cut_dims):
        moved = jnp.moveaxis(grad, cut, 0)
        rows.append(moved.reshape(moved.shape[0], -1))
    total = jnp.concatenate(rows, 1)
    width = total.shape[1]
    total = total.reshape((2,) * bits + (-1, width))
    for bit in range(bits):
        axis = bits - 1 - bit
        mine = (me >> bit) & 1
        sent = lax.dynamic_index_in_dim(total, 1 - mine, axis, keepdims=False)
        kept = lax.dynamic_index_in_dim(total, mine, axis, keepdims=False)
        total = kept + lax.ppermute(sent, "dp", [(i, i ^ (1 << bit)) for i in range(shards)])
    outs = []
    at = 0
    for grad, cut in zip(grads, cut_dims):
        moved = jnp.moveaxis(grad, cut, 0)
        size = moved.size // moved.shape[0]
        piece = lax.slice_in_dim(total, at, at + size, axis=1).reshape((total.shape[0],) + moved.shape[1:])
        at += size
        outs.append(jnp.moveaxis(piece, 0, cut))
    return outs


def body(
    enc_in,
    dec_in,
    cotangent,
    patch_counts,
    table_lengths,
    enc_qkv,
    enc_attn_out,
    enc_mlp_in,
    enc_mlp_out,
    enc_gains,
    dec_self_qkv,
    dec_self_out,
    dec_cross_qkv,
    dec_cross_out,
    dec_mlp_in,
    dec_mlp_out,
    dec_gains,
):
    micro = enc_in.shape[0]
    enc_len = enc_in.shape[1]
    dec_len = dec_in.shape[1]
    enc_pos = jnp.arange(enc_len)
    dec_pos = jnp.arange(dec_len)
    enc_params = (enc_qkv, enc_attn_out, enc_mlp_in, enc_mlp_out, enc_gains)
    dec_params = (
        dec_self_qkv,
        dec_self_out,
        dec_cross_qkv,
        dec_cross_out,
        dec_mlp_in,
        dec_mlp_out,
        dec_gains,
    )
    enc_accum = [jnp.zeros(weight.shape, jnp.float32) for weight in enc_params]
    dec_accum = [jnp.zeros(weight.shape, jnp.float32) for weight in dec_params]
    outputs = []
    enc_grads = []
    dec_grads = []
    for step in range(micro):
        patches = patch_counts[step]
        table = table_lengths[step]
        enc_allowed = jnp.broadcast_to(enc_pos[None, :] < patches, (enc_len, enc_len))
        self_allowed = (dec_pos[None, :] <= dec_pos[:, None]) & (dec_pos[None, :] < table)
        cross_allowed = jnp.broadcast_to(enc_pos[None, :] < patches, (dec_len, enc_len))
        state_zero = enc_in[step].astype(jnp.float32)
        normed, scale_zero = norm_rows(state_zero, enc_gains[0])
        enc_norm_zero = normed.astype(jnp.bfloat16)
        attended, enc_attn_saved = attention_fwd(enc_norm_zero, enc_norm_zero, enc_qkv, enc_allowed)
        state_one = state_zero + branch_sum(project(attended, enc_attn_out))
        normed, scale_one = norm_rows(state_one, enc_gains[1])
        enc_norm_one = normed.astype(jnp.bfloat16)
        hidden_low, enc_mlp_saved = mlp_fwd(enc_norm_one, enc_mlp_in)
        state_two = state_one + branch_sum(project(hidden_low, enc_mlp_out))
        normed, scale_two = norm_rows(state_two, enc_gains[2])
        memory = normed.astype(jnp.bfloat16)
        stream_zero = dec_in[step].astype(jnp.float32)
        normed, dscale_zero = norm_rows(stream_zero, dec_gains[0])
        dec_norm_zero = normed.astype(jnp.bfloat16)
        attended, self_saved = attention_fwd(
            dec_norm_zero, dec_norm_zero, dec_self_qkv, self_allowed
        )
        stream_one = stream_zero + branch_sum(project(attended, dec_self_out))
        normed, dscale_one = norm_rows(stream_one, dec_gains[1])
        dec_norm_one = normed.astype(jnp.bfloat16)
        attended, cross_saved = attention_fwd(dec_norm_one, memory, dec_cross_qkv, cross_allowed)
        stream_two = stream_one + branch_sum(project(attended, dec_cross_out))
        normed, dscale_two = norm_rows(stream_two, dec_gains[2])
        dec_norm_two = normed.astype(jnp.bfloat16)
        hidden_low, dec_mlp_saved = mlp_fwd(dec_norm_two, dec_mlp_in)
        stream_three = stream_two + branch_sum(project(hidden_low, dec_mlp_out))
        outputs.append(stream_three.astype(jnp.bfloat16))
        grad = cotangent[step].astype(jnp.float32)
        grad_inner, grad_outer, partial_grad = mlp_back(
            grad, dec_norm_two, dec_mlp_in, dec_mlp_out, dec_mlp_saved
        )
        grad_in, gain_two = norm_back(input_sum(partial_grad), stream_two, dscale_two, dec_gains[2])
        grad = grad + grad_in
        dec_accum[4] = dec_accum[4] + grad_inner
        dec_accum[5] = dec_accum[5] + grad_outer
        grad_stack, grad_out_weight, from_query, from_memory = attention_back(
            grad, dec_norm_one, memory, dec_cross_qkv, dec_cross_out, cross_saved, cross_allowed
        )
        full_query, full_memory = pair_sum(from_query), pair_sum(from_memory)
        grad_in, gain_one = norm_back(full_query, stream_one, dscale_one, dec_gains[1])
        grad = grad + grad_in
        dec_accum[2] = dec_accum[2] + grad_stack
        dec_accum[3] = dec_accum[3] + grad_out_weight
        grad_stack, grad_out_weight, from_query, from_memory = attention_back(
            grad, dec_norm_zero, dec_norm_zero, dec_self_qkv, dec_self_out, self_saved, self_allowed
        )
        grad_in, gain_zero = norm_back(
            input_sum(from_query + from_memory), stream_zero, dscale_zero, dec_gains[0]
        )
        grad = grad + grad_in
        dec_accum[0] = dec_accum[0] + grad_stack
        dec_accum[1] = dec_accum[1] + grad_out_weight
        dec_accum[6] = dec_accum[6] + jnp.stack([gain_zero, gain_one, gain_two])
        dec_grads.append(grad.astype(jnp.bfloat16))
        back_state, egain_two = norm_back(full_memory, state_two, scale_two, enc_gains[2])
        grad_inner, grad_outer, partial_grad = mlp_back(
            back_state, enc_norm_one, enc_mlp_in, enc_mlp_out, enc_mlp_saved
        )
        grad_in, egain_one = norm_back(input_sum(partial_grad), state_one, scale_one, enc_gains[1])
        back_state = back_state + grad_in
        enc_accum[2] = enc_accum[2] + grad_inner
        enc_accum[3] = enc_accum[3] + grad_outer
        grad_stack, grad_out_weight, from_query, from_memory = attention_back(
            back_state,
            enc_norm_zero,
            enc_norm_zero,
            enc_qkv,
            enc_attn_out,
            enc_attn_saved,
            enc_allowed,
        )
        grad_in, egain_zero = norm_back(
            input_sum(from_query + from_memory), state_zero, scale_zero, enc_gains[0]
        )
        back_state = back_state + grad_in
        enc_accum[0] = enc_accum[0] + grad_stack
        enc_accum[1] = enc_accum[1] + grad_out_weight
        enc_accum[4] = enc_accum[4] + jnp.stack([egain_zero, egain_one, egain_two])
        enc_grads.append(back_state.astype(jnp.bfloat16))
    dec_mlp = scatter_sum(dec_accum[4:6], (1, 1))
    dec_cross = scatter_sum(dec_accum[2:4], (1, 1))
    dec_self = scatter_sum(dec_accum[0:2], (1, 1))
    enc_mlp = scatter_sum(enc_accum[2:4], (1, 1))
    enc_attn = scatter_sum(enc_accum[0:2], (1, 1))
    gains = scatter_sum([enc_accum[4], dec_accum[6]], (1, 1))
    reduced = tuple(
        enc_attn + enc_mlp + gains[:1] + dec_self + dec_cross + dec_mlp + gains[1:]
    )
    return (jnp.stack(outputs), jnp.stack(enc_grads), jnp.stack(dec_grads)) + reduced


def solution(mesh):
    placed = (
        P("dp", None, None),
        P("dp", None, None),
        P("dp", None, None),
        P("dp"),
        P("dp"),
        P(None, None, "mp"),
        P("mp", None),
        P(None, None, "mp"),
        P("mp", None),
        P(),
        P(None, None, "mp"),
        P("mp", None),
        P(None, None, "mp"),
        P("mp", None),
        P(None, None, "mp"),
        P("mp", None),
        P(),
    )
    return jax.shard_map(
        body,
        mesh=mesh,
        in_specs=placed,
        out_specs=(
            P("dp", None, None),
            P("dp", None, None),
            P("dp", None, None),
            P(None, "dp", "mp"),
            P("mp", "dp"),
            P(None, "dp", "mp"),
            P("mp", "dp"),
            P(None, "dp"),
            P(None, "dp", "mp"),
            P("mp", "dp"),
            P(None, "dp", "mp"),
            P("mp", "dp"),
            P(None, "dp", "mp"),
            P("mp", "dp"),
            P(None, "dp"),
        ),
        check_vma=False,
    )
```

```python
import functools

import jax
import jax.numpy as jnp
from jax import lax
from jax.experimental import pallas as pl
from jax.experimental.pallas import tpu as pltpu
from jax.sharding import PartitionSpec as P

HEAD_DIM = 64
PAIR = 2 * HEAD_DIM
EPSILON = 1e-06
NEG_LARGE = -1e30
SCALE = HEAD_DIM ** (-0.5)
BF = jnp.bfloat16
F32 = jnp.float32
MIB = 1024 * 1024


def mm(left, right):
    return jnp.dot(left, right, preferred_element_type=F32)


def mm_nt(left, right):
    return lax.dot_general(left, right, (((1,), (1,)), ((), ())), preferred_element_type=F32)


def mm_tn(left, right):
    return lax.dot_general(left, right, (((0,), (0,)), ((), ())), preferred_element_type=F32)


def norm(hidden, gain):
    scaling = lax.rsqrt(jnp.mean(hidden * hidden, -1, keepdims=True) + EPSILON)
    return (hidden * scaling * gain).astype(BF)


def norm_back(grad, hidden, gain):
    scaling = lax.rsqrt(jnp.mean(hidden * hidden, -1, keepdims=True) + EPSILON)
    normed = hidden * scaling
    grad_hat = grad * gain
    grad_in = scaling * (grad_hat - normed * jnp.mean(grad_hat * normed, -1, keepdims=True))
    return grad_in, jnp.sum(grad * normed, 0, keepdims=True)


def gelu_parts(gate):
    slope = 0.7978845608028654
    square = gate * gate
    bent = jnp.tanh(slope * gate * (1.0 + 0.044715 * square))
    half = 0.5 * (1.0 + bent)
    value = gate * half
    rise = half + 0.5 * gate * (1.0 - bent * bent) * slope * (1.0 + 0.134145 * square)
    return value, rise


def stack_heads(pair):
    lane = lax.broadcasted_iota(jnp.int32, pair.shape, 1)
    zero = jnp.zeros_like(pair)
    return jnp.concatenate(
        [jnp.where(lane < HEAD_DIM, pair, zero), jnp.where(lane < HEAD_DIM, zero, pair)], 0
    )


def merge_heads(stacked):
    rows = stacked.shape[0] // 2
    lane = lax.broadcasted_iota(jnp.int32, (rows, PAIR), 1)
    return jnp.where(lane < HEAD_DIM, stacked[:rows], stacked[rows:])


def soft_of(stacked_query, keys, bias):
    scores = mm_nt(stacked_query, keys) * SCALE + bias
    expon = jnp.exp(scores - jnp.max(scores, -1, keepdims=True))
    return expon / jnp.sum(expon, -1, keepdims=True)


def pair_fwd(query, keys, values, bias):
    soft = soft_of(stack_heads(query), keys, bias)
    return merge_heads(mm(soft.astype(BF), values)).astype(BF)


def pair_back(query, keys, values, grad_out, bias):
    queries = stack_heads(query)
    soft = soft_of(queries, keys, bias)
    grads = stack_heads(grad_out)
    grad_values = mm_tn(soft.astype(BF), grads)
    grad_soft = mm_nt(grads, values)
    grad_scores = (
        soft * (grad_soft - jnp.sum(soft * grad_soft, -1, keepdims=True))
    ).astype(BF)
    grad_query = merge_heads(mm(grad_scores, keys)) * SCALE
    grad_keys = mm_tn(grad_scores, queries) * SCALE
    return grad_query.astype(BF), grad_keys.astype(BF), grad_values.astype(BF)


def length_bias(count, rows, length):
    col = lax.broadcasted_iota(jnp.int32, (2 * rows, length), 1)
    return jnp.where(col < count, 0.0, NEG_LARGE).astype(F32)


def causal_bias(counts, plots, length):
    shape = (plots * length, plots * length)
    row = lax.broadcasted_iota(jnp.int32, shape, 0)
    col = lax.broadcasted_iota(jnp.int32, shape, 1)
    bias = jnp.full(shape, NEG_LARGE, F32)
    for plot in range(plots):
        low = plot * length
        inside = (row >= low) & (row < low + length) & (col >= low)
        inside = inside & (col <= row) & (col < low + counts[plot])
        bias = jnp.where(inside, 0.0, bias)
    return jnp.concatenate([bias, bias], 0)


def pairs_of(width):
    return [slice(at, at + PAIR) for at in range(0, width, PAIR)]


def put(ref, at, value):
    ref[:, at : at + value.shape[1]] = value.astype(ref.dtype)
    return at + value.shape[1]


def put_both(send_ref, keep_ref, at, value):
    put(send_ref, at, value)
    return put(keep_ref, at, value)


def put_cut(send_ref, keep_ref, at, value, order_ref):
    ordered = mm(value, order_ref[...])
    half = ordered.shape[1] // 2
    put(send_ref, at, ordered[:, :half])
    return put(keep_ref, at, ordered[:, half:])


def self_fwd_kernel(causal, length, counts, state, gain, stacked, outer, part, normed_ref, qkv_ref, mixed_ref):
    rows = state.shape[0]
    width = outer.shape[0]
    normed = norm(state[...].astype(F32), gain[...])
    normed_ref[...] = normed
    for which in range(3):
        qkv_ref[:, which * width : (which + 1) * width] = mm(normed, stacked[which]).astype(BF)
    plots = rows // length
    if causal:
        spans = [slice(0, rows)]
        biases = [causal_bias(counts, plots, length)]
    else:
        spans = [slice(p * length, (p + 1) * length) for p in range(plots)]
        biases = [length_bias(counts[p], length, length) for p in range(plots)]
    for span, bias in zip(spans, biases):
        for cols in pairs_of(width):
            mixed_ref[span, cols] = pair_fwd(
                qkv_ref[span, cols],
                qkv_ref[span, width + cols.start : width + cols.stop],
                qkv_ref[span, 2 * width + cols.start : 2 * width + cols.stop],
                bias,
            )
    part[...] = mm(mixed_ref[...], outer[...])


def enc_mlp_fwd_kernel(state, own, other, gain, inner, outer, part, state_ref, normed_ref, gate_ref, up_ref, hidden_ref):
    full = state[...].astype(F32) + own[...] + other[...]
    state_ref[...] = full
    normed_ref[...] = norm(full, gain[...])
    width = outer.shape[0]
    step = 256
    for at in range(0, width, step):
        cols = slice(at, at + step)
        gate = mm(normed_ref[...], inner[0, :, cols])
        up = mm(normed_ref[...], inner[1, :, cols])
        gate_ref[:, cols] = gate
        up_ref[:, cols] = up
        value, _ = gelu_parts(gate)
        hidden_ref[:, cols] = (value * up).astype(BF)
    part[...] = mm(hidden_ref[...], outer[...])


def cross_fwd_kernel(
    length, counts, enc_state, enc_own, enc_other, enc_gain, dec_state, dec_own, dec_other, dec_gain, stacked, outer,
    part, enc_ref, memory_ref, dec_ref, normed_ref, query_ref, kv_ref, mixed_ref,
):
    width = outer.shape[0]
    enc_full = enc_state[...] + enc_own[...] + enc_other[...]
    enc_ref[...] = enc_full
    memory_ref[...] = norm(enc_full, enc_gain[...])
    dec_full = dec_state[...].astype(F32) + dec_own[...] + dec_other[...]
    dec_ref[...] = dec_full
    normed_ref[...] = norm(dec_full, dec_gain[...])
    query_ref[...] = mm(normed_ref[...], stacked[0]).astype(BF)
    kv_ref[:, :width] = mm(memory_ref[...], stacked[1]).astype(BF)
    kv_ref[:, width:] = mm(memory_ref[...], stacked[2]).astype(BF)
    plots = enc_state.shape[0] // length
    rows = dec_state.shape[0] // plots
    for plot in range(plots):
        bias = length_bias(counts[plot], rows, length)
        q_span = slice(plot * rows, (plot + 1) * rows)
        k_span = slice(plot * length, (plot + 1) * length)
        for cols in pairs_of(width):
            mixed_ref[q_span, cols] = pair_fwd(
                query_ref[q_span, cols],
                kv_ref[k_span, cols],
                kv_ref[k_span, width + cols.start : width + cols.stop],
                bias,
            )
    part[...] = mm(mixed_ref[...], outer[...])


def dec_mlp_kernel(state, own, other, gain, cotangent, inner, outer, order, out_part, grad_part, state_ref, send, keep):
    full = state[...] + own[...] + other[...]
    state_ref[...] = full
    normed = norm(full, gain[...])
    width = outer.shape[0]
    at = put_cut(send, keep, 0, normed, order)
    half = at
    low = cotangent[...]
    put_cut(send, keep, half + 2 * width, low, order)
    step = 256
    for col in range(0, width, step):
        cols = slice(col, col + step)
        gate = mm(normed, inner[0, :, cols])
        up = mm(normed, inner[1, :, cols])
        value, rise = gelu_parts(gate)
        grad_hidden = mm_nt(low, outer[cols, :])
        put_both(send, keep, half + col, (grad_hidden * up * rise).astype(BF))
        put_both(send, keep, half + width + col, (grad_hidden * value).astype(BF))
        put_both(send, keep, 2 * half + 2 * width + col, (value * up).astype(BF))
    grad_part[...] = mm_nt(keep[:, half : half + width], inner[0]) + mm_nt(
        keep[:, half + width : half + 2 * width], inner[1]
    )
    out_part[...] = mm(keep[:, 2 * half + 2 * width :], outer[...])


def cross_back_kernel(
    length, counts, grad, own, other, state, gain, normed, memory, query, kv, mixed, stacked, outer, order,
    query_part, memory_part, grad_ref, gain_ref, send, keep, key_grads,
):
    grad_in, gain_ref[...] = norm_back(own[...] + other[...], state[...], gain[...])
    full = grad[...].astype(F32) + grad_in
    grad_ref[...] = full
    low = full.astype(BF)
    width = outer.shape[0]
    at = put_cut(send, keep, 0, normed[...], order)
    half = at
    at = put_cut(send, keep, half + width, low, order)
    put_both(send, keep, at, mixed[...])
    base = at + width
    grad_mixed = mm_nt(low, outer[...]).astype(BF)
    plots = kv.shape[0] // length
    rows = low.shape[0] // plots
    for plot in range(plots):
        bias = length_bias(counts[plot], rows, length)
        q_span = slice(plot * rows, (plot + 1) * rows)
        k_span = slice(plot * length, (plot + 1) * length)
        for cols in pairs_of(width):
            values = slice(width + cols.start, width + cols.stop)
            grad_query, grad_keys, grad_values = pair_back(
                query[q_span, cols], kv[k_span, cols], kv[k_span, values], grad_mixed[q_span, cols], bias
            )
            keep[q_span, half + cols.start : half + cols.stop] = grad_query
            send[q_span, half + cols.start : half + cols.stop] = grad_query.astype(F32)
            key_grads[k_span, cols] = grad_keys
            key_grads[k_span, values] = grad_values
    query_part[...] = mm_nt(keep[:, half : half + width], stacked[0])
    memory_part[...] = mm_nt(key_grads[:, :width], stacked[1]) + mm_nt(key_grads[:, width:], stacked[2])
    ordered = mm(memory[...], order[...])
    folds = kv.shape[0] // low.shape[0]
    for fold in range(folds):
        span = slice(fold * low.shape[0], (fold + 1) * low.shape[0])
        put(send, base, ordered[span, :half])
        put(keep, base, ordered[span, half:])
        base = put_both(send, keep, base + half, key_grads[span, :])


def self_back_kernel(
    causal, length, counts, grad, own, other, state, gain, normed, qkv, mixed, stacked, outer, order,
    part, grad_ref, gain_ref, send, keep,
):
    grad_in, gain_ref[...] = norm_back(own[...] + other[...], state[...], gain[...])
    full = grad[...] + grad_in
    grad_ref[...] = full
    low = full.astype(BF)
    width = outer.shape[0]
    half = put_cut(send, keep, 0, normed[...], order)
    at = put_cut(send, keep, half + 3 * width, low, order)
    put_both(send, keep, at, mixed[...])
    grad_mixed = mm_nt(low, outer[...]).astype(BF)
    rows = low.shape[0]
    plots = rows // length
    if causal:
        spans = [slice(0, rows)]
        biases = [causal_bias(counts, plots, length)]
    else:
        spans = [slice(p * length, (p + 1) * length) for p in range(plots)]
        biases = [length_bias(counts[p], length, length) for p in range(plots)]
    for span, bias in zip(spans, biases):
        for cols in pairs_of(width):
            grads = pair_back(
                qkv[span, cols],
                qkv[span, width + cols.start : width + cols.stop],
                qkv[span, 2 * width + cols.start : 2 * width + cols.stop],
                grad_mixed[span, cols],
                bias,
            )
            for which, piece in enumerate(grads):
                start = half + which * width + cols.start
                keep[span, start : start + PAIR] = piece
                send[span, start : start + PAIR] = piece.astype(F32)
    total = mm_nt(keep[:, half : half + width], stacked[0])
    total += mm_nt(keep[:, half + width : half + 2 * width], stacked[1])
    total += mm_nt(keep[:, half + 2 * width : half + 3 * width], stacked[2])
    part[...] = total


def enc_mlp_back_kernel(
    own, other, state, gain, normed, gate_ref, up_ref, hidden, inner, outer, order,
    part, grad_ref, gain_ref, send, keep,
):
    full, gain_ref[...] = norm_back(own[...] + other[...], state[...], gain[...])
    grad_ref[...] = full
    low = full.astype(BF)
    width = outer.shape[0]
    half = put_cut(send, keep, 0, normed[...], order)
    at = put_cut(send, keep, half + 2 * width, low, order)
    put_both(send, keep, at, hidden[...])
    step = 256
    for col in range(0, width, step):
        cols = slice(col, col + step)
        value, rise = gelu_parts(gate_ref[:, cols])
        grad_hidden = mm_nt(low, outer[cols, :])
        put_both(send, keep, half + col, (grad_hidden * up_ref[:, cols] * rise).astype(BF))
        put_both(send, keep, half + width + col, (grad_hidden * value).astype(BF))
    part[...] = mm_nt(keep[:, half : half + width], inner[0]) + mm_nt(
        keep[:, half + width : half + 2 * width], inner[1]
    )


def last_kernel(
    enc_grad, enc_own, enc_other, enc_state, enc_gain, dec_grad, dec_own, dec_other, dec_state, dec_gain,
    enc_ref, enc_gain_ref, dec_ref, dec_gain_ref,
):
    grad_in, enc_gain_ref[...] = norm_back(
        enc_own[...] + enc_other[...], enc_state[...].astype(F32), enc_gain[...]
    )
    enc_ref[...] = (enc_grad[...] + grad_in).astype(BF)
    grad_in, dec_gain_ref[...] = norm_back(
        dec_own[...] + dec_other[...], dec_state[...].astype(F32), dec_gain[...]
    )
    dec_ref[...] = (dec_grad[...] + grad_in).astype(BF)


def weight_kernel(segments, keep, recv, send_out, keep_out):
    started = set()
    for cut, cut_width, first, columns, target in segments:
        left = jnp.concatenate([keep[:, cut : cut + cut_width], recv[:, cut : cut + cut_width].astype(BF)], 0)
        half = cut_width // 2
        step = 512 if columns % 512 == 0 else 384
        for at in range(0, columns, step):
            cols = slice(first + at, first + at + step)
            right = jnp.concatenate([keep[:, cols], recv[:, cols].astype(BF)], 0)
            total = mm_tn(left, right)
            into = slice(target + at, target + at + step)
            if target in started:
                send_out[:, into] += total[:half]
                keep_out[:, into] += total[half:]
            else:
                send_out[:, into] = total[:half]
                keep_out[:, into] = total[half:]
        started.add(target)


SMEM = pl.BlockSpec(memory_space=pltpu.SMEM)
VMEM = pl.BlockSpec(memory_space=pltpu.VMEM)


def call(kernel, outs, args, flops, name, scalars=0, scratch=(), limit=40):
    shapes = [jax.ShapeDtypeStruct(shape, kind) for shape, kind in outs]
    moved = sum(a.size * a.dtype.itemsize for a in args) + sum(
        s.size * jnp.dtype(s.dtype).itemsize for s in shapes
    )
    return pl.pallas_call(
        kernel,
        out_shape=shapes,
        in_specs=[SMEM] * scalars + [VMEM] * (len(args) - scalars),
        out_specs=[VMEM] * len(shapes),
        scratch_shapes=list(scratch),
        compiler_params=pltpu.CompilerParams(vmem_limit_bytes=limit * MIB),
        cost_estimate=pl.CostEstimate(flops=int(flops), bytes_accessed=int(moved), transcendentals=0),
        name=name,
    )(*args)


def pair_other(part):
    return lax.ppermute(part, "mp", [(0, 1), (1, 0)])


def swap(value, bit):
    shards = lax.axis_size("dp")
    return lax.ppermute(value, "dp", [(i, i ^ (1 << bit)) for i in range(shards)])


def feature_order(features, bits_order):
    shards = lax.axis_size("dp")
    me = lax.axis_index("dp")
    block = features // shards
    column = jnp.arange(features, dtype=jnp.int32)
    place = column // block
    owner = jnp.zeros_like(column)
    count = len(bits_order)
    for at, bit in enumerate(bits_order):
        own = (place >> (count - 1 - at)) & 1
        owner = owner | ((((me >> bit) & 1) ^ (1 - own)) << bit)
    source = owner * block + column % block
    return (jnp.arange(features, dtype=jnp.int32)[:, None] == source[None, :]).astype(BF)


def halve(sent, kept, bits_order):
    bits = list(bits_order[1:])
    total = kept + swap(sent, bits[0])
    for bit in bits[1:]:
        rows = total.shape[0] // 2
        total = total[rows:] + swap(total[:rows], bit)
    return total


def weight_sums(send, keep, segments, columns, bits_order, name):
    recv = swap(send, 0)
    rows = segments[0][1] // 2
    flops = sum(2 * 2 * keep.shape[0] * s[1] * s[3] for s in segments)
    sent, kept = call(
        functools.partial(weight_kernel, segments),
        [((rows, columns), F32), ((rows, columns), F32)],
        [keep, recv],
        flops,
        name,
    )
    return halve(sent, kept, bits_order)


def body(
    enc_in, dec_in, cotangent, patch_counts, table_lengths, enc_qkv, enc_attn_out, enc_mlp_in, enc_mlp_out, enc_gains,
    dec_self_qkv, dec_self_out, dec_cross_qkv, dec_cross_out, dec_mlp_in, dec_mlp_out, dec_gains,
):
    plots, enc_len, features = enc_in.shape
    dec_len = dec_in.shape[1]
    enc_rows, dec_rows = plots * enc_len, plots * dec_len
    heads = enc_attn_out.shape[0]
    units = enc_mlp_out.shape[0]
    half = features // 2
    bits = lax.axis_size("dp").bit_length() - 1
    plain = tuple(range(bits))
    turned = (0, 2, 1) + tuple(range(3, bits))
    order = feature_order(features, plain)
    order_turned = feature_order(features, turned)
    x0 = enc_in.reshape(enc_rows, features)
    y0 = dec_in.reshape(dec_rows, features)
    top = cotangent.reshape(dec_rows, features)
    eg = [enc_gains[i : i + 1] for i in range(3)]
    dg = [dec_gains[i : i + 1] for i in range(3)]
    enc_wide, dec_wide = ((enc_rows, features), F32), ((dec_rows, features), F32)
    enc_low, dec_low = ((enc_rows, features), BF), ((dec_rows, features), BF)
    gain_row = ((1, features), F32)
    attn_flops = 2 * features * heads

    part_e1, u_e0, qkv_e, mixed_e = call(
        functools.partial(self_fwd_kernel, False, enc_len),
        [enc_wide, enc_low, ((enc_rows, 3 * heads), BF), ((enc_rows, heads), BF)],
        [patch_counts, x0, eg[0], enc_qkv, enc_attn_out],
        4 * enc_rows * attn_flops, "enc_attn_fwd", 1,
    )
    other_e1 = pair_other(part_e1)
    part_d1, u_d0, qkv_d, mixed_d = call(
        functools.partial(self_fwd_kernel, True, dec_len),
        [dec_wide, dec_low, ((dec_rows, 3 * heads), BF), ((dec_rows, heads), BF)],
        [table_lengths, y0, dg[0], dec_self_qkv, dec_self_out],
        4 * dec_rows * attn_flops, "dec_self_fwd", 1,
    )
    other_d1 = pair_other(part_d1)
    part_e2, x1, u_e1, gate, up, hidden = call(
        enc_mlp_fwd_kernel,
        [enc_wide, enc_wide, enc_low, ((enc_rows, units), F32), ((enc_rows, units), F32), ((enc_rows, units), BF)],
        [x0, part_e1, other_e1, eg[1], enc_mlp_in, enc_mlp_out],
        6 * enc_rows * features * units, "enc_mlp_fwd",
    )
    other_e2 = pair_other(part_e2)
    part_d2, x2, memory, y1, u_d1, query, kv, mixed_c = call(
        functools.partial(cross_fwd_kernel, enc_len),
        [dec_wide, enc_wide, enc_low, dec_wide, dec_low, ((dec_rows, heads), BF), ((enc_rows, 2 * heads), BF),
         ((dec_rows, heads), BF)],
        [patch_counts, x1, part_e2, other_e2, eg[2], y0, part_d1, other_d1, dg[1], dec_cross_qkv, dec_cross_out],
        2 * (dec_rows + enc_rows) * attn_flops, "cross_fwd", 1,
    )
    other_d2 = pair_other(part_d2)
    wide = 2 * half + 3 * units
    part_out, part_g3, y2, send_m, keep_m = call(
        dec_mlp_kernel,
        [dec_wide, dec_wide, dec_wide, ((dec_rows, wide), F32), ((dec_rows, wide), BF)],
        [y1, part_d2, other_d2, dg[2], top, dec_mlp_in, dec_mlp_out, order],
        12 * dec_rows * features * units, "dec_mlp",
    )
    other_g3 = pair_other(part_g3)
    wide = 2 * half + 2 * heads + (enc_rows // dec_rows) * (half + 2 * heads)
    part_q, part_m, g2, gain_d2, send_c, keep_c = call(
        functools.partial(cross_back_kernel, enc_len),
        [dec_wide, enc_wide, dec_wide, gain_row, ((dec_rows, wide), F32), ((dec_rows, wide), BF)],
        [patch_counts, top, part_g3, other_g3, y2, dg[2], u_d1, memory, query, kv, mixed_c, dec_cross_qkv,
         dec_cross_out, order],
        2 * (dec_rows + enc_rows) * attn_flops, "cross_back", 1,
        scratch=[pltpu.VMEM((enc_rows, 2 * heads), BF)],
    )
    other_m = pair_other(part_m)
    other_q = pair_other(part_q)
    mlp_segments = (
        (0, half, half, 2 * units, 0),
        (half + 2 * units, half, 2 * half + 2 * units, units, 2 * units),
    )
    attn_segments = (
        (0, half, half, 3 * heads, 0),
        (half + 3 * heads, half, 2 * half + 3 * heads, heads, 3 * heads),
    )
    base = 2 * half + 2 * heads
    cross_segments = (
        (0, half, half, heads, 0),
        (half + heads, half, 2 * half + heads, heads, heads),
    ) + tuple(
        (base + f * (half + 2 * heads), half, base + f * (half + 2 * heads) + half, 2 * heads, 2 * heads)
        for f in range(enc_rows // dec_rows)
    )
    sum_m = weight_sums(send_m, keep_m, mlp_segments, 3 * units, plain, "dec_mlp_weights")
    wide = 2 * half + 3 * units
    part_g1, back2, gain_e2, send_f, keep_f = call(
        enc_mlp_back_kernel,
        [enc_wide, enc_wide, gain_row, ((enc_rows, wide), F32), ((enc_rows, wide), BF)],
        [part_m, other_m, x2, eg[2], u_e1, gate, up, hidden, enc_mlp_in, enc_mlp_out, order],
        6 * enc_rows * features * units, "enc_mlp_back",
    )
    other_g1 = pair_other(part_g1)
    sum_c = weight_sums(send_c, keep_c, cross_segments, 4 * heads, plain, "cross_weights")
    wide = 2 * half + 4 * heads
    part_g0, g1, gain_d1, send_s, keep_s = call(
        functools.partial(self_back_kernel, True, dec_len),
        [dec_wide, dec_wide, gain_row, ((dec_rows, wide), F32), ((dec_rows, wide), BF)],
        [table_lengths, g2, part_q, other_q, y1, dg[1], u_d0, qkv_d, mixed_d, dec_self_qkv, dec_self_out,
         order_turned],
        4 * dec_rows * attn_flops, "dec_self_back", 1,
    )
    other_g0 = pair_other(part_g0)
    sum_f = weight_sums(send_f, keep_f, mlp_segments, 3 * units, plain, "enc_mlp_weights")
    sum_s = weight_sums(send_s, keep_s, attn_segments, 4 * heads, turned, "dec_self_weights")
    part_ge, back1, gain_e1, send_a, keep_a = call(
        functools.partial(self_back_kernel, False, enc_len),
        [enc_wide, enc_wide, gain_row, ((enc_rows, wide), F32), ((enc_rows, wide), BF)],
        [patch_counts, back2, part_g1, other_g1, x1, eg[1], u_e0, qkv_e, mixed_e, enc_qkv, enc_attn_out, order],
        4 * enc_rows * attn_flops, "enc_attn_back", 1,
    )
    other_ge = pair_other(part_ge)
    sum_a = weight_sums(send_a, keep_a, attn_segments, 4 * heads, plain, "enc_attn_weights")
    enc_out, gain_e0, dec_out_grad, gain_d0 = call(
        last_kernel,
        [enc_low, gain_row, dec_low, gain_row],
        [back1, part_ge, other_ge, x0, eg[0], g1, part_g0, other_g0, y0, dg[0]],
        100, "input_grads",
    )
    dec_out = (y2 + part_out + pair_other(part_out)).astype(BF)

    gains = jnp.concatenate([gain_e0, gain_e1, gain_e2, gain_d0, gain_d1, gain_d2], 0)
    gains = gains.reshape((gains.shape[0],) + (2,) * bits + (-1,))
    me = lax.axis_index("dp")
    for bit in range(bits):
        axis = bits - bit
        mine = (me >> bit) & 1
        sent = lax.dynamic_index_in_dim(gains, 1 - mine, axis, keepdims=False)
        gains = lax.dynamic_index_in_dim(gains, mine, axis, keepdims=False) + swap(sent, bit)

    def stacked_of(total, count):
        return jnp.moveaxis(total.reshape(total.shape[0], count, -1), 1, 0)

    def attn_grads(total):
        return [stacked_of(total[:, : 3 * heads], 3), total[:, 3 * heads :].T]

    def mlp_grads(total):
        return [stacked_of(total[:, : 2 * units], 2), total[:, 2 * units :].T]

    cross_in = jnp.concatenate([sum_c[:, :heads], sum_c[:, 2 * heads :]], 1)
    cross = [stacked_of(cross_in, 3), sum_c[:, heads : 2 * heads].T]
    grads = (
        attn_grads(sum_a) + mlp_grads(sum_f) + [gains[:3]] + attn_grads(sum_s) + cross + mlp_grads(sum_m) + [gains[3:]]
    )
    return (
        dec_out.reshape(cotangent.shape),
        enc_out.reshape(enc_in.shape),
        dec_out_grad.reshape(dec_in.shape),
    ) + tuple(grads)


def solution(mesh):
    rows = P("dp", None, None)
    inner, outer = P(None, None, "mp"), P("mp", None)
    enc = (inner, outer, inner, outer, P())
    dec = (inner, outer, inner, outer, inner, outer, P())
    inner_grad, outer_grad, gain_grad = P(None, "dp", "mp"), P("mp", "dp"), P(None, "dp")
    return jax.shard_map(
        body,
        mesh=mesh,
        in_specs=(rows, rows, rows, P("dp"), P("dp")) + enc + dec,
        out_specs=(rows, rows, rows)
        + (inner_grad, outer_grad) * 2 + (gain_grad,)
        + (inner_grad, outer_grad) * 3 + (gain_grad,),
        check_vma=False,
    )
```

```python
import functools

import jax
import jax.numpy as jnp
from jax import lax
from jax.experimental import pallas as pl
from jax.experimental.pallas import tpu as pltpu
from jax.sharding import PartitionSpec as P

HEAD_DIM = 64
PAIR = 2 * HEAD_DIM
EPSILON = 1e-06
NEG_LARGE = -1e30
SCALE = HEAD_DIM ** (-0.5)
BF = jnp.bfloat16
F32 = jnp.float32
MIB = 1024 * 1024


def mm(left, right):
    return jnp.dot(left, right, preferred_element_type=F32)


def mm_nt(left, right):
    return lax.dot_general(left, right, (((1,), (1,)), ((), ())), preferred_element_type=F32)


def mm_tn(left, right):
    return lax.dot_general(left, right, (((0,), (0,)), ((), ())), preferred_element_type=F32)


def norm(hidden, gain):
    scaling = lax.rsqrt(jnp.mean(hidden * hidden, -1, keepdims=True) + EPSILON)
    return (hidden * scaling * gain).astype(BF)


def norm_back(grad, hidden, gain):
    scaling = lax.rsqrt(jnp.mean(hidden * hidden, -1, keepdims=True) + EPSILON)
    normed = hidden * scaling
    grad_hat = grad * gain
    grad_in = scaling * (grad_hat - normed * jnp.mean(grad_hat * normed, -1, keepdims=True))
    return grad_in, jnp.sum(grad * normed, 0, keepdims=True)


def gelu_parts(gate):
    slope = 0.7978845608028654
    square = gate * gate
    bent = jnp.tanh(slope * gate * (1.0 + 0.044715 * square))
    half = 0.5 * (1.0 + bent)
    value = gate * half
    rise = half + 0.5 * gate * (1.0 - bent * bent) * slope * (1.0 + 0.134145 * square)
    return value, rise


def stack_heads(pair):
    lane = lax.broadcasted_iota(jnp.int32, pair.shape, 1)
    zero = jnp.zeros_like(pair)
    return jnp.concatenate(
        [jnp.where(lane < HEAD_DIM, pair, zero), jnp.where(lane < HEAD_DIM, zero, pair)], 0
    )


def merge_heads(stacked):
    rows = stacked.shape[0] // 2
    lane = lax.broadcasted_iota(jnp.int32, (rows, PAIR), 1)
    return jnp.where(lane < HEAD_DIM, stacked[:rows], stacked[rows:])


def soft_of(stacked_query, keys, bias):
    scores = mm_nt(stacked_query, keys) * SCALE + bias
    expon = jnp.exp(scores - jnp.max(scores, -1, keepdims=True))
    return expon / jnp.sum(expon, -1, keepdims=True)


def pair_fwd(query, keys, values, bias):
    soft = soft_of(stack_heads(query), keys, bias)
    return merge_heads(mm(soft.astype(BF), values)).astype(BF)


def pair_back(query, keys, values, grad_out, bias):
    queries = stack_heads(query)
    soft = soft_of(queries, keys, bias)
    grads = stack_heads(grad_out)
    grad_values = mm_tn(soft.astype(BF), grads)
    grad_soft = mm_nt(grads, values)
    grad_scores = (
        soft * (grad_soft - jnp.sum(soft * grad_soft, -1, keepdims=True))
    ).astype(BF)
    grad_query = merge_heads(mm(grad_scores, keys)) * SCALE
    grad_keys = mm_tn(grad_scores, queries) * SCALE
    return grad_query.astype(BF), grad_keys.astype(BF), grad_values.astype(BF)


def length_bias(count, rows, length):
    col = lax.broadcasted_iota(jnp.int32, (2 * rows, length), 1)
    return jnp.where(col < count, 0.0, NEG_LARGE).astype(F32)


def causal_bias(counts, plots, length):
    shape = (plots * length, plots * length)
    row = lax.broadcasted_iota(jnp.int32, shape, 0)
    col = lax.broadcasted_iota(jnp.int32, shape, 1)
    bias = jnp.full(shape, NEG_LARGE, F32)
    for plot in range(plots):
        low = plot * length
        inside = (row >= low) & (row < low + length) & (col >= low)
        inside = inside & (col <= row) & (col < low + counts[plot])
        bias = jnp.where(inside, 0.0, bias)
    return jnp.concatenate([bias, bias], 0)


def pairs_of(width):
    return [slice(at, at + PAIR) for at in range(0, width, PAIR)]


def put(ref, at, value):
    last = at + value.shape[1]
    ref[:, at:last] = value.astype(ref.dtype)
    ref.flush(at, last)
    return last


def put_both(send, keep, at, value):
    put(send, at, value)
    return put(keep, at, value)


def put_cut(send, keep, at, value, order):
    ordered = mm(value, order[...])
    half = ordered.shape[1] // 2
    put(send, at, ordered[:, :half])
    return put(keep, at, ordered[:, half:])


def keys_of(causal, length, rows, counts):
    plots = rows // length
    if causal:
        return [(slice(0, rows), causal_bias(counts, plots, length))]
    return [(slice(p * length, (p + 1) * length), length_bias(counts[p], length, length)) for p in range(plots)]


def self_fwd_kernel(causal, length, counts, state, gain, stacked, outer, part, normed_ref, qkv, mixed):
    rows, width = state.shape[0], outer.shape[0]
    normed = norm(state[...].astype(F32), gain[0:1, :])
    normed_ref[...] = normed
    normed_ref.flush()
    for which in range(3):
        put(qkv, which * width, mm(normed, stacked[which]))
    for span, bias in keys_of(causal, length, rows, counts):
        for cols in pairs_of(width):
            mixed[span, cols] = pair_fwd(
                qkv[span, cols],
                qkv[span, width + cols.start : width + cols.stop],
                qkv[span, 2 * width + cols.start : 2 * width + cols.stop],
                bias,
            )
    mixed.flush()
    part[...] = mm(mixed[...], outer[...])


def enc_mlp_fwd_kernel(state, own, other, gain, inner, outer, part, state_ref, normed, gate_ref, up_ref, hidden):
    full = state[...].astype(F32) + own[...] + other[...]
    state_ref[...] = full
    normed[...] = norm(full, gain[1:2, :])
    flush(state_ref, normed)
    width = outer.shape[0]
    step = 256
    for at in range(0, width, step):
        cols = slice(at, at + step)
        gate = mm(normed[...], inner[0, :, cols])
        up = mm(normed[...], inner[1, :, cols])
        value, _ = gelu_parts(gate)
        put(gate_ref, at, gate)
        put(up_ref, at, up)
        put(hidden, at, value * up)
    part[...] = mm(hidden[...], outer[...])


def cross_fwd_kernel(
    length, counts, enc_state, enc_own, enc_other, enc_gain, dec_state, dec_own, dec_other, dec_gain, stacked, outer,
    part, enc_ref, memory, dec_ref, normed, query, kv, mixed,
):
    width = outer.shape[0]
    dec_full = dec_state[...].astype(F32) + dec_own[...] + dec_other[...]
    dec_ref[...] = dec_full
    normed[...] = norm(dec_full, dec_gain[1:2, :])
    flush(dec_ref, normed)
    put(query, 0, mm(normed[...], stacked[0]))
    enc_full = enc_state[...] + enc_own[...] + enc_other[...]
    enc_ref[...] = enc_full
    memory[...] = norm(enc_full, enc_gain[2:3, :])
    flush(enc_ref, memory)
    put(kv, 0, mm(memory[...], stacked[1]))
    put(kv, width, mm(memory[...], stacked[2]))
    plots = enc_state.shape[0] // length
    rows = dec_state.shape[0] // plots
    for plot in range(plots):
        bias = length_bias(counts[plot], rows, length)
        q_span = slice(plot * rows, (plot + 1) * rows)
        k_span = slice(plot * length, (plot + 1) * length)
        for cols in pairs_of(width):
            mixed[q_span, cols] = pair_fwd(
                query[q_span, cols],
                kv[k_span, cols],
                kv[k_span, width + cols.start : width + cols.stop],
                bias,
            )
    mixed.flush()
    part[...] = mm(mixed[...], outer[...])


def dec_mlp_kernel(
    state, own, other, gain, cotangent, inner, outer, order, order_outer, part, state_ref, send, keep
):
    full = state[...] + own[...] + other[...]
    state_ref[...] = full
    state_ref.flush()
    normed = norm(full, gain[2:3, :])
    low = cotangent[...]
    width, half = outer.shape[0], order.shape[0] // 2
    step = 256
    for col in range(0, width, step):
        cols = slice(col, col + step)
        gate = mm(normed, inner[0, :, cols])
        up = mm(normed, inner[1, :, cols])
        value, rise = gelu_parts(gate)
        grad_hidden = mm_nt(low, outer[cols, :])
        put_both(send, keep, half + col, (grad_hidden * up * rise).astype(BF))
        put_both(send, keep, half + width + col, (grad_hidden * value).astype(BF))
        put_both(send, keep, 2 * half + 2 * width + col, (value * up).astype(BF))
    part[...] = mm_nt(keep[:, half : half + width], inner[0]) + mm_nt(
        keep[:, half + width : half + 2 * width], inner[1]
    )
    part.flush()
    put_cut(send, keep, 0, normed, order)
    put_cut(send, keep, half + 2 * width, low, order_outer)


def out_part_kernel(keep, outer, part):
    part[...] = mm(keep[:, keep.shape[1] - outer.shape[0] :], outer[...])


def query_part_kernel(keep, stacked, part):
    half = stacked.shape[1] // 2
    part[...] = mm_nt(keep[:, half : half + stacked.shape[2]], stacked[0])


def cross_back_kernel(
    length, counts, own, other, state, gain, grad, outer, query, kv, stacked, order, normed, memory, mixed,
    part, grad_ref, gain_ref, send, keep, key_grads,
):
    grad_in, gain_ref[...] = norm_back(own[...] + other[...], state[...], gain[2:3, :])
    full = grad[...].astype(F32) + grad_in
    grad_ref[...] = full
    flush(gain_ref, grad_ref)
    low = full.astype(BF)
    width, half = outer.shape[0], order.shape[0] // 2
    grad_mixed = mm_nt(low, outer[...]).astype(BF)
    plots = kv.shape[0] // length
    rows = low.shape[0] // plots
    for plot in range(plots):
        bias = length_bias(counts[plot], rows, length)
        q_span = slice(plot * rows, (plot + 1) * rows)
        k_span = slice(plot * length, (plot + 1) * length)
        for cols in pairs_of(width):
            values = slice(width + cols.start, width + cols.stop)
            grad_query, grad_keys, grad_values = pair_back(
                query[q_span, cols], kv[k_span, cols], kv[k_span, values], grad_mixed[q_span, cols], bias
            )
            keep[q_span, half + cols.start : half + cols.stop] = grad_query
            send[q_span, half + cols.start : half + cols.stop] = grad_query.astype(F32)
            key_grads[k_span, cols] = grad_keys
            key_grads[k_span, values] = grad_values
    send.flush(half, half + width)
    keep.flush(half, half + width)
    part[...] = mm_nt(key_grads[:, :width], stacked[1]) + mm_nt(key_grads[:, width:], stacked[2])
    part.flush()
    put_cut(send, keep, 0, normed[...], order)
    at = put_cut(send, keep, half + width, low, order)
    base = put_both(send, keep, at, mixed[...])
    ordered = mm(memory[...], order[...])
    for fold in range(kv.shape[0] // low.shape[0]):
        span = slice(fold * low.shape[0], (fold + 1) * low.shape[0])
        put(send, base, ordered[span, :half])
        put(keep, base, ordered[span, half:])
        base = put_both(send, keep, base + half, key_grads[span, :])


def self_back_kernel(
    causal, length, counts, own, other, state, gain, grad, outer, qkv, stacked, order, normed, mixed,
    part, grad_ref, gain_ref, send, keep,
):
    grad_in, gain_ref[...] = norm_back(own[...] + other[...], state[...], gain[1:2, :])
    full = grad[...] + grad_in
    grad_ref[...] = full
    flush(gain_ref, grad_ref)
    low = full.astype(BF)
    width, half = outer.shape[0], order.shape[0] // 2
    grad_mixed = mm_nt(low, outer[...]).astype(BF)
    for span, bias in keys_of(causal, length, low.shape[0], counts):
        for cols in pairs_of(width):
            grads = pair_back(
                qkv[span, cols],
                qkv[span, width + cols.start : width + cols.stop],
                qkv[span, 2 * width + cols.start : 2 * width + cols.stop],
                grad_mixed[span, cols],
                bias,
            )
            for which, piece in enumerate(grads):
                start = half + which * width + cols.start
                keep[span, start : start + PAIR] = piece
                send[span, start : start + PAIR] = piece.astype(F32)
    send.flush(half, half + 3 * width)
    keep.flush(half, half + 3 * width)
    total = mm_nt(keep[:, half : half + width], stacked[0])
    total += mm_nt(keep[:, half + width : half + 2 * width], stacked[1])
    total += mm_nt(keep[:, half + 2 * width : half + 3 * width], stacked[2])
    part[...] = total
    part.flush()
    put_cut(send, keep, 0, normed[...], order)
    at = put_cut(send, keep, half + 3 * width, low, order)
    put_both(send, keep, at, mixed[...])


def enc_mlp_back_kernel(
    own, other, state, gain, outer, gate, up, inner, order, order_outer, normed, hidden,
    part, grad_ref, gain_ref, send, keep,
):
    full, gain_ref[...] = norm_back(own[...] + other[...], state[...], gain[2:3, :])
    grad_ref[...] = full
    flush(gain_ref, grad_ref)
    low = full.astype(BF)
    width, half = outer.shape[0], order.shape[0] // 2
    step = 256
    for col in range(0, width, step):
        cols = slice(col, col + step)
        value, rise = gelu_parts(gate[:, cols])
        grad_hidden = mm_nt(low, outer[cols, :])
        put_both(send, keep, half + col, (grad_hidden * up[:, cols] * rise).astype(BF))
        put_both(send, keep, half + width + col, (grad_hidden * value).astype(BF))
    part[...] = mm_nt(keep[:, half : half + width], inner[0]) + mm_nt(
        keep[:, half + width : half + 2 * width], inner[1]
    )
    part.flush()
    put_cut(send, keep, 0, normed[...], order)
    at = put_cut(send, keep, half + 2 * width, low, order_outer)
    put_both(send, keep, at, hidden[...])


def last_kernel(
    enc_own, enc_other, enc_state, enc_gain, enc_grad, dec_own, dec_other, dec_state, dec_gain, dec_grad,
    enc_ref, enc_gain_ref, dec_ref, dec_gain_ref,
):
    grad_in, enc_gain_ref[...] = norm_back(
        enc_own[...] + enc_other[...], enc_state[...].astype(F32), enc_gain[0:1, :]
    )
    enc_ref[...] = (enc_grad[...] + grad_in).astype(BF)
    flush(enc_ref, enc_gain_ref)
    grad_in, dec_gain_ref[...] = norm_back(
        dec_own[...] + dec_other[...], dec_state[...].astype(F32), dec_gain[0:1, :]
    )
    dec_ref[...] = (dec_grad[...] + grad_in).astype(BF)


def weight_kernel(segments, keep, recv, *outs):
    last_of = {(group, target): at for at, (_, _, _, _, group, target) in enumerate(segments)}
    started = set()
    for number, (cut, cut_width, first, columns, group, target) in enumerate(segments):
        send_out, keep_out = outs[2 * group], outs[2 * group + 1]
        left = jnp.concatenate([keep[:, cut : cut + cut_width], recv[:, cut : cut + cut_width].astype(BF)], 0)
        half = cut_width // 2
        step = 512 if columns % 512 == 0 else 384
        for at in range(0, columns, step):
            cols = slice(first + at, first + at + step)
            right = jnp.concatenate([keep[:, cols], recv[:, cols].astype(BF)], 0)
            total = mm_tn(left, right)
            into = slice(target + at, target + at + step)
            if (group, target) in started:
                total += jnp.concatenate([send_out[:, into], keep_out[:, into]], 0)
            send_out[:, into] = total[:half]
            keep_out[:, into] = total[half:]
            if last_of[group, target] == number:
                send_out.flush(into.start, into.stop)
                keep_out.flush(into.start, into.stop)
        started.add((group, target))


def halve_kernel(kept, recv, send_out, keep_out):
    rows = send_out.shape[0]
    send_out[...] = kept[:rows] + recv[:rows]
    send_out.flush()
    keep_out[...] = kept[rows:] + recv[rows:]


SMEM = pl.BlockSpec(memory_space=pltpu.SMEM)
VMEM = pl.BlockSpec(memory_space=pltpu.VMEM)
ANY = pl.BlockSpec(memory_space=pl.ANY)


COST = {
    "enc_attn_fwd": 2.3, "dec_self_fwd": 2.5, "enc_mlp_fwd": 1.7, "cross_fwd": 4.2, "dec_mlp": 2.7,
    "dec_mlp_weights": 0.8, "cross_back": 4.6, "enc_mlp_back": 3.0, "cross_weights": 0.8, "enc_attn_back": 6.8,
    "query_part": 0.3, "enc_mlp_weights": 2.4, "dec_self_back": 4.8, "dec_self_weights": 0.6,
    "enc_attn_weights": 2.8, "dec_out_part": 0.4, "input_grads": 3.0, "halve": 1.0,
}
COST_SCALE = 1.0
VMEM_LIMIT = 8


class Stored:
    def __init__(self, ref):
        self.ref = ref
        self.shape, self.dtype = ref.shape, ref.dtype

    def __getitem__(self, at):
        return self.ref[at]

    def __setitem__(self, at, value):
        self.ref[at] = value

    def flush(self, first=0, last=None):
        pass


def flush(*refs):
    for ref in refs:
        ref.flush()


class Line:
    def __init__(self):
        self.last = None

    def call(self, kernel, outs, args, name, scratch=()):
        shapes = [jax.ShapeDtypeStruct(*out) for out in outs]
        count, made = len(args), len(outs)
        in_specs = [VMEM if a.ndim > 1 else SMEM for a in args]
        if self.last is not None:
            args = list(args) + [self.last]
            in_specs.append(ANY)
        total = len(args)

        def run(*refs):
            stored = [Stored(ref) for ref in refs[total : total + made]]
            kernel(*refs[:count], *stored, *refs[total + made :])

        cost = COST[name] * COST_SCALE
        results = pl.pallas_call(
            run,
            out_shape=shapes,
            in_specs=in_specs,
            out_specs=[VMEM] * made,
            scratch_shapes=list(scratch),
            compiler_params=pltpu.CompilerParams(vmem_limit_bytes=VMEM_LIMIT * MIB),
            cost_estimate=pl.CostEstimate(
                flops=int(cost * 1.15e9), bytes_accessed=int(cost * 3.69e6), transcendentals=0
            ),
            name=name,
        )(*args)
        self.last = min(results, key=lambda r: r.size)
        return results


def pair_other(part):
    return lax.ppermute(part, "mp", [(0, 1), (1, 0)])


def swap(value, bit):
    shards = lax.axis_size("dp")
    return lax.ppermute(value, "dp", [(i, i ^ (1 << bit)) for i in range(shards)])


def feature_order(features, bits_order):
    shards = lax.axis_size("dp")
    me = lax.axis_index("dp")
    block = features // shards
    column = jnp.arange(features, dtype=jnp.int32)
    place = column // block
    owner = jnp.zeros_like(column)
    count = len(bits_order)
    for at, bit in enumerate(bits_order):
        own = (place >> (count - 1 - at)) & 1
        owner = owner | ((((me >> bit) & 1) ^ (1 - own)) << bit)
    source = owner * block + column % block
    return (jnp.arange(features, dtype=jnp.int32)[:, None] == source[None, :]).astype(BF)


class Halving:
    def __init__(self, sent, kept, bits_order):
        self.bits = list(bits_order[1:])
        self.kept = kept
        self.flying = swap(sent, self.bits[0])
        self.steps = 1

    def step(self, line):
        rows, columns = self.kept.shape[0] // 2, self.kept.shape[1]
        shape = ((rows, columns), F32)
        sent, self.kept = line.call(halve_kernel, [shape, shape], [self.kept, self.flying], "halve")
        self.flying = swap(sent, self.bits[self.steps])
        self.steps += 1

    def finish(self):
        total = self.kept + self.flying
        for bit in self.bits[self.steps :]:
            rows = total.shape[0] // 2
            total = total[rows:] + swap(total[:rows], bit)
        return total


def body(
    enc_in, dec_in, cotangent, patch_counts, table_lengths, enc_qkv, enc_attn_out, enc_mlp_in, enc_mlp_out, enc_gains,
    dec_self_qkv, dec_self_out, dec_cross_qkv, dec_cross_out, dec_mlp_in, dec_mlp_out, dec_gains,
):
    plots, enc_len, features = enc_in.shape
    dec_len = dec_in.shape[1]
    enc_rows, dec_rows = plots * enc_len, plots * dec_len
    heads = enc_attn_out.shape[0]
    units = enc_mlp_out.shape[0]
    half = features // 2
    bits = lax.axis_size("dp").bit_length() - 1
    plain = tuple(range(bits))
    turned = (0, 2, 1) + tuple(range(3, bits))
    order = feature_order(features, plain)
    order_turned = feature_order(features, turned)
    x0 = enc_in.reshape(enc_rows, features)
    y0 = dec_in.reshape(dec_rows, features)
    top = cotangent.reshape(dec_rows, features)
    enc_wide, dec_wide = ((enc_rows, features), F32), ((dec_rows, features), F32)
    enc_low, dec_low = ((enc_rows, features), BF), ((dec_rows, features), BF)
    gain_row = ((1, features), F32)
    quarter = half // 2
    line = Line()

    def group(columns):
        return [((quarter, columns), F32)] * 2

    mlp_groups = group(2 * units) + group(units)

    mlp_segments = (
        (0, half, half, 2 * units, 0, 0),
        (half + 2 * units, half, 2 * half + 2 * units, units, 1, 0),
    )
    attn_segments = (
        (0, half, half, 3 * heads, 0, 0),
        (half + 3 * heads, half, 2 * half + 3 * heads, heads, 0, 3 * heads),
    )
    base, fold_width = 2 * half + 2 * heads, half + 2 * heads
    folds = enc_rows // dec_rows
    cross_segments = (
        (0, half, half, heads, 0, 0),
        (half + heads, half, 2 * half + heads, heads, 0, heads),
    ) + tuple(
        (base + f * fold_width, half, base + f * fold_width + half, 2 * heads, 0, 2 * heads) for f in range(folds)
    )
    attn_group = group(4 * heads)
    mlp_wide = 2 * half + 3 * units
    attn_wide = 2 * half + 4 * heads
    cross_wide = base + folds * fold_width
    order_m, order_mo, order_f, order_fo, order_c, order_s, order_a = (
        order, order_turned, order, order, order, order_turned, order
    )
    bits_m, bits_mo, bits_f, bits_fo, bits_c, bits_s, bits_a = plain, turned, plain, plain, plain, turned, plain

    part_e1, u_e0, qkv_e, mixed_e = line.call(
        functools.partial(self_fwd_kernel, False, enc_len),
        [enc_wide, enc_low, ((enc_rows, 3 * heads), BF), ((enc_rows, heads), BF)],
        [patch_counts, x0, enc_gains, enc_qkv, enc_attn_out], "enc_attn_fwd",
    )
    other_e1 = pair_other(part_e1)
    part_d1, u_d0, qkv_d, mixed_d = line.call(
        functools.partial(self_fwd_kernel, True, dec_len),
        [dec_wide, dec_low, ((dec_rows, 3 * heads), BF), ((dec_rows, heads), BF)],
        [table_lengths, y0, dec_gains, dec_self_qkv, dec_self_out], "dec_self_fwd",
    )
    other_d1 = pair_other(part_d1)
    part_e2, x1, u_e1, gate, up, hidden = line.call(
        enc_mlp_fwd_kernel,
        [enc_wide, enc_wide, enc_low, ((enc_rows, units), F32), ((enc_rows, units), F32),
         ((enc_rows, units), BF)],
        [x0, part_e1, other_e1, enc_gains, enc_mlp_in, enc_mlp_out], "enc_mlp_fwd",
    )
    other_e2 = pair_other(part_e2)
    part_d2, x2, memory, y1, u_d1, query, kv, mixed_c = line.call(
        functools.partial(cross_fwd_kernel, enc_len),
        [dec_wide, enc_wide, enc_low, dec_wide, dec_low, ((dec_rows, heads), BF),
         ((enc_rows, 2 * heads), BF), ((dec_rows, heads), BF)],
        [patch_counts, x1, part_e2, other_e2, enc_gains, y0, part_d1, other_d1, dec_gains, dec_cross_qkv, dec_cross_out],
        "cross_fwd",
    )
    other_d2 = pair_other(part_d2)
    part_g3, y2, send_m, keep_m = line.call(
        dec_mlp_kernel,
        [dec_wide, dec_wide, ((dec_rows, mlp_wide), F32), ((dec_rows, mlp_wide), BF)],
        [y1, part_d2, other_d2, dec_gains, top, dec_mlp_in, dec_mlp_out, order_m, order_mo], "dec_mlp",
    )
    other_g3 = pair_other(part_g3)
    recv_m = swap(send_m, 0)
    products = line.call(
        functools.partial(weight_kernel, mlp_segments), mlp_groups, [keep_m, recv_m], "dec_mlp_weights"
    )
    sum_mo = Halving(products[2], products[3], bits_mo)
    sum_m = Halving(products[0], products[1], bits_m)
    part_m, g2, gain_d2, send_c, keep_c = line.call(
        functools.partial(cross_back_kernel, enc_len),
        [enc_wide, dec_wide, gain_row, ((dec_rows, cross_wide), F32), ((dec_rows, cross_wide), BF)],
        [patch_counts, part_g3, other_g3, y2, dec_gains, top, dec_cross_out, query, kv, dec_cross_qkv, order_c, u_d1,
         memory, mixed_c],
        "cross_back", scratch=[pltpu.VMEM((enc_rows, 2 * heads), BF)],
    )
    other_m = pair_other(part_m)
    recv_c = swap(send_c, 0)
    sum_mo.step(line)
    sum_m.step(line)
    part_g1, back2, gain_e2, send_f, keep_f = line.call(
        enc_mlp_back_kernel,
        [enc_wide, enc_wide, gain_row, ((enc_rows, mlp_wide), F32), ((enc_rows, mlp_wide), BF)],
        [part_m, other_m, x2, enc_gains, enc_mlp_out, gate, up, enc_mlp_in, order_f, order_fo, u_e1, hidden],
        "enc_mlp_back",
    )
    other_g1 = pair_other(part_g1)
    recv_f = swap(send_f, 0)
    products = line.call(
        functools.partial(weight_kernel, cross_segments), attn_group, [keep_c, recv_c], "cross_weights"
    )
    sum_c = Halving(products[0], products[1], bits_c)
    sum_mo.step(line)
    part_ge, back1, gain_e1, send_a, keep_a = line.call(
        functools.partial(self_back_kernel, False, enc_len),
        [enc_wide, enc_wide, gain_row, ((enc_rows, attn_wide), F32), ((enc_rows, attn_wide), BF)],
        [patch_counts, part_g1, other_g1, x1, enc_gains, back2, enc_attn_out, qkv_e, enc_qkv, order_a, u_e0, mixed_e],
        "enc_attn_back",
    )
    recv_a = swap(send_a, 0)
    (part_q,) = line.call(query_part_kernel, [dec_wide], [keep_c, dec_cross_qkv], "query_part")
    other_q = pair_other(part_q)
    other_ge = pair_other(part_ge)
    products = line.call(
        functools.partial(weight_kernel, mlp_segments), mlp_groups, [keep_f, recv_f], "enc_mlp_weights"
    )
    sum_fo = Halving(products[2], products[3], bits_fo)
    sum_f = Halving(products[0], products[1], bits_f)
    sum_m.step(line)
    sum_c.step(line)
    part_g0, g1, gain_d1, send_s, keep_s = line.call(
        functools.partial(self_back_kernel, True, dec_len),
        [dec_wide, dec_wide, gain_row, ((dec_rows, attn_wide), F32), ((dec_rows, attn_wide), BF)],
        [table_lengths, part_q, other_q, y1, dec_gains, g2, dec_self_out, qkv_d, dec_self_qkv, order_s, u_d0, mixed_d],
        "dec_self_back",
    )
    other_g0 = pair_other(part_g0)
    recv_s = swap(send_s, 0)
    products = line.call(
        functools.partial(weight_kernel, attn_segments), attn_group, [keep_s, recv_s], "dec_self_weights"
    )
    sum_s = Halving(products[0], products[1], bits_s)
    sum_c.step(line)
    sum_fo.step(line)
    products = line.call(
        functools.partial(weight_kernel, attn_segments), attn_group, [keep_a, recv_a], "enc_attn_weights"
    )
    sum_a = Halving(products[0], products[1], bits_a)
    (part_out,) = line.call(out_part_kernel, [dec_wide], [keep_m, dec_mlp_out], "dec_out_part")
    other_out = pair_other(part_out)
    enc_out, gain_e0, dec_out_grad, gain_d0 = line.call(
        last_kernel,
        [enc_low, gain_row, dec_low, gain_row],
        [part_ge, other_ge, x0, enc_gains, back1, part_g0, other_g0, y0, dec_gains, g1], "input_grads",
    )
    dec_out = (y2 + part_out + other_out).astype(BF)
    sum_f.step(line)
    sum_s.step(line)
    sum_fo.step(line)
    sum_a.step(line)
    sum_f.step(line)
    sum_s.step(line)
    sum_a.step(line)
    total_m, total_mo, total_c, total_s, total_f, total_fo, total_a = [
        group.finish() for group in (sum_m, sum_mo, sum_c, sum_s, sum_f, sum_fo, sum_a)
    ]

    gains = jnp.concatenate([gain_e0, gain_e1, gain_e2, gain_d0, gain_d1, gain_d2], 0)
    gains = gains.reshape((gains.shape[0],) + (2,) * bits + (-1,))
    me = lax.axis_index("dp")
    for bit in range(bits):
        axis = bits - bit
        mine = (me >> bit) & 1
        sent = lax.dynamic_index_in_dim(gains, 1 - mine, axis, keepdims=False)
        gains = lax.dynamic_index_in_dim(gains, mine, axis, keepdims=False) + swap(sent, bit)

    def stacked_of(total, count):
        return jnp.moveaxis(total.reshape(total.shape[0], count, -1), 1, 0)

    def attn_grads(total):
        return [stacked_of(total[:, : 3 * heads], 3), total[:, 3 * heads :].T]

    cross_in = jnp.concatenate([total_c[:, :heads], total_c[:, 2 * heads :]], 1)
    cross = [stacked_of(cross_in, 3), total_c[:, heads : 2 * heads].T]
    grads = (
        attn_grads(total_a) + [stacked_of(total_f, 2), total_fo.T] + [gains[:3]]
        + attn_grads(total_s) + cross + [stacked_of(total_m, 2), total_mo.T] + [gains[3:]]
    )
    return (
        dec_out.reshape(cotangent.shape),
        enc_out.reshape(enc_in.shape),
        dec_out_grad.reshape(dec_in.shape),
    ) + tuple(grads)


def solution(mesh):
    rows = P("dp", None, None)
    inner, outer = P(None, None, "mp"), P("mp", None)
    enc = (inner, outer, inner, outer, P())
    dec = (inner, outer, inner, outer, inner, outer, P())
    inner_grad, outer_grad, gain_grad = P(None, "dp", "mp"), P("mp", "dp"), P(None, "dp")
    return jax.shard_map(
        body,
        mesh=mesh,
        in_specs=(rows, rows, rows, P("dp"), P("dp")) + enc + dec,
        out_specs=(rows, rows, rows)
        + (inner_grad, outer_grad) * 2 + (gain_grad,)
        + (inner_grad, outer_grad) * 3 + (gain_grad,),
        check_vma=False,
    )
```

```python
import functools

import jax
import jax.numpy as jnp
from jax import lax
from jax.experimental import pallas as pl
from jax.experimental.pallas import tpu as pltpu
from jax.sharding import PartitionSpec as P

HEAD_DIM = 64
PAIR = 2 * HEAD_DIM
EPSILON = 1e-06
NEG_LARGE = -1e30
SCALE = HEAD_DIM ** (-0.5)
BF = jnp.bfloat16
F32 = jnp.float32
MIB = 1024 * 1024


def mm(left, right):
    return jnp.dot(left, right, preferred_element_type=F32)


def mm_nt(left, right):
    return lax.dot_general(left, right, (((1,), (1,)), ((), ())), preferred_element_type=F32)


def mm_tn(left, right):
    return lax.dot_general(left, right, (((0,), (0,)), ((), ())), preferred_element_type=F32)


def norm(hidden, gain):
    scaling = lax.rsqrt(jnp.mean(hidden * hidden, -1, keepdims=True) + EPSILON)
    return (hidden * scaling * gain).astype(BF)


def norm_back(grad, hidden, gain):
    scaling = lax.rsqrt(jnp.mean(hidden * hidden, -1, keepdims=True) + EPSILON)
    normed = hidden * scaling
    grad_hat = grad * gain
    grad_in = scaling * (grad_hat - normed * jnp.mean(grad_hat * normed, -1, keepdims=True))
    return grad_in, jnp.sum(grad * normed, 0, keepdims=True)


def gelu_parts(gate):
    slope = 0.7978845608028654
    square = gate * gate
    bent = jnp.tanh(slope * gate * (1.0 + 0.044715 * square))
    half = 0.5 * (1.0 + bent)
    value = gate * half
    rise = half + 0.5 * gate * (1.0 - bent * bent) * slope * (1.0 + 0.134145 * square)
    return value, rise


def stack_heads(pair):
    lane = lax.broadcasted_iota(jnp.int32, pair.shape, 1)
    zero = jnp.zeros_like(pair)
    return jnp.concatenate(
        [jnp.where(lane < HEAD_DIM, pair, zero), jnp.where(lane < HEAD_DIM, zero, pair)], 0
    )


def merge_heads(stacked):
    rows = stacked.shape[0] // 2
    lane = lax.broadcasted_iota(jnp.int32, (rows, PAIR), 1)
    return jnp.where(lane < HEAD_DIM, stacked[:rows], stacked[rows:])


def soft_of(stacked_query, keys, bias):
    scores = mm_nt(stacked_query, keys) * SCALE + bias
    expon = jnp.exp(scores - jnp.max(scores, -1, keepdims=True))
    return expon / jnp.sum(expon, -1, keepdims=True)


def pair_fwd(query, keys, values, bias):
    soft = soft_of(stack_heads(query), keys, bias)
    return merge_heads(mm(soft.astype(BF), values)).astype(BF)


def pair_back(query, keys, values, grad_out, bias):
    queries = stack_heads(query)
    soft = soft_of(queries, keys, bias)
    grads = stack_heads(grad_out)
    grad_values = mm_tn(soft.astype(BF), grads)
    grad_soft = mm_nt(grads, values)
    grad_scores = (
        soft * (grad_soft - jnp.sum(soft * grad_soft, -1, keepdims=True))
    ).astype(BF)
    grad_query = merge_heads(mm(grad_scores, keys)) * SCALE
    grad_keys = mm_tn(grad_scores, queries) * SCALE
    return grad_query.astype(BF), grad_keys.astype(BF), grad_values.astype(BF)


def length_bias(count, rows, length):
    col = lax.broadcasted_iota(jnp.int32, (2 * rows, length), 1)
    return jnp.where(col < count, 0.0, NEG_LARGE).astype(F32)


def causal_bias(counts, plots, length):
    shape = (plots * length, plots * length)
    row = lax.broadcasted_iota(jnp.int32, shape, 0)
    col = lax.broadcasted_iota(jnp.int32, shape, 1)
    bias = jnp.full(shape, NEG_LARGE, F32)
    for plot in range(plots):
        low = plot * length
        inside = (row >= low) & (row < low + length) & (col >= low)
        inside = inside & (col <= row) & (col < low + counts[plot])
        bias = jnp.where(inside, 0.0, bias)
    return jnp.concatenate([bias, bias], 0)


def pairs_of(width):
    return [slice(at, at + PAIR) for at in range(0, width, PAIR)]


def put(ref, at, value):
    last = at + value.shape[1]
    ref[:, at:last] = value.astype(ref.dtype)
    ref.flush(at, last)
    return last


def put_both(send, keep, at, value):
    put(send, at, value)
    return put(keep, at, value)


def put_cut(send, keep, at, value, order):
    ordered = mm(value, order[...])
    half = ordered.shape[1] // 2
    put(send, at, ordered[:, :half])
    return put(keep, at, ordered[:, half:])


def keys_of(causal, length, rows, counts):
    plots = rows // length
    if causal:
        return [(slice(0, rows), causal_bias(counts, plots, length))]
    return [(slice(p * length, (p + 1) * length), length_bias(counts[p], length, length)) for p in range(plots)]


def self_fwd_kernel(causal, length, counts, state, gain, stacked, outer, part, normed_ref, qkv, mixed):
    rows, width = state.shape[0], outer.shape[0]
    normed = norm(state[...].astype(F32), gain[0:1, :])
    normed_ref[...] = normed
    normed_ref.flush()
    for which in range(3):
        put(qkv, which * width, mm(normed, stacked[which]))
    for span, bias in keys_of(causal, length, rows, counts):
        for cols in pairs_of(width):
            mixed[span, cols] = pair_fwd(
                qkv[span, cols],
                qkv[span, width + cols.start : width + cols.stop],
                qkv[span, 2 * width + cols.start : 2 * width + cols.stop],
                bias,
            )
    mixed.flush()
    part[...] = mm(mixed[...], outer[...])


def enc_mlp_fwd_kernel(state, own, other, gain, inner, outer, part, state_ref, normed, gate_ref, up_ref, hidden):
    full = state[...].astype(F32) + own[...] + other[...]
    state_ref[...] = full
    normed[...] = norm(full, gain[1:2, :])
    flush(state_ref, normed)
    width = outer.shape[0]
    step = 256
    for at in range(0, width, step):
        cols = slice(at, at + step)
        gate = mm(normed[...], inner[0, :, cols])
        up = mm(normed[...], inner[1, :, cols])
        value, _ = gelu_parts(gate)
        put(gate_ref, at, gate)
        put(up_ref, at, up)
        put(hidden, at, value * up)
    part[...] = mm(hidden[...], outer[...])


def cross_fwd_kernel(
    length, counts, enc_state, enc_own, enc_other, enc_gain, dec_state, dec_own, dec_other, dec_gain, stacked, outer,
    part, enc_ref, memory, dec_ref, normed, query, kv, mixed,
):
    width = outer.shape[0]
    dec_full = dec_state[...].astype(F32) + dec_own[...] + dec_other[...]
    dec_ref[...] = dec_full
    normed[...] = norm(dec_full, dec_gain[1:2, :])
    flush(dec_ref, normed)
    put(query, 0, mm(normed[...], stacked[0]))
    enc_full = enc_state[...] + enc_own[...] + enc_other[...]
    enc_ref[...] = enc_full
    memory[...] = norm(enc_full, enc_gain[2:3, :])
    flush(enc_ref, memory)
    put(kv, 0, mm(memory[...], stacked[1]))
    put(kv, width, mm(memory[...], stacked[2]))
    plots = enc_state.shape[0] // length
    rows = dec_state.shape[0] // plots
    for plot in range(plots):
        bias = length_bias(counts[plot], rows, length)
        q_span = slice(plot * rows, (plot + 1) * rows)
        k_span = slice(plot * length, (plot + 1) * length)
        for cols in pairs_of(width):
            mixed[q_span, cols] = pair_fwd(
                query[q_span, cols],
                kv[k_span, cols],
                kv[k_span, width + cols.start : width + cols.stop],
                bias,
            )
    mixed.flush()
    part[...] = mm(mixed[...], outer[...])


def dec_mlp_kernel(
    state, own, other, gain, cotangent, inner, outer, order, order_outer, part, state_ref, send, keep
):
    full = state[...] + own[...] + other[...]
    state_ref[...] = full
    state_ref.flush()
    normed = norm(full, gain[2:3, :])
    low = cotangent[...]
    width, half = outer.shape[0], order.shape[0] // 2
    step = 256
    for col in range(0, width, step):
        cols = slice(col, col + step)
        gate = mm(normed, inner[0, :, cols])
        up = mm(normed, inner[1, :, cols])
        value, rise = gelu_parts(gate)
        grad_hidden = mm_nt(low, outer[cols, :])
        put_both(send, keep, half + col, (grad_hidden * up * rise).astype(BF))
        put_both(send, keep, half + width + col, (grad_hidden * value).astype(BF))
        put_both(send, keep, 2 * half + 2 * width + col, (value * up).astype(BF))
    part[...] = mm_nt(keep[:, half : half + width], inner[0]) + mm_nt(
        keep[:, half + width : half + 2 * width], inner[1]
    )
    part.flush()
    put_cut(send, keep, 0, normed, order)
    put_cut(send, keep, half + 2 * width, low, order_outer)


def sum_kernel(state, own, other, out):
    out[...] = (state[...] + own[...] + other[...]).astype(BF)


def out_part_kernel(keep, outer, part):
    part[...] = mm(keep[:, keep.shape[1] - outer.shape[0] :], outer[...])


def query_part_kernel(keep, stacked, part):
    half = stacked.shape[1] // 2
    part[...] = mm_nt(keep[:, half : half + stacked.shape[2]], stacked[0])


def cross_back_kernel(
    length, counts, own, other, state, gain, grad, outer, query, kv, stacked, order, normed, memory, mixed,
    part, grad_ref, gain_ref, send, keep, key_grads,
):
    grad_in, gain_ref[...] = norm_back(own[...] + other[...], state[...], gain[2:3, :])
    full = grad[...].astype(F32) + grad_in
    grad_ref[...] = full
    flush(gain_ref, grad_ref)
    low = full.astype(BF)
    width, half = outer.shape[0], order.shape[0] // 2
    grad_mixed = mm_nt(low, outer[...]).astype(BF)
    plots = kv.shape[0] // length
    rows = low.shape[0] // plots
    for plot in range(plots):
        bias = length_bias(counts[plot], rows, length)
        q_span = slice(plot * rows, (plot + 1) * rows)
        k_span = slice(plot * length, (plot + 1) * length)
        for cols in pairs_of(width):
            values = slice(width + cols.start, width + cols.stop)
            grad_query, grad_keys, grad_values = pair_back(
                query[q_span, cols], kv[k_span, cols], kv[k_span, values], grad_mixed[q_span, cols], bias
            )
            keep[q_span, half + cols.start : half + cols.stop] = grad_query
            send[q_span, half + cols.start : half + cols.stop] = grad_query.astype(F32)
            key_grads[k_span, cols] = grad_keys
            key_grads[k_span, values] = grad_values
    send.flush(half, half + width)
    keep.flush(half, half + width)
    part[...] = mm_nt(key_grads[:, :width], stacked[1]) + mm_nt(key_grads[:, width:], stacked[2])
    part.flush()
    put_cut(send, keep, 0, normed[...], order)
    at = put_cut(send, keep, half + width, low, order)
    base = put_both(send, keep, at, mixed[...])
    ordered = mm(memory[...], order[...])
    for fold in range(kv.shape[0] // low.shape[0]):
        span = slice(fold * low.shape[0], (fold + 1) * low.shape[0])
        put(send, base, ordered[span, :half])
        put(keep, base, ordered[span, half:])
        base = put_both(send, keep, base + half, key_grads[span, :])


def self_back_kernel(
    causal, length, counts, own, other, state, gain, grad, outer, qkv, stacked, order, normed, mixed,
    part, grad_ref, gain_ref, send, keep,
):
    grad_in, gain_ref[...] = norm_back(own[...] + other[...], state[...], gain[1:2, :])
    full = grad[...] + grad_in
    grad_ref[...] = full
    flush(gain_ref, grad_ref)
    low = full.astype(BF)
    width, half = outer.shape[0], order.shape[0] // 2
    grad_mixed = mm_nt(low, outer[...]).astype(BF)
    for span, bias in keys_of(causal, length, low.shape[0], counts):
        for cols in pairs_of(width):
            grads = pair_back(
                qkv[span, cols],
                qkv[span, width + cols.start : width + cols.stop],
                qkv[span, 2 * width + cols.start : 2 * width + cols.stop],
                grad_mixed[span, cols],
                bias,
            )
            for which, piece in enumerate(grads):
                start = half + which * width + cols.start
                keep[span, start : start + PAIR] = piece
                send[span, start : start + PAIR] = piece.astype(F32)
    send.flush(half, half + 3 * width)
    keep.flush(half, half + 3 * width)
    total = mm_nt(keep[:, half : half + width], stacked[0])
    total += mm_nt(keep[:, half + width : half + 2 * width], stacked[1])
    total += mm_nt(keep[:, half + 2 * width : half + 3 * width], stacked[2])
    part[...] = total
    part.flush()
    put_cut(send, keep, 0, normed[...], order)
    at = put_cut(send, keep, half + 3 * width, low, order)
    put_both(send, keep, at, mixed[...])


def enc_mlp_back_kernel(
    own, other, state, gain, outer, gate, up, inner, order, order_outer, normed, hidden,
    part, grad_ref, gain_ref, send, keep,
):
    full, gain_ref[...] = norm_back(own[...] + other[...], state[...], gain[2:3, :])
    grad_ref[...] = full
    flush(gain_ref, grad_ref)
    low = full.astype(BF)
    width, half = outer.shape[0], order.shape[0] // 2
    step = 256
    for col in range(0, width, step):
        cols = slice(col, col + step)
        value, rise = gelu_parts(gate[:, cols])
        grad_hidden = mm_nt(low, outer[cols, :])
        put_both(send, keep, half + col, (grad_hidden * up[:, cols] * rise).astype(BF))
        put_both(send, keep, half + width + col, (grad_hidden * value).astype(BF))
    part[...] = mm_nt(keep[:, half : half + width], inner[0]) + mm_nt(
        keep[:, half + width : half + 2 * width], inner[1]
    )
    part.flush()
    put_cut(send, keep, 0, normed[...], order)
    at = put_cut(send, keep, half + 2 * width, low, order_outer)
    for col in range(0, width, step):
        at = put_both(send, keep, at, hidden[:, col : col + step])


def last_kernel(
    enc_own, enc_other, enc_state, enc_gain, enc_grad, dec_own, dec_other, dec_state, dec_gain, dec_grad, order,
    e1, e2, d1, d2, enc_ref, dec_ref, send, keep,
):
    grad_in, e0 = norm_back(enc_own[...] + enc_other[...], enc_state[...].astype(F32), enc_gain[0:1, :])
    enc_ref[...] = (enc_grad[...] + grad_in).astype(BF)
    grad_in, d0 = norm_back(dec_own[...] + dec_other[...], dec_state[...].astype(F32), dec_gain[0:1, :])
    dec_ref[...] = (dec_grad[...] + grad_in).astype(BF)
    rest = jnp.concatenate(
        [e0, e1[...], e2[...], d0, d1[...], d2[...], jnp.zeros((122, e0.shape[1]), F32)], 0
    )
    total = None
    for _ in range(3):
        low = rest.astype(BF)
        rest = rest - low.astype(F32)
        moved = lax.dot_general(order[...], low, (((0,), (1,)), ((), ())), preferred_element_type=F32)
        total = moved if total is None else total + moved
    half = total.shape[0] // 2
    send[...] = total[:half]
    keep[...] = total[half:]


def gains_weight_kernel(segments, keep, recv, gains, other_gains, send_out, keep_out):
    weight_kernel(segments, keep, recv, send_out, keep_out)
    total = gains[...] + other_gains[...]
    half, first = send_out.shape[0], send_out.shape[1] - total.shape[1]
    send_out[:, first:] = total[:half]
    keep_out[:, first:] = total[half:]


def weight_kernel(segments, keep, recv, *outs):
    last_of = {(group, target): at for at, (_, _, _, _, group, target) in enumerate(segments)}
    started = set()
    for number, (cut, cut_width, first, columns, group, target) in enumerate(segments):
        send_out, keep_out = outs[2 * group], outs[2 * group + 1]
        left = jnp.concatenate([keep[:, cut : cut + cut_width], recv[:, cut : cut + cut_width].astype(BF)], 0)
        half = cut_width // 2
        step = 512 if columns % 512 == 0 else 384
        for at in range(0, columns, step):
            cols = slice(first + at, first + at + step)
            right = jnp.concatenate([keep[:, cols], recv[:, cols].astype(BF)], 0)
            total = mm_tn(left, right)
            into = slice(target + at, target + at + step)
            if (group, target) in started:
                total += jnp.concatenate([send_out[:, into], keep_out[:, into]], 0)
            send_out[:, into] = total[:half]
            keep_out[:, into] = total[half:]
            if last_of[group, target] == number:
                send_out.flush(into.start, into.stop)
                keep_out.flush(into.start, into.stop)
        started.add((group, target))


def halve_kernel(kept, recv, send_out, keep_out):
    rows = send_out.shape[0]
    send_out[...] = kept[:rows] + recv[:rows]
    send_out.flush()
    keep_out[...] = kept[rows:] + recv[rows:]


SMEM = pl.BlockSpec(memory_space=pltpu.SMEM)
VMEM = pl.BlockSpec(memory_space=pltpu.VMEM)
ANY = pl.BlockSpec(memory_space=pl.ANY)


COST = {"enc_attn_fwd": 2.3, "dec_self_fwd": 2.5, "enc_mlp_fwd": 1.7, "cross_fwd": 4.2, "dec_mlp": 2.7}
VMEM_LIMIT = 8


class Stored:
    def __init__(self, ref):
        self.ref = ref
        self.shape, self.dtype = ref.shape, ref.dtype

    def __getitem__(self, at):
        return self.ref[at]

    def __setitem__(self, at, value):
        self.ref[at] = value

    def flush(self, first=0, last=None):
        pass


class Columns:
    def __init__(self, refs):
        self.refs = refs
        self.shape = (refs[0].shape[0], sum(ref.shape[1] for ref in refs))
        self.dtype = refs[0].dtype

    def part(self, at):
        rows, cols = at
        first = cols.start or 0
        last = self.shape[1] if cols.stop is None else cols.stop
        for ref in self.refs:
            if last <= ref.shape[1]:
                return ref, (rows, slice(first, last))
            first, last = first - ref.shape[1], last - ref.shape[1]
        raise ValueError(at)

    def __getitem__(self, at):
        rows, cols = at
        first, last = cols.start or 0, self.shape[1] if cols.stop is None else cols.stop
        pieces, start = [], 0
        for ref in self.refs:
            low, high = max(first - start, 0), min(last - start, ref.shape[1])
            if low < high:
                pieces.append(ref[rows, low:high])
            start += ref.shape[1]
        return pieces[0] if len(pieces) == 1 else jnp.concatenate(pieces, 1)

    def __setitem__(self, at, value):
        ref, inside = self.part(at)
        ref[inside] = value

    def flush(self, first=0, last=None):
        pass


def flush(*refs):
    for ref in refs:
        ref.flush()


class Line:
    def __init__(self):
        self.last = None

    def call(self, kernel, outs, args, name, scratch=(), cost=None):
        flat_args, args_tree = jax.tree.flatten(list(args))
        widths = [out if isinstance(out, list) else [out] for out in outs]
        shapes = [jax.ShapeDtypeStruct(*out) for group in widths for out in group]
        in_specs = [VMEM if a.ndim > 1 else SMEM for a in flat_args]
        count, made = len(flat_args), len(shapes)
        operands = list(flat_args)
        if self.last is not None:
            operands.append(self.last)
            in_specs.append(ANY)
        total = len(operands)

        def run(*refs):
            ins = jax.tree.unflatten(args_tree, refs[:count])
            ins = [Columns(i) if isinstance(i, list) else i for i in ins]
            left = list(refs[total : total + made])
            results = []
            for group, out in zip(widths, outs):
                taken, left = [Stored(ref) for ref in left[: len(group)]], left[len(group) :]
                results.append(Columns(taken) if isinstance(out, list) else taken[0])
            kernel(*ins, *results, *refs[total + made :])

        cost = COST.get(name, 0.3) if cost is None else cost
        flat = pl.pallas_call(
            run,
            out_shape=shapes,
            in_specs=in_specs,
            out_specs=[VMEM] * made,
            scratch_shapes=list(scratch),
            compiler_params=pltpu.CompilerParams(vmem_limit_bytes=VMEM_LIMIT * MIB),
            cost_estimate=pl.CostEstimate(
                flops=int(cost * 1.15e9), bytes_accessed=int(cost * 3.69e6), transcendentals=0
            ),
            name=name,
        )(*operands)
        self.last = min(flat, key=lambda r: r.size)
        results, left = [], list(flat)
        for group, out in zip(widths, outs):
            results.append(left[: len(group)] if isinstance(out, list) else left[0])
            left = left[len(group) :]
        return results


def finish_kernel(pieces, kept, recv, *outs):
    for out, (first, count) in zip(outs, pieces):
        width = out.shape[-1]
        for i in range(count):
            cols = slice(first + i * width, first + (i + 1) * width)
            total = kept[:, cols] + recv[:, cols]
            if count > 1:
                out[i] = total
            else:
                out[...] = total


def tick_kernel(source, target):
    target[...] = source[0:1, 0:128]


def pair_other(part, name):
    with jax.named_scope("pair_" + name):
        return lax.ppermute(part, "mp", [(0, 1), (1, 0)])


def swap(value, bit, name):
    shards = lax.axis_size("dp")
    with jax.named_scope("swap_%s_bit%d" % (name, bit)):
        return lax.ppermute(value, "dp", [(i, i ^ (1 << bit)) for i in range(shards)])


def feature_order(features, bits_order):
    shards = lax.axis_size("dp")
    me = lax.axis_index("dp")
    block = features // shards
    column = jnp.arange(features, dtype=jnp.int32)
    place = column // block
    owner = jnp.zeros_like(column)
    count = len(bits_order)
    for at, bit in enumerate(bits_order):
        own = (place >> (count - 1 - at)) & 1
        owner = owner | ((((me >> bit) & 1) ^ (1 - own)) << bit)
    source = owner * block + column % block
    return (jnp.arange(features, dtype=jnp.int32)[:, None] == source[None, :]).astype(BF)


class Halving:
    def __init__(self, sent, kept, bits_order, name):
        self.bits = list(bits_order[1:])
        self.kept = kept
        self.name = name
        self.flying = swap(sent, self.bits[0], name)
        self.steps = 1

    def step(self, line):
        rows, columns = self.kept.shape[0] // 2, self.kept.shape[1]
        shape = ((rows, columns), F32)
        sent, self.kept = line.call(halve_kernel, [shape, shape], [self.kept, self.flying], "halve")
        self.flying = swap(sent, self.bits[self.steps], self.name)
        self.steps += 1

    def finish(self, line, *pieces):
        for bit in self.bits[self.steps :]:
            rows = self.kept.shape[0] // 2
            total = self.kept + self.flying
            self.kept, self.flying = total[rows:], swap(total[:rows], bit, self.name)
        rows = self.kept.shape[0]
        outs = [(((count, rows, width) if count > 1 else (rows, width)), F32) for _, count, width in pieces]
        return line.call(
            functools.partial(finish_kernel, [(first, count) for first, count, _ in pieces]),
            outs, [self.kept, self.flying], "finish",
        )


def body(
    enc_in, dec_in, cotangent, patch_counts, table_lengths, enc_qkv, enc_attn_out, enc_mlp_in, enc_mlp_out, enc_gains,
    dec_self_qkv, dec_self_out, dec_cross_qkv, dec_cross_out, dec_mlp_in, dec_mlp_out, dec_gains,
):
    plots, enc_len, features = enc_in.shape
    dec_len = dec_in.shape[1]
    enc_rows, dec_rows = plots * enc_len, plots * dec_len
    heads = enc_attn_out.shape[0]
    units = enc_mlp_out.shape[0]
    half = features // 2
    bits = lax.axis_size("dp").bit_length() - 1
    plain = tuple(range(bits))
    turned = (0, 2, 1) + tuple(range(3, bits))
    order = feature_order(features, plain)
    order_turned = feature_order(features, turned)
    x0 = enc_in.reshape(enc_rows, features)
    y0 = dec_in.reshape(dec_rows, features)
    top = cotangent.reshape(dec_rows, features)
    enc_wide, dec_wide = ((enc_rows, features), F32), ((dec_rows, features), F32)
    enc_low, dec_low = ((enc_rows, features), BF), ((dec_rows, features), BF)
    gain_row = ((1, features), F32)
    quarter = half // 2
    line = Line()

    def tick(cost=2.0):
        line.call(tick_kernel, [((1, 128), F32)], [enc_gains], "tick", cost=cost)

    def wide(rows, *columns):
        return [((rows, c), F32) for c in columns]

    def group(columns):
        return [((quarter, columns), F32)] * 2

    mlp_groups = group(2 * units) + group(units)

    mlp_segments = (
        (0, half, half, 2 * units, 0, 0),
        (half + 2 * units, half, 2 * half + 2 * units, units, 1, 0),
    )
    attn_segments = (
        (0, half, half, 3 * heads, 0, 0),
        (half + 3 * heads, half, 2 * half + 3 * heads, heads, 0, 3 * heads),
    )
    base, fold_width = 2 * half + 2 * heads, half + 2 * heads
    folds = enc_rows // dec_rows
    cross_segments = (
        (0, half, half, heads, 0, 0),
        (half + heads, half, 2 * half + heads, heads, 0, heads),
    ) + tuple(
        (base + f * fold_width, half, base + f * fold_width + half, 2 * heads, 0, 2 * heads) for f in range(folds)
    )
    attn_group = group(4 * heads)
    mlp_wide = 2 * half + 3 * units
    attn_wide = 2 * half + 4 * heads
    cross_wide = base + folds * fold_width
    order_m, order_mo, order_f, order_fo, order_c, order_s, order_a = (
        order, order_turned, order, order_turned, order_turned, order, order_turned
    )
    bits_m, bits_mo, bits_f, bits_fo, bits_c, bits_s, bits_a = plain, turned, plain, turned, turned, plain, turned

    tick(6.0)
    part_e1, u_e0, qkv_e, mixed_e = line.call(
        functools.partial(self_fwd_kernel, False, enc_len),
        [enc_wide, enc_low, ((enc_rows, 3 * heads), BF), ((enc_rows, heads), BF)],
        [patch_counts, x0, enc_gains, enc_qkv, enc_attn_out], "enc_attn_fwd",
    )
    other_e1 = pair_other(part_e1, "e1")
    part_d1, u_d0, qkv_d, mixed_d = line.call(
        functools.partial(self_fwd_kernel, True, dec_len),
        [dec_wide, dec_low, ((dec_rows, 3 * heads), BF), ((dec_rows, heads), BF)],
        [table_lengths, y0, dec_gains, dec_self_qkv, dec_self_out], "dec_self_fwd",
    )
    other_d1 = pair_other(part_d1, "d1")
    part_e2, x1, u_e1, gate, up, hidden = line.call(
        enc_mlp_fwd_kernel,
        [enc_wide, enc_wide, enc_low, ((enc_rows, units), F32), ((enc_rows, units), F32),
         ((enc_rows, units), BF)],
        [x0, part_e1, other_e1, enc_gains, enc_mlp_in, enc_mlp_out], "enc_mlp_fwd",
    )
    other_e2 = pair_other(part_e2, "e2")
    tick(6.0)
    part_d2, x2, memory, y1, u_d1, query, kv, mixed_c = line.call(
        functools.partial(cross_fwd_kernel, enc_len),
        [dec_wide, enc_wide, enc_low, dec_wide, dec_low, ((dec_rows, heads), BF),
         ((enc_rows, 2 * heads), BF), ((dec_rows, heads), BF)],
        [patch_counts, x1, part_e2, other_e2, enc_gains, y0, part_d1, other_d1, dec_gains, dec_cross_qkv, dec_cross_out],
        "cross_fwd",
    )
    other_d2 = pair_other(part_d2, "d2")
    tick(6.0)
    part_g3, y2, send_m, keep_m = line.call(
        dec_mlp_kernel,
        [dec_wide, dec_wide, ((dec_rows, mlp_wide), F32), ((dec_rows, mlp_wide), BF)],
        [y1, part_d2, other_d2, dec_gains, top, dec_mlp_in, dec_mlp_out, order_m, order_mo], "dec_mlp",
    )
    other_g3 = pair_other(part_g3, "g3")
    recv_m = swap(send_m, 0, "m")
    tick()
    products = line.call(
        functools.partial(weight_kernel, mlp_segments), mlp_groups, [keep_m, recv_m], "dec_mlp_weights"
    )
    sum_mo = Halving(products[2], products[3], bits_mo, "mo")
    sum_m = Halving(products[0], products[1], bits_m, "m")
    part_m, g2, gain_d2, send_c, keep_c = line.call(
        functools.partial(cross_back_kernel, enc_len),
        [enc_wide, dec_wide, gain_row, wide(dec_rows, half + heads, half + heads, *[half, 2 * heads] * folds), ((dec_rows, cross_wide), BF)],
        [patch_counts, part_g3, other_g3, y2, dec_gains, top, dec_cross_out, query, kv, dec_cross_qkv, order_c, u_d1,
         memory, mixed_c],
        "cross_back", scratch=[pltpu.VMEM((enc_rows, 2 * heads), BF)],
    )
    other_m = pair_other(part_m, "m")
    recv_c = [swap(part, 0, "c") for part in send_c]
    tick()
    sum_mo.step(line)
    products = line.call(
        functools.partial(weight_kernel, cross_segments), attn_group, [keep_c, recv_c], "cross_weights"
    )
    sum_c = Halving(products[0], products[1], bits_c, "c")
    sum_m.step(line)
    part_g1, back2, gain_e2, send_f, keep_f = line.call(
        enc_mlp_back_kernel,
        [enc_wide, enc_wide, gain_row, wide(enc_rows, half + units // 4, *[units // 2] * 3, half + units // 4, *[units // 2] * 2),
         ((enc_rows, mlp_wide), BF)],
        [part_m, other_m, x2, enc_gains, enc_mlp_out, gate, up, enc_mlp_in, order_f, order_fo, u_e1, hidden],
        "enc_mlp_back",
    )
    other_g1 = pair_other(part_g1, "g1")
    recv_f = [swap(part, 0, "f") for part in send_f]
    tick()
    products = line.call(
        functools.partial(weight_kernel, mlp_segments), mlp_groups, [keep_f, recv_f], "enc_mlp_weights"
    )
    sum_fo = Halving(products[2], products[3], bits_fo, "fo")
    sum_f = Halving(products[0], products[1], bits_f, "f")
    sum_mo.step(line)
    sum_c.step(line)
    part_ge, back1, gain_e1, send_a, keep_a = line.call(
        functools.partial(self_back_kernel, False, enc_len),
        [enc_wide, enc_wide, gain_row, wide(enc_rows, half, heads, heads, heads, half, heads), ((enc_rows, attn_wide), BF)],
        [patch_counts, part_g1, other_g1, x1, enc_gains, back2, enc_attn_out, qkv_e, enc_qkv, order_a, u_e0, mixed_e],
        "enc_attn_back",
    )
    (part_q,) = line.call(query_part_kernel, [dec_wide], [keep_c, dec_cross_qkv], "query_part")
    other_q = pair_other(part_q, "q")
    other_ge = pair_other(part_ge, "ge")
    recv_a = [swap(part, 0, "a") for part in send_a]
    tick()
    sum_m.step(line)
    products = line.call(
        functools.partial(weight_kernel, attn_segments), attn_group, [keep_a, recv_a], "enc_attn_weights"
    )
    sum_a = Halving(products[0], products[1], bits_a, "a")
    sum_c.step(line)
    part_g0, g1, gain_d1, send_s, keep_s = line.call(
        functools.partial(self_back_kernel, True, dec_len),
        [dec_wide, dec_wide, gain_row, wide(dec_rows, half + heads, 2 * heads, half + heads),
         ((dec_rows, attn_wide), BF)],
        [table_lengths, part_q, other_q, y1, dec_gains, g2, dec_self_out, qkv_d, dec_self_qkv, order_s, u_d0, mixed_d],
        "dec_self_back",
    )
    other_g0 = pair_other(part_g0, "g0")
    recv_s = [swap(part, 0, "s") for part in send_s]
    tick()
    (grad_mo,) = sum_mo.finish(line, (0, 1, units))
    sum_fo.step(line)
    (grad_m,) = sum_m.finish(line, (0, 2, units))
    enc_out, dec_out_grad, send_g, keep_g = line.call(
        last_kernel,
        [enc_low, dec_low, ((half, 128), F32), ((half, 128), F32)],
        [part_ge, other_ge, x0, enc_gains, back1, part_g0, other_g0, y0, dec_gains, g1, order_s, gain_e1, gain_e2,
         gain_d1, gain_d2],
        "input_grads",
    )
    recv_g = swap(send_g, 0, "g")
    sum_f.step(line)
    products = line.call(
        functools.partial(gains_weight_kernel, attn_segments), group(4 * heads + 128),
        [keep_s, recv_s, keep_g, recv_g], "dec_self_weights",
    )
    sum_s = Halving(products[0], products[1], bits_s, "s")
    grad_cq, grad_co, grad_ckv = sum_c.finish(line, (0, 1, heads), (heads, 1, heads), (2 * heads, 2, heads))
    (part_out,) = line.call(out_part_kernel, [dec_wide], [keep_m, dec_mlp_out], "dec_out_part")
    other_out = pair_other(part_out, "out")
    sum_fo.step(line)
    sum_a.step(line)
    sum_f.step(line)
    (grad_fo,) = sum_fo.finish(line, (0, 1, units))
    sum_a.step(line)
    sum_s.step(line)
    (dec_out,) = line.call(sum_kernel, [dec_low], [y2, part_out, other_out], "dec_out")
    (grad_f,) = sum_f.finish(line, (0, 2, units))
    grad_a, grad_ao = sum_a.finish(line, (0, 3, heads), (3 * heads, 1, heads))
    sum_s.step(line)
    grad_s, grad_so, gains = sum_s.finish(line, (0, 3, heads), (3 * heads, 1, heads), (4 * heads, 1, 128))
    gains = gains[:, :6].T
    grad_c = jnp.concatenate([grad_cq[None], grad_ckv], 0)
    grads = (
        grad_a, grad_ao.T, grad_f, grad_fo.T, gains[:3],
        grad_s, grad_so.T, grad_c, grad_co.T, grad_m, grad_mo.T, gains[3:],
    )
    return (
        dec_out.reshape(cotangent.shape),
        enc_out.reshape(enc_in.shape),
        dec_out_grad.reshape(dec_in.shape),
    ) + tuple(grads)


def solution(mesh):
    rows = P("dp", None, None)
    inner, outer = P(None, None, "mp"), P("mp", None)
    enc = (inner, outer, inner, outer, P())
    dec = (inner, outer, inner, outer, inner, outer, P())
    inner_grad, outer_grad, gain_grad = P(None, "dp", "mp"), P("mp", "dp"), P(None, "dp")
    return jax.shard_map(
        body,
        mesh=mesh,
        in_specs=(rows, rows, rows, P("dp"), P("dp")) + enc + dec,
        out_specs=(rows, rows, rows)
        + (inner_grad, outer_grad) * 2 + (gain_grad,)
        + (inner_grad, outer_grad) * 3 + (gain_grad,),
        check_vma=False,
    )
```

```python
import functools

import jax
import jax.numpy as jnp
from jax import lax
from jax.experimental import pallas as pl
from jax.experimental.pallas import tpu as pltpu
from jax.sharding import PartitionSpec as P

HEAD_DIM = 64
PAIR = 2 * HEAD_DIM
EPSILON = 1e-06
NEG_LARGE = -1e30
SCALE = HEAD_DIM ** (-0.5)
BF = jnp.bfloat16
F32 = jnp.float32
MIB = 1024 * 1024


def mm(left, right):
    return jnp.dot(left, right, preferred_element_type=F32)


def mm_nt(left, right):
    return lax.dot_general(left, right, (((1,), (1,)), ((), ())), preferred_element_type=F32)


def mm_tn(left, right):
    return lax.dot_general(left, right, (((0,), (0,)), ((), ())), preferred_element_type=F32)


def norm(hidden, gain):
    scaling = lax.rsqrt(jnp.mean(hidden * hidden, -1, keepdims=True) + EPSILON)
    return (hidden * scaling * gain).astype(BF)


def norm_back(grad, hidden, gain):
    scaling = lax.rsqrt(jnp.mean(hidden * hidden, -1, keepdims=True) + EPSILON)
    normed = hidden * scaling
    grad_hat = grad * gain
    grad_in = scaling * (grad_hat - normed * jnp.mean(grad_hat * normed, -1, keepdims=True))
    return grad_in, jnp.sum(grad * normed, 0, keepdims=True)


def gelu_parts(gate):
    slope = 0.7978845608028654
    square = gate * gate
    bent = jnp.tanh(slope * gate * (1.0 + 0.044715 * square))
    half = 0.5 * (1.0 + bent)
    value = gate * half
    rise = half + 0.5 * gate * (1.0 - bent * bent) * slope * (1.0 + 0.134145 * square)
    return value, rise


def stack_heads(pair):
    lane = lax.broadcasted_iota(jnp.int32, pair.shape, 1)
    zero = jnp.zeros_like(pair)
    return jnp.concatenate(
        [jnp.where(lane < HEAD_DIM, pair, zero), jnp.where(lane < HEAD_DIM, zero, pair)], 0
    )


def merge_heads(stacked):
    rows = stacked.shape[0] // 2
    lane = lax.broadcasted_iota(jnp.int32, (rows, PAIR), 1)
    return jnp.where(lane < HEAD_DIM, stacked[:rows], stacked[rows:])


def soft_of(stacked_query, keys, bias):
    scores = mm_nt(stacked_query, keys) * SCALE + bias
    expon = jnp.exp(scores - jnp.max(scores, -1, keepdims=True))
    return expon / jnp.sum(expon, -1, keepdims=True)


def pair_fwd(query, keys, values, bias):
    soft = soft_of(stack_heads(query), keys, bias)
    return merge_heads(mm(soft.astype(BF), values)).astype(BF)


def pair_back(query, keys, values, grad_out, bias):
    queries = stack_heads(query)
    soft = soft_of(queries, keys, bias)
    grads = stack_heads(grad_out)
    grad_values = mm_tn(soft.astype(BF), grads)
    grad_soft = mm_nt(grads, values)
    grad_scores = (
        soft * (grad_soft - jnp.sum(soft * grad_soft, -1, keepdims=True))
    ).astype(BF)
    grad_query = merge_heads(mm(grad_scores, keys)) * SCALE
    grad_keys = mm_tn(grad_scores, queries) * SCALE
    return grad_query.astype(BF), grad_keys.astype(BF), grad_values.astype(BF)


def length_bias(count, rows, length):
    col = lax.broadcasted_iota(jnp.int32, (2 * rows, length), 1)
    return jnp.where(col < count, 0.0, NEG_LARGE).astype(F32)


def causal_bias(counts, plots, length):
    shape = (plots * length, plots * length)
    row = lax.broadcasted_iota(jnp.int32, shape, 0)
    col = lax.broadcasted_iota(jnp.int32, shape, 1)
    bias = jnp.full(shape, NEG_LARGE, F32)
    for plot in range(plots):
        low = plot * length
        inside = (row >= low) & (row < low + length) & (col >= low)
        inside = inside & (col <= row) & (col < low + counts[plot])
        bias = jnp.where(inside, 0.0, bias)
    return jnp.concatenate([bias, bias], 0)


def pairs_of(width):
    return [slice(at, at + PAIR) for at in range(0, width, PAIR)]


def put(ref, at, value):
    last = at + value.shape[1]
    ref[:, at:last] = value.astype(ref.dtype)
    ref.flush(at, last)
    return last


def put_both(send, keep, at, value):
    put(send, at, value)
    return put(keep, at, value)


def put_cut(send, keep, at, value, order):
    ordered = mm(value, order[...])
    half = ordered.shape[1] // 2
    put(send, at, ordered[:, :half])
    return put(keep, at, ordered[:, half:])


def keys_of(causal, length, rows, counts, first=0):
    plots = rows // length
    if causal:
        return [(slice(0, rows), causal_bias(counts, plots, length))]
    return [
        (slice(p * length, (p + 1) * length), length_bias(counts[first + p], length, length)) for p in range(plots)
    ]


def self_fwd_kernel(causal, length, first, counts, state, gain, stacked, outer, part, saved):
    rows, width = part.shape[0], outer.shape[0]
    normed = norm(state[first * length : first * length + rows, :].astype(F32), gain[0:1, :])
    for which in range(3):
        put(saved, which * width, mm(normed, stacked[which]))
    for span, bias in keys_of(causal, length, rows, counts, first):
        for cols in pairs_of(width):
            mixed = slice(3 * width + cols.start, 3 * width + cols.stop)
            saved[span, mixed] = pair_fwd(
                saved[span, cols],
                saved[span, width + cols.start : width + cols.stop],
                saved[span, 2 * width + cols.start : 2 * width + cols.stop],
                bias,
            )
    part[...] = mm(saved[:, 3 * width :], outer[...])


def enc_mlp_fwd_kernel(first, state, own, other, gain, inner, outer, part, state_ref, pre):
    rows, width = part.shape[0], outer.shape[0]
    full = state[first * rows : (first + 1) * rows, :].astype(F32) + own[...] + other[...]
    state_ref[...] = full
    normed = norm(full, gain[1:2, :])
    step = 256
    total = None
    for at in range(0, width, step):
        cols = slice(at, at + step)
        gate = mm(normed, inner[0, :, cols])
        up = mm(normed, inner[1, :, cols])
        value, _ = gelu_parts(gate)
        pre[:, cols] = gate
        pre[:, width + at : width + at + step] = up
        add = mm((value * up).astype(BF), outer[cols, :])
        total = add if total is None else total + add
    part[...] = total


def cross_fwd_kernel(
    length, first, counts, enc_state, enc_own, enc_other, enc_gain, dec_state, dec_own, dec_other, dec_gain, stacked,
    outer, part, states, saved,
):
    rows, width = part.shape[0], outer.shape[0]
    span = slice(first * rows, (first + 1) * rows)
    dec_full = dec_state[span, :].astype(F32) + dec_own[span, :] + dec_other[span, :]
    states[length:, :] = dec_full
    normed = norm(dec_full, dec_gain[1:2, :])
    saved[length:, :width] = mm(normed, stacked[0]).astype(BF)
    enc_full = enc_state[...] + enc_own[...] + enc_other[...]
    states[:length, :] = enc_full
    memory = norm(enc_full, enc_gain[2:3, :])
    saved[:length, :width] = mm(memory, stacked[1]).astype(BF)
    saved[:length, width:] = mm(memory, stacked[2]).astype(BF)
    bias = length_bias(counts[first], rows, length)
    for cols in pairs_of(width):
        beside = slice(width + cols.start, width + cols.stop)
        saved[length:, beside] = pair_fwd(saved[length:, cols], saved[:length, cols], saved[:length, beside], bias)
    part[...] = mm(saved[length:, width:], outer[...])


def dec_mlp_kernel(
    state, own, other, gain, cotangent, inner, outer, order, order_outer, part, state_ref, send, keep
):
    full = state[...] + own[...] + other[...]
    state_ref[...] = full
    state_ref.flush()
    normed = norm(full, gain[2:3, :])
    low = cotangent[...]
    width, half = outer.shape[0], order.shape[0] // 2
    step = 256
    for col in range(0, width, step):
        cols = slice(col, col + step)
        gate = mm(normed, inner[0, :, cols])
        up = mm(normed, inner[1, :, cols])
        value, rise = gelu_parts(gate)
        grad_hidden = mm_nt(low, outer[cols, :])
        put_both(send, keep, half + col, (grad_hidden * up * rise).astype(BF))
        put_both(send, keep, half + width + col, (grad_hidden * value).astype(BF))
        put_both(send, keep, 2 * half + 2 * width + col, (value * up).astype(BF))
    part[...] = mm_nt(keep[:, half : half + width], inner[0]) + mm_nt(
        keep[:, half + width : half + 2 * width], inner[1]
    )
    part.flush()
    put_cut(send, keep, 0, normed, order)
    put_cut(send, keep, half + 2 * width, low, order_outer)


def sum_kernel(state, own, other, out):
    out[...] = (state[...] + own[...] + other[...]).astype(BF)


def out_part_kernel(keep, outer, part):
    part[...] = mm(keep[:, keep.shape[1] - outer.shape[0] :], outer[...])


def query_part_kernel(keep, stacked, part):
    half = stacked.shape[1] // 2
    part[...] = mm_nt(keep[:, half : half + stacked.shape[2]], stacked[0])


def cross_back_kernel(
    length, counts, own, other, state, gain, grad, outer, query, kv, stacked, order, dec_state, enc_state, enc_gain,
    part, grad_ref, gain_ref, send, keep, key_grads,
):
    grad_in, gain_ref[...] = norm_back(own[...] + other[...], state[...], gain[2:3, :])
    full = grad[...].astype(F32) + grad_in
    grad_ref[...] = full
    flush(gain_ref, grad_ref)
    low = full.astype(BF)
    width, half = outer.shape[0], order.shape[0] // 2
    grad_mixed = mm_nt(low, outer[...]).astype(BF)
    plots = kv.shape[0] // length
    rows = low.shape[0] // plots
    for plot in range(plots):
        bias = length_bias(counts[plot], rows, length)
        q_span = slice(plot * rows, (plot + 1) * rows)
        k_span = slice(plot * length, (plot + 1) * length)
        for cols in pairs_of(width):
            values = slice(width + cols.start, width + cols.stop)
            grad_query, grad_keys, grad_values = pair_back(
                query[q_span, cols], kv[k_span, cols], kv[k_span, values], grad_mixed[q_span, cols], bias
            )
            keep[q_span, half + cols.start : half + cols.stop] = grad_query
            send[q_span, half + cols.start : half + cols.stop] = grad_query.astype(F32)
            key_grads[k_span, cols] = grad_keys
            key_grads[k_span, values] = grad_values
    send.flush(half, half + width)
    keep.flush(half, half + width)
    part[...] = mm_nt(key_grads[:, :width], stacked[1]) + mm_nt(key_grads[:, width:], stacked[2])
    part.flush()
    put_cut(send, keep, 0, norm(dec_state[...], gain[1:2, :]), order)
    at = put_cut(send, keep, half + width, low, order)
    base = put_both(send, keep, at, query[:, width : 2 * width])
    ordered = mm(norm(enc_state[...], enc_gain[2:3, :]), order[...])
    for fold in range(kv.shape[0] // low.shape[0]):
        span = slice(fold * low.shape[0], (fold + 1) * low.shape[0])
        put(send, base, ordered[span, :half])
        put(keep, base, ordered[span, half:])
        base = put_both(send, keep, base + half, key_grads[span, :])


def self_back_kernel(
    causal, length, counts, own, other, state, gain, grad, outer, qkv, stacked, order, inputs,
    part, grad_ref, gain_ref, send, keep,
):
    grad_in, gain_ref[...] = norm_back(own[...] + other[...], state[...], gain[1:2, :])
    full = grad[...] + grad_in
    grad_ref[...] = full
    flush(gain_ref, grad_ref)
    low = full.astype(BF)
    width, half = outer.shape[0], order.shape[0] // 2
    grad_mixed = mm_nt(low, outer[...]).astype(BF)
    for span, bias in keys_of(causal, length, low.shape[0], counts):
        for cols in pairs_of(width):
            grads = pair_back(
                qkv[span, cols],
                qkv[span, width + cols.start : width + cols.stop],
                qkv[span, 2 * width + cols.start : 2 * width + cols.stop],
                grad_mixed[span, cols],
                bias,
            )
            for which, piece in enumerate(grads):
                start = half + which * width + cols.start
                keep[span, start : start + PAIR] = piece
                send[span, start : start + PAIR] = piece.astype(F32)
    send.flush(half, half + 3 * width)
    keep.flush(half, half + 3 * width)
    total = mm_nt(keep[:, half : half + width], stacked[0])
    total += mm_nt(keep[:, half + width : half + 2 * width], stacked[1])
    total += mm_nt(keep[:, half + 2 * width : half + 3 * width], stacked[2])
    part[...] = total
    part.flush()
    put_cut(send, keep, 0, norm(inputs[...].astype(F32), gain[0:1, :]), order)
    at = put_cut(send, keep, half + 3 * width, low, order)
    put_both(send, keep, at, qkv[:, 3 * width : 4 * width])


def enc_mlp_back_kernel(
    own, other, state, gain, outer, pre, inner, order, order_outer, middle,
    part, grad_ref, gain_ref, send, keep,
):
    full, gain_ref[...] = norm_back(own[...] + other[...], state[...], gain[2:3, :])
    grad_ref[...] = full
    flush(gain_ref, grad_ref)
    low = full.astype(BF)
    width, half = outer.shape[0], order.shape[0] // 2
    step = 256
    for col in range(0, width, step):
        cols = slice(col, col + step)
        value, rise = gelu_parts(pre[:, cols])
        up = pre[:, width + col : width + col + step]
        grad_hidden = mm_nt(low, outer[cols, :])
        put_both(send, keep, half + col, (grad_hidden * up * rise).astype(BF))
        put_both(send, keep, half + width + col, (grad_hidden * value).astype(BF))
        put_both(send, keep, 2 * half + 2 * width + col, (value * up).astype(BF))
    part[...] = mm_nt(keep[:, half : half + width], inner[0]) + mm_nt(
        keep[:, half + width : half + 2 * width], inner[1]
    )
    part.flush()
    put_cut(send, keep, 0, norm(middle[...], gain[1:2, :]), order)
    put_cut(send, keep, half + 2 * width, low, order_outer)


def last_kernel(
    enc_own, enc_other, enc_state, enc_gain, enc_grad, dec_own, dec_other, dec_state, dec_gain, dec_grad, order,
    e1, e2, d1, d2, enc_ref, dec_ref, send, keep,
):
    grad_in, e0 = norm_back(enc_own[...] + enc_other[...], enc_state[...].astype(F32), enc_gain[0:1, :])
    enc_ref[...] = (enc_grad[...] + grad_in).astype(BF)
    grad_in, d0 = norm_back(dec_own[...] + dec_other[...], dec_state[...].astype(F32), dec_gain[0:1, :])
    dec_ref[...] = (dec_grad[...] + grad_in).astype(BF)
    rest = jnp.concatenate(
        [e0, e1[...], e2[...], d0, d1[...], d2[...], jnp.zeros((122, e0.shape[1]), F32)], 0
    )
    total = None
    for _ in range(3):
        low = rest.astype(BF)
        rest = rest - low.astype(F32)
        moved = lax.dot_general(order[...], low, (((0,), (1,)), ((), ())), preferred_element_type=F32)
        total = moved if total is None else total + moved
    half = total.shape[0] // 2
    send[...] = total[:half]
    keep[...] = total[half:]


def gains_weight_kernel(segments, keep, recv, gains, other_gains, send_out, keep_out):
    weight_kernel(segments, keep, recv, send_out, keep_out)
    total = gains[...] + other_gains[...]
    half, first = send_out.shape[0], send_out.shape[1] - total.shape[1]
    send_out[:, first:] = total[:half]
    keep_out[:, first:] = total[half:]


def weight_kernel(segments, keep, recv, *outs):
    last_of = {(group, target): at for at, (_, _, _, _, group, target) in enumerate(segments)}
    started = set()
    for number, (cut, cut_width, first, columns, group, target) in enumerate(segments):
        send_out, keep_out = outs[2 * group], outs[2 * group + 1]
        left = jnp.concatenate([keep[:, cut : cut + cut_width], recv[:, cut : cut + cut_width].astype(BF)], 0)
        half = cut_width // 2
        step = 512 if columns % 512 == 0 else 384
        for at in range(0, columns, step):
            cols = slice(first + at, first + at + step)
            right = jnp.concatenate([keep[:, cols], recv[:, cols].astype(BF)], 0)
            total = mm_tn(left, right)
            into = slice(target + at, target + at + step)
            if (group, target) in started:
                total += jnp.concatenate([send_out[:, into], keep_out[:, into]], 0)
            send_out[:, into] = total[:half]
            keep_out[:, into] = total[half:]
            if last_of[group, target] == number:
                send_out.flush(into.start, into.stop)
                keep_out.flush(into.start, into.stop)
        started.add((group, target))


def halve_kernel(kept, recv, send_out, keep_out):
    rows = send_out.shape[0]
    send_out[...] = kept[:rows] + recv[:rows]
    send_out.flush()
    keep_out[...] = kept[rows:] + recv[rows:]


SMEM = pl.BlockSpec(memory_space=pltpu.SMEM)
VMEM = pl.BlockSpec(memory_space=pltpu.VMEM)
ANY = pl.BlockSpec(memory_space=pl.ANY)


COST = {
    "enc_attn_fwd": 2.3, "dec_self_fwd": 2.5, "enc_mlp_fwd": 1.7, "cross_fwd": 4.2, "dec_mlp": 2.7,
    "dec_out_part": 3, "finish_f": 0.3, "query_part": 3, "weights_f": 0.1, "cross_back": 3,
    "dec_self_back": 1, "halve_s": 3, "weights_m": 8, "weights_a": 0.3, "halve_m": 20,
    "halve_f": 0.3,
}
VMEM_LIMIT = 8

LINE = (
    "pause", "enc_attn_0", "enc_attn_1", "dec_self", "pause", "enc_mlp_0", "enc_mlp_1", "pause",
    "cross_0", "cross_1", "pause", "dec_mlp", "tick", "w_m", "tick", "cross_back",
    "h_mo", "h_m", "tick", "enc_mlp_back", "h_mo", "w_c", "w_f", "h_c",
    "tick", "query_part", "enc_attn_back", "e_mo", "h_m", "w_a", "e_m", "h_c",
    "dec_self_back", "h_f", "h_a", "input_grads", "e_c", "w_s", "h_f", "out_part",
    "h_s", "h_a", "e_f", "dec_out", "h_s", "e_a", "e_s",
)
ACROSS, NEAR, FAR = 1, 2, 3
HALVINGS = {"m": (ACROSS, NEAR, FAR), "mo": (NEAR, ACROSS, FAR), "c": (ACROSS, NEAR, FAR), "f": (ACROSS, NEAR, FAR), "a": (NEAR, ACROSS, FAR), "s": (ACROSS, NEAR, FAR)}
PARTS = {"m": 1, "c": 1, "f": 3, "a": 1, "s": 1}
TICK = 4
GAINS_WITH = "s"


class Stored:
    def __init__(self, ref):
        self.ref = ref
        self.shape, self.dtype = ref.shape, ref.dtype

    def __getitem__(self, at):
        return self.ref[at]

    def __setitem__(self, at, value):
        self.ref[at] = value

    def flush(self, first=0, last=None):
        pass


class Columns:
    def __init__(self, refs):
        self.refs = refs
        self.shape = (refs[0].shape[0], sum(ref.shape[1] for ref in refs))
        self.dtype = refs[0].dtype

    def __getitem__(self, at):
        rows, cols = at
        first, last = cols.start or 0, self.shape[1] if cols.stop is None else cols.stop
        pieces, start = [], 0
        for ref in self.refs:
            low, high = max(first - start, 0), min(last - start, ref.shape[1])
            if low < high:
                pieces.append(ref[rows, low:high])
            start += ref.shape[1]
        return pieces[0] if len(pieces) == 1 else jnp.concatenate(pieces, 1)

    def __setitem__(self, at, value):
        rows, cols = at
        first, last = cols.start or 0, self.shape[1] if cols.stop is None else cols.stop
        start = 0
        for ref in self.refs:
            low, high = max(first - start, 0), min(last - start, ref.shape[1])
            if low < high:
                ref[rows, low:high] = value[:, low + start - first : high + start - first]
            start += ref.shape[1]

    def flush(self, first=0, last=None):
        pass


class Stack:
    def __init__(self, *parts):
        self.parts = parts


class Rows:
    def __init__(self, refs, spans):
        self.refs = [ref.at[first:last] if (first, last) != (0, ref.shape[0]) else ref
                     for ref, (first, last) in zip(refs, spans)]
        self.heights = [last - first for first, last in spans]
        self.shape = (sum(self.heights),) + tuple(refs[0].shape[1:])
        self.dtype = refs[0].dtype

    def __getitem__(self, at):
        rows, cols = (slice(None), slice(None)) if at is Ellipsis else at
        first, last, _ = rows.indices(self.shape[0])
        pieces, start = [], 0
        for ref, height in zip(self.refs, self.heights):
            low, high = max(first - start, 0), min(last - start, height)
            if low < high:
                pieces.append(ref[low:high, cols])
            start += height
        return pieces[0] if len(pieces) == 1 else jnp.concatenate(pieces, 0)


def flush(*refs):
    for ref in refs:
        ref.flush()


class Line:
    def __init__(self):
        self.last = None

    def call(self, kernel, outs, args, name, scratch=(), cost=None):
        spans = [[part[1:] for part in a.parts] if isinstance(a, Stack) else None for a in args]
        args = [[part[0] for part in a.parts] if isinstance(a, Stack) else a for a in args]
        flat_args, args_tree = jax.tree.flatten(list(args))
        widths = [out if isinstance(out, list) else [out] for out in outs]
        shapes = [jax.ShapeDtypeStruct(*out) for group in widths for out in group]
        in_specs = [VMEM if a.ndim > 1 else SMEM for a in flat_args]
        count, made = len(flat_args), len(shapes)
        operands = list(flat_args)
        if self.last is not None:
            operands.append(self.last)
            in_specs.append(ANY)
        total = len(operands)

        def run(*refs):
            ins = jax.tree.unflatten(args_tree, refs[:count])
            ins = [Rows(i, span) if span else Columns(i) if isinstance(i, list) else i for i, span in zip(ins, spans)]
            left = list(refs[total : total + made])
            results = []
            for group, out in zip(widths, outs):
                taken, left = [Stored(ref) for ref in left[: len(group)]], left[len(group) :]
                results.append(Columns(taken) if isinstance(out, list) else taken[0])
            kernel(*ins, *results, *refs[total + made :])

        cost = COST.get(name, 0.3) if cost is None else cost
        flat = pl.pallas_call(
            run,
            out_shape=shapes,
            in_specs=in_specs,
            out_specs=[VMEM] * made,
            scratch_shapes=list(scratch),
            compiler_params=pltpu.CompilerParams(vmem_limit_bytes=VMEM_LIMIT * MIB),
            cost_estimate=pl.CostEstimate(
                flops=int(cost * 1.15e9), bytes_accessed=int(cost * 3.69e6), transcendentals=0
            ),
            name=name,
        )(*operands)
        self.last = min(flat, key=lambda r: r.size)
        results, left = [], list(flat)
        for group, out in zip(widths, outs):
            results.append(left[: len(group)] if isinstance(out, list) else left[0])
            left = left[len(group) :]
        return results


def finish_kernel(pieces, kept, recv, *outs):
    for out, (first, count) in zip(outs, pieces):
        width = out.shape[-1]
        for i in range(count):
            cols = slice(first + i * width, first + (i + 1) * width)
            total = kept[:, cols] + recv[:, cols]
            if count > 1:
                out[i] = total
            else:
                out[...] = total


def tick_kernel(source, target):
    target[...] = source[0:1, 0:128]


def pair_other(part, name):
    with jax.named_scope("pair_" + name):
        return lax.ppermute(part, "mp", [(0, 1), (1, 0)])


def swap(value, bit, name):
    shards = lax.axis_size("dp")
    with jax.named_scope("swap_%s_bit%d" % (name, bit)):
        return lax.ppermute(value, "dp", [(i, i ^ (1 << bit)) for i in range(shards)])


def feature_order(features, bits_order):
    shards = lax.axis_size("dp")
    me = lax.axis_index("dp")
    block = features // shards
    column = jnp.arange(features, dtype=jnp.int32)
    place = column // block
    owner = jnp.zeros_like(column)
    count = len(bits_order)
    for at, bit in enumerate(bits_order):
        own = (place >> (count - 1 - at)) & 1
        owner = owner | ((((me >> bit) & 1) ^ (1 - own)) << bit)
    source = owner * block + column % block
    return (jnp.arange(features, dtype=jnp.int32)[:, None] == source[None, :]).astype(BF)


class Halving:
    def __init__(self, sent, kept, bits_order, name):
        self.bits = list(bits_order[1:])
        self.kept = kept
        self.name = name
        self.flying = swap(sent, self.bits[0], name)
        self.steps = 1

    def step(self, line):
        rows, columns = self.kept.shape[0] // 2, self.kept.shape[1]
        shape = ((rows, columns), F32)
        sent, self.kept = line.call(halve_kernel, [shape, shape], [self.kept, self.flying], "halve_" + self.name)
        self.flying = swap(sent, self.bits[self.steps], self.name)
        self.steps += 1

    def finish(self, line, *pieces):
        for bit in self.bits[self.steps :]:
            rows = self.kept.shape[0] // 2
            total = self.kept + self.flying
            self.kept, self.flying = total[rows:], swap(total[:rows], bit, self.name)
        rows = self.kept.shape[0]
        outs = [(((count, rows, width) if count > 1 else (rows, width)), F32) for _, count, width in pieces]
        return line.call(
            functools.partial(finish_kernel, [(first, count) for first, count, _ in pieces]),
            outs, [self.kept, self.flying], "finish_" + self.name,
        )


def body(
    enc_in, dec_in, cotangent, patch_counts, table_lengths, enc_qkv, enc_attn_out, enc_mlp_in, enc_mlp_out, enc_gains,
    dec_self_qkv, dec_self_out, dec_cross_qkv, dec_cross_out, dec_mlp_in, dec_mlp_out, dec_gains,
):
    plots, enc_len, features = enc_in.shape
    dec_len = dec_in.shape[1]
    enc_rows, dec_rows = plots * enc_len, plots * dec_len
    heads = enc_attn_out.shape[0]
    units = enc_mlp_out.shape[0]
    half = features // 2
    bits = lax.axis_size("dp").bit_length() - 1
    orders = {}

    def halving(*first):
        chosen = [0] + [bit for bit in first if bit < bits]
        chosen = tuple(chosen + [bit for bit in range(bits) if bit not in chosen])
        if chosen not in orders:
            orders[chosen] = feature_order(features, chosen)
        return chosen, orders[chosen]

    halvings = {name: halving(*first) for name, first in HALVINGS.items()}
    bits_of = {name: pair[0] for name, pair in halvings.items()}
    order_of = {name: pair[1] for name, pair in halvings.items()}
    x0 = enc_in.reshape(enc_rows, features)
    y0 = dec_in.reshape(dec_rows, features)
    top = cotangent.reshape(dec_rows, features)
    enc_wide, dec_wide = ((enc_rows, features), F32), ((dec_rows, features), F32)
    enc_low, dec_low = ((enc_rows, features), BF), ((dec_rows, features), BF)
    gain_row = ((1, features), F32)
    quarter = half // 2
    line = Line()

    def tick(cost=TICK):
        line.call(tick_kernel, [((1, 128), F32)], [enc_gains], "tick", cost=cost)

    def parts_of(name, rows, width):
        count, tiles = PARTS[name], width // 128
        edges = [128 * (tiles * i // count) for i in range(count + 1)]
        return [((rows, high - low), F32) for low, high in zip(edges, edges[1:])]

    def swap_cores(name, parts):
        return [swap(part, 0, name) for part in parts]

    def group(columns):
        return [((quarter, columns), F32)] * 2

    def mlp_of(name):
        apart = name + "o" in HALVINGS
        target = (1, 0) if apart else (0, 2 * units)
        segments = (
            (0, half, half, 2 * units, 0, 0),
            (half + 2 * units, half, 2 * half + 2 * units, units) + target,
        )
        return segments, group(2 * units) + group(units) if apart else group(3 * units)

    attn_segments = (
        (0, half, half, 3 * heads, 0, 0),
        (half + 3 * heads, half, 2 * half + 3 * heads, heads, 0, 3 * heads),
    )
    base, fold_width = 2 * half + 2 * heads, half + 2 * heads
    folds = enc_rows // dec_rows
    cross_segments = (
        (0, half, half, heads, 0, 0),
        (half + heads, half, 2 * half + heads, heads, 0, heads),
    ) + tuple(
        (base + f * fold_width, half, base + f * fold_width + half, 2 * heads, 0, 2 * heads) for f in range(folds)
    )
    attn_group = group(4 * heads)
    mlp_wide = 2 * half + 3 * units
    attn_wide = 2 * half + 4 * heads
    cross_wide = base + folds * fold_width
    v, sums, grad_of = {}, {}, {}

    def pause():
        tick(6.0)

    def enc_attn(p):
        v["part_e1", p], v["enc_saved", p] = line.call(
            functools.partial(self_fwd_kernel, False, enc_len, p),
            [((enc_len, features), F32), ((enc_len, 4 * heads), BF)],
            [patch_counts, x0, enc_gains, enc_qkv, enc_attn_out], "enc_attn_fwd",
        )
        v["other_e1", p] = pair_other(v["part_e1", p], "e1")

    def dec_self():
        v["part_d1"], v["dec_saved"] = line.call(
            functools.partial(self_fwd_kernel, True, dec_len, 0),
            [dec_wide, ((dec_rows, 4 * heads), BF)],
            [table_lengths, y0, dec_gains, dec_self_qkv, dec_self_out], "dec_self_fwd",
        )
        v["other_d1"] = pair_other(v["part_d1"], "d1")

    def enc_mlp(p):
        v["part_e2", p], v["x1", p], v["pre", p] = line.call(
            functools.partial(enc_mlp_fwd_kernel, p),
            [((enc_len, features), F32), ((enc_len, features), F32), ((enc_len, 2 * units), F32)],
            [x0, v["part_e1", p], v["other_e1", p], enc_gains, enc_mlp_in, enc_mlp_out], "enc_mlp_fwd",
        )
        v["other_e2", p] = pair_other(v["part_e2", p], "e2")

    def cross(p):
        v["part_d2", p], v["states", p], v["saved", p] = line.call(
            functools.partial(cross_fwd_kernel, enc_len, p),
            [((dec_len, features), F32), ((enc_len + dec_len, features), F32), ((enc_len + dec_len, 2 * heads), BF)],
            [patch_counts, v["x1", p], v["part_e2", p], v["other_e2", p], enc_gains, y0, v["part_d1"], v["other_d1"],
             dec_gains, dec_cross_qkv, dec_cross_out],
            "cross_fwd",
        )
        v["other_d2", p] = pair_other(v["part_d2", p], "d2")

    def stack(name, first, last):
        return Stack(*[(v[name, p], first, last) for p in range(plots)])

    def enc_part(name):
        return stack(name, 0, enc_len)

    def dec_part(name):
        return stack(name, enc_len, enc_len + dec_len)

    def dec_mlp():
        v["part_g3"], v["y2"], send, v["keep_m"] = line.call(
            dec_mlp_kernel,
            [dec_wide, dec_wide, parts_of("m", dec_rows, mlp_wide), ((dec_rows, mlp_wide), BF)],
            [dec_part("states"), stack("part_d2", 0, dec_len), stack("other_d2", 0, dec_len), dec_gains, top,
             dec_mlp_in, dec_mlp_out, order_of["m"], order_of.get("mo", order_of["m"])],
            "dec_mlp",
        )
        v["other_g3"] = pair_other(v["part_g3"], "g3")
        v["recv_m"] = swap_cores("m", send)


    def start_sums(name, products):
        for group_name, pair in zip((name, name + "o"), zip(products[::2], products[1::2])):
            sums[group_name] = Halving(pair[0], pair[1], bits_of[group_name], group_name)

    def mlp_weights(name, keep, recv):
        segments, groups = mlp_of(name)
        start_sums(
            name, line.call(functools.partial(weight_kernel, segments), groups, [keep, recv], "weights_" + name)
        )

    def dec_mlp_weights():
        mlp_weights("m", v["keep_m"], v["recv_m"])

    def cross_back():
        v["part_m"], v["g2"], v["gain_d2"], send, v["keep_c"] = line.call(
            functools.partial(cross_back_kernel, enc_len),
            [enc_wide, dec_wide, gain_row, parts_of("c", dec_rows, cross_wide), ((dec_rows, cross_wide), BF)],
            [patch_counts, v["part_g3"], v["other_g3"], v["y2"], dec_gains, top, dec_cross_out, dec_part("saved"),
             enc_part("saved"), dec_cross_qkv, order_of["c"], dec_part("states"), enc_part("states"), enc_gains],
            "cross_back", scratch=[pltpu.VMEM((enc_rows, 2 * heads), BF)],
        )
        v["other_m"] = pair_other(v["part_m"], "m")
        v["recv_c"] = swap_cores("c", send)

    def cross_weights():
        start_sums("c", line.call(
            functools.partial(weight_kernel, cross_segments), attn_group, [v["keep_c"], v["recv_c"]], "weights_c"
        ))

    def enc_mlp_back():
        v["part_g1"], v["back2"], v["gain_e2"], send, v["keep_f"] = line.call(
            enc_mlp_back_kernel,
            [enc_wide, enc_wide, gain_row, parts_of("f", enc_rows, mlp_wide), ((enc_rows, mlp_wide), BF)],
            [v["part_m"], v["other_m"], enc_part("states"), enc_gains, enc_mlp_out, enc_part("pre"), enc_mlp_in,
             order_of["f"], order_of.get("fo", order_of["f"]), enc_part("x1")],
            "enc_mlp_back",
        )
        v["other_g1"] = pair_other(v["part_g1"], "g1")
        v["recv_f"] = swap_cores("f", send)

    def enc_mlp_weights():
        mlp_weights("f", v["keep_f"], v["recv_f"])

    def enc_attn_back():
        v["part_ge"], v["back1"], v["gain_e1"], send, v["keep_a"] = line.call(
            functools.partial(self_back_kernel, False, enc_len),
            [enc_wide, enc_wide, gain_row, parts_of("a", enc_rows, attn_wide), ((enc_rows, attn_wide), BF)],
            [patch_counts, v["part_g1"], v["other_g1"], enc_part("x1"), enc_gains, v["back2"], enc_attn_out,
             enc_part("enc_saved"), enc_qkv, order_of["a"], x0],
            "enc_attn_back",
        )
        v["other_ge"] = pair_other(v["part_ge"], "ge")
        v["recv_a"] = swap_cores("a", send)

    def query_part():
        (v["part_q"],) = line.call(query_part_kernel, [dec_wide], [v["keep_c"], dec_cross_qkv], "query_part")
        v["other_q"] = pair_other(v["part_q"], "q")

    def dec_self_back():
        v["part_g0"], v["g1"], v["gain_d1"], send, v["keep_s"] = line.call(
            functools.partial(self_back_kernel, True, dec_len),
            [dec_wide, dec_wide, gain_row, parts_of("s", dec_rows, attn_wide), ((dec_rows, attn_wide), BF)],
            [table_lengths, v["part_q"], v["other_q"], dec_part("states"), dec_gains, v["g2"], dec_self_out,
             v["dec_saved"], dec_self_qkv, order_of["s"], y0],
            "dec_self_back",
        )
        v["other_g0"] = pair_other(v["part_g0"], "g0")
        v["recv_s"] = swap_cores("s", send)

    def input_grads():
        v["enc_out"], v["dec_out_grad"], send, v["keep_g"] = line.call(
            last_kernel,
            [enc_low, dec_low, ((half, 128), F32), ((half, 128), F32)],
            [v["part_ge"], v["other_ge"], x0, enc_gains, v["back1"], v["part_g0"], v["other_g0"], y0, dec_gains,
             v["g1"], order_of[GAINS_WITH], v["gain_e1"], v["gain_e2"], v["gain_d1"], v["gain_d2"]],
            "input_grads",
        )
        v["recv_g"] = swap(send, 0, "g")

    def attn_weights(name):
        if name == GAINS_WITH:
            products = line.call(
                functools.partial(gains_weight_kernel, attn_segments), group(4 * heads + 128),
                [v["keep_" + name], v["recv_" + name], v["keep_g"], v["recv_g"]], "weights_" + name,
            )
        else:
            products = line.call(
                functools.partial(weight_kernel, attn_segments), attn_group,
                [v["keep_" + name], v["recv_" + name]], "weights_" + name,
            )
        start_sums(name, products)

    def out_part():
        (v["part_out"],) = line.call(out_part_kernel, [dec_wide], [v["keep_m"], dec_mlp_out], "dec_out_part")
        v["other_out"] = pair_other(v["part_out"], "out")

    def dec_out_sum():
        (v["dec_out"],) = line.call(sum_kernel, [dec_low], [v["y2"], v["part_out"], v["other_out"]], "dec_out")

    attn_pieces = ((0, 3, heads), (3 * heads, 1, heads))
    ends = {
        "m": ((0, 2, units),), "f": ((0, 2, units),), "mo": ((0, 1, units),), "fo": ((0, 1, units),),
        "c": ((0, 1, heads), (heads, 1, heads), (2 * heads, 2, heads)), "a": attn_pieces, "s": attn_pieces,
    }
    for name in ("m", "f"):
        if name + "o" not in HALVINGS:
            ends[name] += ((2 * units, 1, units),)
    ends[GAINS_WITH] += ((4 * heads, 1, 128),)
    stages = {
        "tick": tick, "pause": pause, "dec_self": dec_self, "dec_mlp": dec_mlp, "w_m": dec_mlp_weights,
        "cross_back": cross_back, "w_c": cross_weights, "enc_mlp_back": enc_mlp_back,
        "w_f": enc_mlp_weights, "enc_attn_back": enc_attn_back, "query_part": query_part,
        "w_a": functools.partial(attn_weights, "a"), "dec_self_back": dec_self_back, "input_grads": input_grads,
        "w_s": functools.partial(attn_weights, "s"), "out_part": out_part, "dec_out": dec_out_sum,
    }
    for name, stage in (("enc_attn", enc_attn), ("enc_mlp", enc_mlp), ("cross", cross)):
        for p in range(plots):
            stages["%s_%d" % (name, p)] = functools.partial(stage, p)
    for stage in LINE:
        kind, _, name = stage.partition("_")
        if stage in stages:
            stages[stage]()
        elif kind == "h":
            sums[name].step(line)
        else:
            grad_of[name] = sums[name].finish(line, *ends[name])
    mlp_grads = {
        name: grad_of[name] if name + "o" not in HALVINGS else grad_of[name] + grad_of[name + "o"] for name in ("m", "f")
    }
    gains = grad_of[GAINS_WITH][2]
    gains = gains[:, :6].T
    grad_c = jnp.concatenate([grad_of["c"][0][None], grad_of["c"][2]], 0)
    grads = (
        grad_of["a"][0], grad_of["a"][1].T, mlp_grads["f"][0], mlp_grads["f"][1].T, gains[:3],
        grad_of["s"][0], grad_of["s"][1].T, grad_c, grad_of["c"][1].T, mlp_grads["m"][0], mlp_grads["m"][1].T,
        gains[3:],
    )
    return (
        v["dec_out"].reshape(cotangent.shape),
        v["enc_out"].reshape(enc_in.shape),
        v["dec_out_grad"].reshape(dec_in.shape),
    ) + grads


def solution(mesh):
    rows = P("dp", None, None)
    inner, outer = P(None, None, "mp"), P("mp", None)
    enc = (inner, outer, inner, outer, P())
    dec = (inner, outer, inner, outer, inner, outer, P())
    inner_grad, outer_grad, gain_grad = P(None, "dp", "mp"), P("mp", "dp"), P(None, "dp")
    return jax.shard_map(
        body,
        mesh=mesh,
        in_specs=(rows, rows, rows, P("dp"), P("dp")) + enc + dec,
        out_specs=(rows, rows, rows)
        + (inner_grad, outer_grad) * 2 + (gain_grad,)
        + (inner_grad, outer_grad) * 3 + (gain_grad,),
        check_vma=False,
    )
```

```python
import functools

import jax
import jax.numpy as jnp
from jax import lax
from jax.experimental import pallas as pl
from jax.experimental.pallas import tpu as pltpu
from jax.sharding import PartitionSpec as P

HEAD_DIM = 64
PAIR = 2 * HEAD_DIM
EPSILON = 1e-06
NEG_LARGE = -1e30
SCALE = HEAD_DIM ** (-0.5)
BF = jnp.bfloat16
F32 = jnp.float32
MIB = 1024 * 1024


def mm(left, right):
    return jnp.dot(left, right, preferred_element_type=F32)


def mm_nt(left, right):
    return lax.dot_general(left, right, (((1,), (1,)), ((), ())), preferred_element_type=F32)


def mm_tn(left, right):
    return lax.dot_general(left, right, (((0,), (0,)), ((), ())), preferred_element_type=F32)


def scaled(hidden):
    return hidden * lax.rsqrt(jnp.mean(hidden * hidden, -1, keepdims=True) + EPSILON)


def norm(hidden, gain):
    return (scaled(hidden) * gain).astype(BF)


def norm_back(grad, hidden, gain):
    scaling = lax.rsqrt(jnp.mean(hidden * hidden, -1, keepdims=True) + EPSILON)
    normed = hidden * scaling
    grad_hat = grad * gain
    return scaling * (grad_hat - normed * jnp.mean(grad_hat * normed, -1, keepdims=True)), normed


def gain_part(part, normed):
    return jnp.sum(part * normed, 0, keepdims=True)


def gelu_parts(gate):
    slope = 0.7978845608028654
    square = gate * gate
    bent = jnp.tanh(slope * gate * (1.0 + 0.044715 * square))
    half = 0.5 * (1.0 + bent)
    value = gate * half
    rise = half + 0.5 * gate * (1.0 - bent * bent) * slope * (1.0 + 0.134145 * square)
    return value, rise


def stack_heads(pair):
    lane = lax.broadcasted_iota(jnp.int32, pair.shape, 1)
    zero = jnp.zeros_like(pair)
    return jnp.concatenate(
        [jnp.where(lane < HEAD_DIM, pair, zero), jnp.where(lane < HEAD_DIM, zero, pair)], 0
    )


def merge_heads(stacked):
    rows = stacked.shape[0] // 2
    lane = lax.broadcasted_iota(jnp.int32, (rows, PAIR), 1)
    return jnp.where(lane < HEAD_DIM, stacked[:rows], stacked[rows:])


def soft_of(stacked_query, keys, bias):
    scores = mm_nt(stacked_query, keys) * SCALE + bias
    expon = jnp.exp(scores - jnp.max(scores, -1, keepdims=True))
    return expon / jnp.sum(expon, -1, keepdims=True)


def pair_fwd(query, keys, values, bias):
    soft = soft_of(stack_heads(query), keys, bias)
    return merge_heads(mm(soft.astype(BF), values)).astype(BF)


def pair_back(query, keys, values, grad_out, bias):
    queries = stack_heads(query)
    soft = soft_of(queries, keys, bias)
    grads = stack_heads(grad_out)
    grad_values = mm_tn(soft.astype(BF), grads)
    grad_soft = mm_nt(grads, values)
    grad_scores = (
        soft * (grad_soft - jnp.sum(soft * grad_soft, -1, keepdims=True))
    ).astype(BF)
    grad_query = merge_heads(mm(grad_scores, keys)) * SCALE
    grad_keys = mm_tn(grad_scores, queries) * SCALE
    return grad_query.astype(BF), grad_keys.astype(BF), grad_values.astype(BF)


def length_bias(count, rows, length):
    col = lax.broadcasted_iota(jnp.int32, (2 * rows, length), 1)
    return jnp.where(col < count, 0.0, NEG_LARGE).astype(F32)


def causal_bias(counts, plots, length):
    shape = (plots * length, plots * length)
    row = lax.broadcasted_iota(jnp.int32, shape, 0)
    col = lax.broadcasted_iota(jnp.int32, shape, 1)
    bias = jnp.full(shape, NEG_LARGE, F32)
    for plot in range(plots):
        low = plot * length
        inside = (row >= low) & (row < low + length) & (col >= low)
        inside = inside & (col <= row) & (col < low + counts[plot])
        bias = jnp.where(inside, 0.0, bias)
    return jnp.concatenate([bias, bias], 0)


def pairs_of(width):
    return [slice(at, at + PAIR) for at in range(0, width, PAIR)]


def put(ref, at, value):
    last = at + value.shape[1]
    ref[:, at:last] = value.astype(ref.dtype)
    ref.flush(at, last)
    return last


def put_both(send, keep, at, value):
    put(send, at, value)
    return put(keep, at, value)


def put_cut(send, keep, at, value, order):
    ordered = mm(value, order[...])
    half = ordered.shape[1] // 2
    put(send, at, ordered[:, :half])
    return put(keep, at, ordered[:, half:])


def keys_of(causal, length, rows, counts, first=0):
    plots = rows // length
    if causal:
        return [(slice(0, rows), causal_bias(counts, plots, length))]
    return [
        (slice(p * length, (p + 1) * length), length_bias(counts[first + p], length, length)) for p in range(plots)
    ]


def self_fwd_kernel(causal, length, first, counts, state, gain, stacked, outer, part, saved):
    rows, width = part.shape[0], outer.shape[0]
    normed = norm(state[first * length : first * length + rows, :].astype(F32), gain[0:1, :])
    for which in range(3):
        put(saved, which * width, mm(normed, stacked[which]))
    for span, bias in keys_of(causal, length, rows, counts, first):
        for cols in pairs_of(width):
            mixed = slice(3 * width + cols.start, 3 * width + cols.stop)
            saved[span, mixed] = pair_fwd(
                saved[span, cols],
                saved[span, width + cols.start : width + cols.stop],
                saved[span, 2 * width + cols.start : 2 * width + cols.stop],
                bias,
            )
    part[...] = mm(saved[:, 3 * width :], outer[...])


def enc_mlp_fwd_kernel(first, state, own, other, gain, inner, outer, part, state_ref, pre):
    rows, width = part.shape[0], outer.shape[0]
    full = state[first * rows : (first + 1) * rows, :].astype(F32) + own[...] + other[...]
    state_ref[...] = full
    normed = norm(full, gain[1:2, :])
    step = 256
    total = None
    for at in range(0, width, step):
        cols = slice(at, at + step)
        gate = mm(normed, inner[0, :, cols])
        up = mm(normed, inner[1, :, cols])
        value, _ = gelu_parts(gate)
        pre[:, cols] = gate
        pre[:, width + at : width + at + step] = up
        add = mm((value * up).astype(BF), outer[cols, :])
        total = add if total is None else total + add
    part[...] = total


def cross_fwd_kernel(
    length, first, counts, enc_state, enc_own, enc_other, enc_gain, dec_state, dec_own, dec_other, dec_gain, stacked,
    outer, part, states, saved,
):
    rows, width = part.shape[0], outer.shape[0]
    span = slice(first * rows, (first + 1) * rows)
    dec_full = dec_state[span, :].astype(F32) + dec_own[span, :] + dec_other[span, :]
    states[length:, :] = dec_full
    normed = norm(dec_full, dec_gain[1:2, :])
    saved[length:, :width] = mm(normed, stacked[0]).astype(BF)
    enc_full = enc_state[...] + enc_own[...] + enc_other[...]
    states[:length, :] = enc_full
    memory = norm(enc_full, enc_gain[2:3, :])
    saved[:length, :width] = mm(memory, stacked[1]).astype(BF)
    saved[:length, width:] = mm(memory, stacked[2]).astype(BF)
    bias = length_bias(counts[first], rows, length)
    for cols in pairs_of(width):
        beside = slice(width + cols.start, width + cols.stop)
        saved[length:, beside] = pair_fwd(saved[length:, cols], saved[:length, cols], saved[:length, beside], bias)
    part[...] = mm(saved[length:, width:], outer[...])


def dec_mlp_kernel(
    state, own, other, gain, cotangent, inner, outer, order, order_outer, part, state_ref, send, keep
):
    full = state[...] + own[...] + other[...]
    state_ref[...] = full
    state_ref.flush()
    normed = norm(full, gain[2:3, :])
    low = cotangent[...]
    width, half = outer.shape[0], order.shape[0] // 2
    step = 256
    for col in range(0, width, step):
        cols = slice(col, col + step)
        gate = mm(normed, inner[0, :, cols])
        up = mm(normed, inner[1, :, cols])
        value, rise = gelu_parts(gate)
        grad_hidden = mm_nt(low, outer[cols, :])
        put_both(send, keep, half + col, (grad_hidden * up * rise).astype(BF))
        put_both(send, keep, half + width + col, (grad_hidden * value).astype(BF))
        put_both(send, keep, 2 * half + 2 * width + col, (value * up).astype(BF))
    part[...] = mm_nt(keep[:, half : half + width], inner[0]) + mm_nt(
        keep[:, half + width : half + 2 * width], inner[1]
    )
    part.flush()
    put_cut(send, keep, 0, normed, order)
    put_cut(send, keep, half + 2 * width, low, order_outer)


def tail_parts_kernel(enc_part, dec_part, keep, outer, part):
    enc_rows, dec_rows = enc_part.shape[0], dec_part.shape[0]
    part[:enc_rows, :] = enc_part[...]
    part[enc_rows : enc_rows + dec_rows, :] = dec_part[...]
    part[enc_rows + dec_rows :, :] = mm(keep[:, keep.shape[1] - outer.shape[0] :], outer[...])


def tail_kernel(own, other, enc_state, enc_gain, enc_grad, dec_state, dec_gain, dec_grad, state, enc_out, dec_out, out):
    enc_rows, dec_rows = enc_out.shape[0], dec_out.shape[0]
    span = slice(0, enc_rows)
    grad_in, _ = norm_back(own[span, :] + other[span, :], enc_state[...].astype(F32), enc_gain[0:1, :])
    enc_out[...] = (enc_grad[...] + grad_in).astype(BF)
    span = slice(enc_rows, enc_rows + dec_rows)
    grad_in, _ = norm_back(own[span, :] + other[span, :], dec_state[...].astype(F32), dec_gain[0:1, :])
    dec_out[...] = (dec_grad[...] + grad_in).astype(BF)
    span = slice(enc_rows + dec_rows, enc_rows + 2 * dec_rows)
    out[...] = (state[...] + own[span, :] + other[span, :]).astype(BF)


def query_part_kernel(keep, stacked, part):
    half = stacked.shape[1] // 2
    part[...] = mm_nt(keep[:, half : half + stacked.shape[2]], stacked[0])


def cross_back_kernel(
    length, counts, own, other, state, gain, grad, outer, query, kv, stacked, order, dec_state, enc_state, enc_gain,
    part, grad_ref, gain_ref, send, keep, key_grads,
):
    grad_in, normed = norm_back(own[...] + other[...], state[...], gain[2:3, :])
    gain_ref[...] = gain_part(own[...], normed)
    full = grad[...].astype(F32) + grad_in
    grad_ref[...] = full
    flush(gain_ref, grad_ref)
    low = full.astype(BF)
    width, half = outer.shape[0], order.shape[0] // 2
    grad_mixed = mm_nt(low, outer[...]).astype(BF)
    plots = kv.shape[0] // length
    rows = low.shape[0] // plots
    for plot in range(plots):
        bias = length_bias(counts[plot], rows, length)
        q_span = slice(plot * rows, (plot + 1) * rows)
        k_span = slice(plot * length, (plot + 1) * length)
        for cols in pairs_of(width):
            values = slice(width + cols.start, width + cols.stop)
            grad_query, grad_keys, grad_values = pair_back(
                query[q_span, cols], kv[k_span, cols], kv[k_span, values], grad_mixed[q_span, cols], bias
            )
            keep[q_span, half + cols.start : half + cols.stop] = grad_query
            send[q_span, half + cols.start : half + cols.stop] = grad_query.astype(F32)
            key_grads[k_span, cols] = grad_keys
            key_grads[k_span, values] = grad_values
    send.flush(half, half + width)
    keep.flush(half, half + width)
    part[...] = mm_nt(key_grads[:, :width], stacked[1]) + mm_nt(key_grads[:, width:], stacked[2])
    part.flush()
    put_cut(send, keep, 0, norm(dec_state[...], gain[1:2, :]), order)
    at = put_cut(send, keep, half + width, low, order)
    base = put_both(send, keep, at, query[:, width : 2 * width])
    ordered = mm(norm(enc_state[...], enc_gain[2:3, :]), order[...])
    for fold in range(kv.shape[0] // low.shape[0]):
        span = slice(fold * low.shape[0], (fold + 1) * low.shape[0])
        put(send, base, ordered[span, :half])
        put(keep, base, ordered[span, half:])
        base = put_both(send, keep, base + half, key_grads[span, :])


def self_back_kernel(
    causal, length, counts, own, other, state, gain, grad, outer, qkv, stacked, order, inputs,
    part, grad_ref, gain_ref, send, keep,
):
    grad_in, normed = norm_back(own[...] + other[...], state[...], gain[1:2, :])
    gain_ref[0:1, :] = gain_part(own[...], normed)
    full = grad[...] + grad_in
    grad_ref[...] = full
    flush(gain_ref, grad_ref)
    low = full.astype(BF)
    width, half = outer.shape[0], order.shape[0] // 2
    grad_mixed = mm_nt(low, outer[...]).astype(BF)
    for span, bias in keys_of(causal, length, low.shape[0], counts):
        for cols in pairs_of(width):
            grads = pair_back(
                qkv[span, cols],
                qkv[span, width + cols.start : width + cols.stop],
                qkv[span, 2 * width + cols.start : 2 * width + cols.stop],
                grad_mixed[span, cols],
                bias,
            )
            for which, piece in enumerate(grads):
                start = half + which * width + cols.start
                keep[span, start : start + PAIR] = piece
                send[span, start : start + PAIR] = piece.astype(F32)
    send.flush(half, half + 3 * width)
    keep.flush(half, half + 3 * width)
    total = mm_nt(keep[:, half : half + width], stacked[0])
    total += mm_nt(keep[:, half + width : half + 2 * width], stacked[1])
    total += mm_nt(keep[:, half + 2 * width : half + 3 * width], stacked[2])
    part[...] = total
    normed = scaled(inputs[...].astype(F32))
    gain_ref[1:2, :] = gain_part(total, normed)
    put_cut(send, keep, 0, (normed * gain[0:1, :]).astype(BF), order)
    at = put_cut(send, keep, half + 3 * width, low, order)
    put_both(send, keep, at, qkv[:, 3 * width : 4 * width])


def enc_mlp_back_kernel(
    own, other, state, gain, outer, pre, inner, order, order_outer, middle,
    part, grad_ref, gain_ref, send, keep,
):
    full, normed = norm_back(own[...] + other[...], state[...], gain[2:3, :])
    gain_ref[...] = gain_part(own[...], normed)
    grad_ref[...] = full
    flush(gain_ref, grad_ref)
    low = full.astype(BF)
    width, half = outer.shape[0], order.shape[0] // 2
    step = 256
    for col in range(0, width, step):
        cols = slice(col, col + step)
        value, rise = gelu_parts(pre[:, cols])
        up = pre[:, width + col : width + col + step]
        grad_hidden = mm_nt(low, outer[cols, :])
        put_both(send, keep, half + col, (grad_hidden * up * rise).astype(BF))
        put_both(send, keep, half + width + col, (grad_hidden * value).astype(BF))
        put_both(send, keep, 2 * half + 2 * width + col, (value * up).astype(BF))
    part[...] = mm_nt(keep[:, half : half + width], inner[0]) + mm_nt(
        keep[:, half + width : half + 2 * width], inner[1]
    )
    part.flush()
    put_cut(send, keep, 0, norm(middle[...], gain[1:2, :]), order)
    put_cut(send, keep, half + 2 * width, low, order_outer)


def gains_kernel(enc_attn, enc_mlp, dec_self, dec_cross, order, send, keep):
    rows = [enc_attn[1:2, :], enc_attn[0:1, :], enc_mlp[...], dec_self[1:2, :], dec_self[0:1, :], dec_cross[...]]
    rest = jnp.concatenate(rows + [jnp.zeros((128 - len(rows), order.shape[0]), F32)], 0)
    total = None
    for _ in range(3):
        low = rest.astype(BF)
        rest = rest - low.astype(F32)
        moved = lax.dot_general(order[...], low, (((0,), (1,)), ((), ())), preferred_element_type=F32)
        total = moved if total is None else total + moved
    half = total.shape[0] // 2
    send[...] = total[:half]
    keep[...] = total[half:]


def gains_out_kernel(own, other, enc_out, dec_out):
    total = own[...] + other[...]
    rows, columns = total.shape
    total = jnp.concatenate([total, jnp.zeros((columns - rows, columns), F32)], 0).T
    enc_out[...] = total[0:3, :rows]
    dec_out[...] = total[3:6, :rows]


def gains_weight_kernel(segments, keep, recv, gains, other_gains, send_out, keep_out):
    weight_kernel(segments, keep, recv, send_out, keep_out)
    total = gains[...] + other_gains[...]
    half, first = send_out.shape[0], send_out.shape[1] - total.shape[1]
    send_out[:, first:] = total[:half]
    keep_out[:, first:] = total[half:]


def weight_kernel(segments, keep, recv, *outs):
    last_of = {(group, target): at for at, (_, _, _, _, group, target) in enumerate(segments)}
    started = set()
    for number, (cut, cut_width, first, columns, group, target) in enumerate(segments):
        send_out, keep_out = outs[2 * group], outs[2 * group + 1]
        left = jnp.concatenate([keep[:, cut : cut + cut_width], recv[:, cut : cut + cut_width].astype(BF)], 0)
        half = cut_width // 2
        step = 512 if columns % 512 == 0 else 384
        for at in range(0, columns, step):
            cols = slice(first + at, first + at + step)
            right = jnp.concatenate([keep[:, cols], recv[:, cols].astype(BF)], 0)
            total = mm_tn(left, right)
            into = slice(target + at, target + at + step)
            if (group, target) in started:
                total += jnp.concatenate([send_out[:, into], keep_out[:, into]], 0)
            send_out[:, into] = total[:half]
            keep_out[:, into] = total[half:]
            if last_of[group, target] == number:
                send_out.flush(into.start, into.stop)
                keep_out.flush(into.start, into.stop)
        started.add((group, target))


def halve_kernel(kept, recv, send_out, keep_out):
    rows = send_out.shape[0]
    send_out[...] = kept[:rows] + recv[:rows]
    send_out.flush()
    keep_out[...] = kept[rows:] + recv[rows:]


SMEM = pl.BlockSpec(memory_space=pltpu.SMEM)
VMEM = pl.BlockSpec(memory_space=pltpu.VMEM)
ANY = pl.BlockSpec(memory_space=pl.ANY)


COST = {
    "enc_attn_fwd": 2.3, "dec_self_fwd": 2.5, "enc_mlp_fwd": 1.7, "cross_fwd": 4.2, "dec_mlp": 2.7,
    "cross_back": 0.1, "dec_self_back": 0.3, "enc_attn_back": 0.1, "enc_mlp_back": 8, "finish_a": 20,
    "finish_c": 3, "finish_f": 20, "finish_fo": 20, "finish_m": 0.1, "finish_mo": 3,
    "finish_s": 0.3, "gains": 20, "gains_out": 8, "halve_a": 3, "halve_c": 3,
    "halve_f": 0.3, "halve_fo": 0.3, "halve_m": 1, "halve_mo": 0.3, "halve_s": 0.3,
    "query_part": 8, "tail": 3, "tail_parts": 0.1, "weights_a": 8, "weights_c": 3,
    "weights_f": 3, "weights_m": 0.3, "weights_s": 0.1,
}
VMEM_LIMIT = 8

LINE = (
    "pause", "enc_attn_0", "enc_attn_1", "dec_self", "pause", "enc_mlp_0", "enc_mlp_1", "pause",
    "cross_0", "cross_1", "pause", "dec_mlp", "tick", "w_m", "cross_back", "tick",
    "tick", "tick", "tick", "tick", "tick", "tick", "tick", "tick",
    "tick", "tick", "tick", "tick", "tick", "tick", "tick", "tick",
    "tick", "tick", "w_c", "tick", "tick", "tick", "enc_mlp_back", "tick",
    "tick", "tick", "tick", "tick", "tick", "tick", "tick", "tick",
    "tick", "tick", "tick", "tick", "tick", "query_part", "tick", "tick",
    "w_f", "tick", "tick", "tick", "h_c", "h_m", "enc_attn_back", "h_fo",
    "tick", "h_f", "tick", "dec_self_back", "h_c", "tick", "gains", "w_a",
    "w_s", "h_f", "h_c", "h_m", "tick", "tick", "tail_parts", "h_f",
    "h_s", "h_a", "h_s", "h_m", "tail", "e_c", "h_a", "h_s",
    "e_m", "h_fo", "h_a", "e_s", "h_fo", "e_f", "gains_out", "e_a",
    "e_fo",
)
HALVINGS = {"a": "xpme", "c": "xpme", "f": "xpme", "m": "pxme", "s": "pxme", "fo": "pxme"}
PARTS = {"a": 1, "c": 1, "f": 1, "m": 1, "s": 1}
TICK = 2
GAINS_WITH = "s"


class Stored:
    def __init__(self, ref):
        self.ref = ref
        self.shape, self.dtype = ref.shape, ref.dtype

    def __getitem__(self, at):
        return self.ref[at]

    def __setitem__(self, at, value):
        self.ref[at] = value

    def flush(self, first=0, last=None):
        pass


class Columns:
    def __init__(self, refs):
        self.refs = refs
        self.shape = (refs[0].shape[0], sum(ref.shape[1] for ref in refs))
        self.dtype = refs[0].dtype

    def __getitem__(self, at):
        rows, cols = at
        first, last = cols.start or 0, self.shape[1] if cols.stop is None else cols.stop
        pieces, start = [], 0
        for ref in self.refs:
            low, high = max(first - start, 0), min(last - start, ref.shape[1])
            if low < high:
                pieces.append(ref[rows, low:high])
            start += ref.shape[1]
        return pieces[0] if len(pieces) == 1 else jnp.concatenate(pieces, 1)

    def __setitem__(self, at, value):
        rows, cols = at
        first, last = cols.start or 0, self.shape[1] if cols.stop is None else cols.stop
        start = 0
        for ref in self.refs:
            low, high = max(first - start, 0), min(last - start, ref.shape[1])
            if low < high:
                ref[rows, low:high] = value[:, low + start - first : high + start - first]
            start += ref.shape[1]

    def flush(self, first=0, last=None):
        pass


class Stack:
    def __init__(self, *parts):
        self.parts = parts


class Rows:
    def __init__(self, refs, spans):
        self.refs = [ref.at[first:last] if (first, last) != (0, ref.shape[0]) else ref
                     for ref, (first, last) in zip(refs, spans)]
        self.heights = [last - first for first, last in spans]
        self.shape = (sum(self.heights),) + tuple(refs[0].shape[1:])
        self.dtype = refs[0].dtype

    def __getitem__(self, at):
        rows, cols = (slice(None), slice(None)) if at is Ellipsis else at
        first, last, _ = rows.indices(self.shape[0])
        pieces, start = [], 0
        for ref, height in zip(self.refs, self.heights):
            low, high = max(first - start, 0), min(last - start, height)
            if low < high:
                pieces.append(ref[low:high, cols])
            start += height
        return pieces[0] if len(pieces) == 1 else jnp.concatenate(pieces, 0)


def flush(*refs):
    for ref in refs:
        ref.flush()


class Line:
    def __init__(self):
        self.last = None

    def call(self, kernel, outs, args, name, scratch=(), cost=None):
        spans = [[part[1:] for part in a.parts] if isinstance(a, Stack) else None for a in args]
        args = [[part[0] for part in a.parts] if isinstance(a, Stack) else a for a in args]
        flat_args, args_tree = jax.tree.flatten(list(args))
        widths = [out if isinstance(out, list) else [out] for out in outs]
        shapes = [jax.ShapeDtypeStruct(*out) for group in widths for out in group]
        in_specs = [VMEM if a.ndim > 1 else SMEM for a in flat_args]
        count, made = len(flat_args), len(shapes)
        operands = list(flat_args)
        if self.last is not None:
            operands.append(self.last)
            in_specs.append(ANY)
        total = len(operands)

        def run(*refs):
            ins = jax.tree.unflatten(args_tree, refs[:count])
            ins = [Rows(i, span) if span else Columns(i) if isinstance(i, list) else i for i, span in zip(ins, spans)]
            left = list(refs[total : total + made])
            results = []
            for group, out in zip(widths, outs):
                taken, left = [Stored(ref) for ref in left[: len(group)]], left[len(group) :]
                results.append(Columns(taken) if isinstance(out, list) else taken[0])
            kernel(*ins, *results, *refs[total + made :])

        cost = COST.get(name, 0.3) if cost is None else cost
        flat = pl.pallas_call(
            run,
            out_shape=shapes,
            in_specs=in_specs,
            out_specs=[VMEM] * made,
            scratch_shapes=list(scratch),
            compiler_params=pltpu.CompilerParams(vmem_limit_bytes=VMEM_LIMIT * MIB),
            cost_estimate=pl.CostEstimate(
                flops=int(cost * 1.15e9), bytes_accessed=int(cost * 3.69e6), transcendentals=0
            ),
            name=name,
        )(*operands)
        self.last = min(flat, key=lambda r: r.size)
        results, left = [], list(flat)
        for group, out in zip(widths, outs):
            results.append(left[: len(group)] if isinstance(out, list) else left[0])
            left = left[len(group) :]
        return results


def join_kernel(kept, recv, out):
    out[...] = kept[...] + recv[...]


def middle_kernel(kept, recv, send_out, keep_out):
    rows = send_out.shape[0]
    me = lax.axis_index("dp")
    inner = ((me >> 2) ^ (me >> 3)) & 1
    send_out[...] = jnp.where(inner == 1, recv[rows:], kept[:rows])
    keep_out[...] = jnp.where(inner == 1, recv[:rows], kept[rows:])


def finish_kernel(pieces, kept, recv, *outs):
    for out, (first, count) in zip(outs, pieces):
        width = out.shape[-1]
        for i in range(count):
            cols = slice(first + i * width, first + (i + 1) * width)
            total = kept[:, cols] + recv[:, cols]
            if count > 1:
                out[i] = total
            else:
                out[...] = total


def tick_kernel(source, target):
    target[...] = source[0:1, 0:128]


def pair_other(part, name):
    with jax.named_scope("pair_" + name):
        return lax.ppermute(part, "mp", [(0, 1), (1, 0)])


def swap(value, step, name):
    shards = lax.axis_size("dp")
    bit = {"x": 1, "p": 2, "e": 2}.get(step, step)
    if step == "m":
        pairs = [(i, i ^ 12) for i in range(shards) if (i >> 2 ^ i >> 3) & 1]
    else:
        pairs = [(i, i ^ (1 << bit)) for i in range(shards)]
    with jax.named_scope("swap_%s_%s" % (name, step)):
        return lax.ppermute(value, "dp", pairs)


def feature_order(features, steps):
    shards = lax.axis_size("dp")
    me = lax.axis_index("dp")
    block = features // shards
    column = jnp.arange(features, dtype=jnp.int32)
    place = column // block
    owner = jnp.zeros_like(column)
    other = {step: 1 - ((place >> (len(steps) - 1 - at)) & 1) for at, step in enumerate(steps)}
    near = (me >> 2) & 1
    for step in steps:
        if step == "p":
            owner = owner | ((near ^ other["p"]) << 3)
        elif step == "e":
            owner = owner | ((near ^ other["e"] ^ other["p"]) << 2)
        else:
            bit = 1 if step == "x" else step
            owner = owner | ((((me >> bit) & 1) ^ other[step]) << bit)
    source = owner * block + column % block
    return (jnp.arange(features, dtype=jnp.int32)[:, None] == source[None, :]).astype(BF)


class Halving:
    def __init__(self, sent, kept, steps, name):
        self.steps, self.name, self.at = steps, name, 0
        self.kept = kept
        self.flying = swap(sent, steps[0], name)

    def step(self, line):
        came, self.at = self.steps[self.at], self.at + 1
        rows, columns = self.kept.shape
        args, name = [self.kept, self.flying], "halve_" + self.name
        if self.steps[self.at] == "m":
            (self.kept,) = line.call(join_kernel, [((rows, columns), F32)], args, name)
            sent = self.kept
        else:
            shape = ((rows // 2, columns), F32)
            sent, self.kept = line.call(middle_kernel if came == "m" else halve_kernel, [shape, shape], args, name)
        self.flying = swap(sent, self.steps[self.at], self.name)

    def finish(self, line, *pieces):
        for bit in range(4, lax.axis_size("dp").bit_length() - 1):
            rows = self.kept.shape[0] // 2
            total = self.kept + self.flying
            self.kept, self.flying = total[rows:], swap(total[:rows], bit, self.name)
        rows = self.kept.shape[0]
        outs = [(((count, rows, width) if count > 1 else (rows, width)), F32) for _, count, width in pieces]
        return line.call(
            functools.partial(finish_kernel, [(first, count) for first, count, _ in pieces]),
            outs, [self.kept, self.flying], "finish_" + self.name,
        )


def body(
    enc_in, dec_in, cotangent, patch_counts, table_lengths, enc_qkv, enc_attn_out, enc_mlp_in, enc_mlp_out, enc_gains,
    dec_self_qkv, dec_self_out, dec_cross_qkv, dec_cross_out, dec_mlp_in, dec_mlp_out, dec_gains,
):
    plots, enc_len, features = enc_in.shape
    dec_len = dec_in.shape[1]
    enc_rows, dec_rows = plots * enc_len, plots * dec_len
    heads = enc_attn_out.shape[0]
    units = enc_mlp_out.shape[0]
    half = features // 2
    bits = lax.axis_size("dp").bit_length() - 1
    orders = {}

    def order_by(steps):
        cuts = (0,) + tuple(step for step in steps if step != "m") + tuple(range(4, bits))
        if cuts not in orders:
            orders[cuts] = feature_order(features, cuts)
        return orders[cuts]

    order_of = {name: order_by(steps) for name, steps in HALVINGS.items()}
    x0 = enc_in.reshape(enc_rows, features)
    y0 = dec_in.reshape(dec_rows, features)
    top = cotangent.reshape(dec_rows, features)
    enc_wide, dec_wide = ((enc_rows, features), F32), ((dec_rows, features), F32)
    enc_low, dec_low = ((enc_rows, features), BF), ((dec_rows, features), BF)
    gain_row, gain_rows = ((1, features), F32), ((2, features), F32)
    quarter = half // 2
    line = Line()

    def tick(cost=TICK):
        line.call(tick_kernel, [((1, 128), F32)], [enc_gains], "tick", cost=cost)

    def parts_of(name, rows, width):
        count, tiles = PARTS[name], width // 128
        edges = [128 * (tiles * i // count) for i in range(count + 1)]
        return [((rows, high - low), F32) for low, high in zip(edges, edges[1:])]

    def swap_cores(name, parts):
        return [swap(part, 0, name) for part in parts]

    def group(columns):
        return [((quarter, columns), F32)] * 2

    def mlp_of(name):
        apart = name + "o" in HALVINGS
        target = (1, 0) if apart else (0, 2 * units)
        segments = (
            (0, half, half, 2 * units, 0, 0),
            (half + 2 * units, half, 2 * half + 2 * units, units) + target,
        )
        return segments, group(2 * units) + group(units) if apart else group(3 * units)

    attn_segments = (
        (0, half, half, 3 * heads, 0, 0),
        (half + 3 * heads, half, 2 * half + 3 * heads, heads, 0, 3 * heads),
    )
    base, fold_width = 2 * half + 2 * heads, half + 2 * heads
    folds = enc_rows // dec_rows
    cross_segments = (
        (0, half, half, heads, 0, 0),
        (half + heads, half, 2 * half + heads, heads, 0, heads),
    ) + tuple(
        (base + f * fold_width, half, base + f * fold_width + half, 2 * heads, 0, 2 * heads) for f in range(folds)
    )
    attn_group = group(4 * heads)
    mlp_wide = 2 * half + 3 * units
    attn_wide = 2 * half + 4 * heads
    cross_wide = base + folds * fold_width
    v, sums, grad_of = {}, {}, {}

    def pause():
        tick(6.0)

    def enc_attn(p):
        v["part_e1", p], v["enc_saved", p] = line.call(
            functools.partial(self_fwd_kernel, False, enc_len, p),
            [((enc_len, features), F32), ((enc_len, 4 * heads), BF)],
            [patch_counts, x0, enc_gains, enc_qkv, enc_attn_out], "enc_attn_fwd",
        )
        v["other_e1", p] = pair_other(v["part_e1", p], "e1")

    def dec_self():
        v["part_d1"], v["dec_saved"] = line.call(
            functools.partial(self_fwd_kernel, True, dec_len, 0),
            [dec_wide, ((dec_rows, 4 * heads), BF)],
            [table_lengths, y0, dec_gains, dec_self_qkv, dec_self_out], "dec_self_fwd",
        )
        v["other_d1"] = pair_other(v["part_d1"], "d1")

    def enc_mlp(p):
        v["part_e2", p], v["x1", p], v["pre", p] = line.call(
            functools.partial(enc_mlp_fwd_kernel, p),
            [((enc_len, features), F32), ((enc_len, features), F32), ((enc_len, 2 * units), F32)],
            [x0, v["part_e1", p], v["other_e1", p], enc_gains, enc_mlp_in, enc_mlp_out], "enc_mlp_fwd",
        )
        v["other_e2", p] = pair_other(v["part_e2", p], "e2")

    def cross(p):
        v["part_d2", p], v["states", p], v["saved", p] = line.call(
            functools.partial(cross_fwd_kernel, enc_len, p),
            [((dec_len, features), F32), ((enc_len + dec_len, features), F32), ((enc_len + dec_len, 2 * heads), BF)],
            [patch_counts, v["x1", p], v["part_e2", p], v["other_e2", p], enc_gains, y0, v["part_d1"], v["other_d1"],
             dec_gains, dec_cross_qkv, dec_cross_out],
            "cross_fwd",
        )
        v["other_d2", p] = pair_other(v["part_d2", p], "d2")

    def stack(name, first, last):
        return Stack(*[(v[name, p], first, last) for p in range(plots)])

    def enc_part(name):
        return stack(name, 0, enc_len)

    def dec_part(name):
        return stack(name, enc_len, enc_len + dec_len)

    def dec_mlp():
        v["part_g3"], v["y2"], send, v["keep_m"] = line.call(
            dec_mlp_kernel,
            [dec_wide, dec_wide, parts_of("m", dec_rows, mlp_wide), ((dec_rows, mlp_wide), BF)],
            [dec_part("states"), stack("part_d2", 0, dec_len), stack("other_d2", 0, dec_len), dec_gains, top,
             dec_mlp_in, dec_mlp_out, order_of["m"], order_of.get("mo", order_of["m"])],
            "dec_mlp",
        )
        v["other_g3"] = pair_other(v["part_g3"], "g3")
        v["recv_m"] = swap_cores("m", send)

    def start_sums(name, products):
        for group_name, pair in zip((name, name + "o"), zip(products[::2], products[1::2])):
            sums[group_name] = Halving(pair[0], pair[1], HALVINGS[group_name], group_name)

    def mlp_weights(name, keep, recv):
        segments, groups = mlp_of(name)
        start_sums(
            name, line.call(functools.partial(weight_kernel, segments), groups, [keep, recv], "weights_" + name)
        )

    def dec_mlp_weights():
        mlp_weights("m", v["keep_m"], v["recv_m"])

    def cross_back():
        v["part_m"], v["g2"], v["gain_dec_cross"], send, v["keep_c"] = line.call(
            functools.partial(cross_back_kernel, enc_len),
            [enc_wide, dec_wide, gain_row, parts_of("c", dec_rows, cross_wide), ((dec_rows, cross_wide), BF)],
            [patch_counts, v["part_g3"], v["other_g3"], v["y2"], dec_gains, top, dec_cross_out, dec_part("saved"),
             enc_part("saved"), dec_cross_qkv, order_of["c"], dec_part("states"), enc_part("states"), enc_gains],
            "cross_back", scratch=[pltpu.VMEM((enc_rows, 2 * heads), BF)],
        )
        v["other_m"] = pair_other(v["part_m"], "m")
        v["recv_c"] = swap_cores("c", send)

    def cross_weights():
        start_sums("c", line.call(
            functools.partial(weight_kernel, cross_segments), attn_group, [v["keep_c"], v["recv_c"]], "weights_c"
        ))

    def enc_mlp_back():
        v["part_g1"], v["back2"], v["gain_enc_mlp"], send, v["keep_f"] = line.call(
            enc_mlp_back_kernel,
            [enc_wide, enc_wide, gain_row, parts_of("f", enc_rows, mlp_wide), ((enc_rows, mlp_wide), BF)],
            [v["part_m"], v["other_m"], enc_part("states"), enc_gains, enc_mlp_out, enc_part("pre"), enc_mlp_in,
             order_of["f"], order_of.get("fo", order_of["f"]), enc_part("x1")],
            "enc_mlp_back",
        )
        v["other_g1"] = pair_other(v["part_g1"], "g1")
        v["recv_f"] = swap_cores("f", send)

    def enc_mlp_weights():
        mlp_weights("f", v["keep_f"], v["recv_f"])

    def enc_attn_back():
        v["part_ge"], v["back1"], v["gain_enc_attn"], send, v["keep_a"] = line.call(
            functools.partial(self_back_kernel, False, enc_len),
            [enc_wide, enc_wide, gain_rows, parts_of("a", enc_rows, attn_wide), ((enc_rows, attn_wide), BF)],
            [patch_counts, v["part_g1"], v["other_g1"], enc_part("x1"), enc_gains, v["back2"], enc_attn_out,
             enc_part("enc_saved"), enc_qkv, order_of["a"], x0],
            "enc_attn_back",
        )
        v["recv_a"] = swap_cores("a", send)

    def query_part():
        (v["part_q"],) = line.call(query_part_kernel, [dec_wide], [v["keep_c"], dec_cross_qkv], "query_part")
        v["other_q"] = pair_other(v["part_q"], "q")

    def dec_self_back():
        v["part_g0"], v["g1"], v["gain_dec_self"], send, v["keep_s"] = line.call(
            functools.partial(self_back_kernel, True, dec_len),
            [dec_wide, dec_wide, gain_rows, parts_of("s", dec_rows, attn_wide), ((dec_rows, attn_wide), BF)],
            [table_lengths, v["part_q"], v["other_q"], dec_part("states"), dec_gains, v["g2"], dec_self_out,
             v["dec_saved"], dec_self_qkv, order_of["s"], y0],
            "dec_self_back",
        )
        v["recv_s"] = swap_cores("s", send)

    def tail_parts():
        (v["part_tail"],) = line.call(
            tail_parts_kernel, [((enc_rows + 2 * dec_rows, features), F32)],
            [v["part_ge"], v["part_g0"], v["keep_m"], dec_mlp_out], "tail_parts",
        )
        v["other_tail"] = pair_other(v["part_tail"], "tail")

    def tail():
        v["enc_out"], v["dec_out_grad"], v["dec_out"] = line.call(
            tail_kernel, [enc_low, dec_low, dec_low],
            [v["part_tail"], v["other_tail"], x0, enc_gains, v["back1"], y0, dec_gains, v["g1"], v["y2"]], "tail",
        )

    def gains():
        send, v["keep_g"] = line.call(
            gains_kernel, [((half, 128), F32), ((half, 128), F32)],
            [v["gain_enc_attn"], v["gain_enc_mlp"], v["gain_dec_self"], v["gain_dec_cross"], order_of[GAINS_WITH]],
            "gains",
        )
        v["recv_g"] = swap(send, 0, "g")

    def gains_sum():
        v["other_gains"] = pair_other(grad_of[GAINS_WITH][2], "gains")

    def gains_out():
        own = grad_of[GAINS_WITH][2]
        shape = ((3, own.shape[0]), F32)
        v["gains_out"] = line.call(gains_out_kernel, [shape, shape], [own, v["other_gains"]], "gains_out")

    def attn_weights(name):
        if name == GAINS_WITH:
            products = line.call(
                functools.partial(gains_weight_kernel, attn_segments), group(4 * heads + 128),
                [v["keep_" + name], v["recv_" + name], v["keep_g"], v["recv_g"]], "weights_" + name,
            )
        else:
            products = line.call(
                functools.partial(weight_kernel, attn_segments), attn_group,
                [v["keep_" + name], v["recv_" + name]], "weights_" + name,
            )
        start_sums(name, products)

    attn_pieces = ((0, 3, heads), (3 * heads, 1, heads))
    ends = {
        "m": ((0, 2, units),), "f": ((0, 2, units),), "mo": ((0, 1, units),), "fo": ((0, 1, units),),
        "c": ((0, 1, heads), (heads, 1, heads), (2 * heads, 2, heads)), "a": attn_pieces, "s": attn_pieces,
    }
    for name in ("m", "f"):
        if name + "o" not in HALVINGS:
            ends[name] += ((2 * units, 1, units),)
    ends[GAINS_WITH] += ((4 * heads, 1, 128),)
    stages = {
        "tick": tick, "pause": pause, "dec_self": dec_self, "dec_mlp": dec_mlp, "w_m": dec_mlp_weights,
        "cross_back": cross_back, "w_c": cross_weights, "enc_mlp_back": enc_mlp_back,
        "w_f": enc_mlp_weights, "enc_attn_back": enc_attn_back, "query_part": query_part, "gains": gains,
        "tail_parts": tail_parts, "tail": tail, "gains_out": gains_out,
        "w_a": functools.partial(attn_weights, "a"), "dec_self_back": dec_self_back,
        "w_s": functools.partial(attn_weights, "s"),
    }
    for name, stage in (("enc_attn", enc_attn), ("enc_mlp", enc_mlp), ("cross", cross)):
        for p in range(plots):
            stages["%s_%d" % (name, p)] = functools.partial(stage, p)
    for stage in LINE:
        kind, _, name = stage.partition("_")
        if stage in stages:
            stages[stage]()
        elif kind == "h":
            sums[name].step(line)
        else:
            grad_of[name] = sums[name].finish(line, *ends[name])
            if name == GAINS_WITH:
                gains_sum()
    mlp_grads = {
        name: grad_of[name] if name + "o" not in HALVINGS else grad_of[name] + grad_of[name + "o"] for name in ("m", "f")
    }
    grad_c = jnp.concatenate([grad_of["c"][0][None], grad_of["c"][2]], 0)
    grads = (
        grad_of["a"][0], grad_of["a"][1].T, mlp_grads["f"][0], mlp_grads["f"][1].T, v["gains_out"][0],
        grad_of["s"][0], grad_of["s"][1].T, grad_c, grad_of["c"][1].T, mlp_grads["m"][0], mlp_grads["m"][1].T,
        v["gains_out"][1],
    )
    return (
        v["dec_out"].reshape(cotangent.shape),
        v["enc_out"].reshape(enc_in.shape),
        v["dec_out_grad"].reshape(dec_in.shape),
    ) + grads


def solution(mesh):
    rows = P("dp", None, None)
    inner, outer = P(None, None, "mp"), P("mp", None)
    enc = (inner, outer, inner, outer, P())
    dec = (inner, outer, inner, outer, inner, outer, P())
    inner_grad, outer_grad, gain_grad = P(None, "dp", "mp"), P("mp", "dp"), P(None, "dp")
    return jax.shard_map(
        body,
        mesh=mesh,
        in_specs=(rows, rows, rows, P("dp"), P("dp")) + enc + dec,
        out_specs=(rows, rows, rows)
        + (inner_grad, outer_grad) * 2 + (gain_grad,)
        + (inner_grad, outer_grad) * 3 + (gain_grad,),
        check_vma=False,
    )
```

```python
import functools

import jax
import jax.numpy as jnp
from jax import lax
from jax.experimental import pallas as pl
from jax.experimental.pallas import tpu as pltpu
from jax.sharding import PartitionSpec as P

HEAD_DIM = 64
PAIR = 2 * HEAD_DIM
EPSILON = 1e-06
NEG_LARGE = -1e30
SCALE = HEAD_DIM ** (-0.5)
BF = jnp.bfloat16
F32 = jnp.float32
MIB = 1024 * 1024


def mm(left, right):
    return jnp.dot(left, right, preferred_element_type=F32)


def mm_nt(left, right):
    return lax.dot_general(left, right, (((1,), (1,)), ((), ())), preferred_element_type=F32)


def mm_tn(left, right):
    return lax.dot_general(left, right, (((0,), (0,)), ((), ())), preferred_element_type=F32)


def scaled(hidden):
    return hidden * lax.rsqrt(jnp.mean(hidden * hidden, -1, keepdims=True) + EPSILON)


def norm(hidden, gain):
    return (scaled(hidden) * gain).astype(BF)


def norm_back(grad, hidden, gain):
    scaling = lax.rsqrt(jnp.mean(hidden * hidden, -1, keepdims=True) + EPSILON)
    normed = hidden * scaling
    grad_hat = grad * gain
    return scaling * (grad_hat - normed * jnp.mean(grad_hat * normed, -1, keepdims=True)), normed


def gain_part(part, normed):
    return jnp.sum(part * normed, 0, keepdims=True)


def gelu_parts(gate):
    slope = 0.7978845608028654
    square = gate * gate
    bent = jnp.tanh(slope * gate * (1.0 + 0.044715 * square))
    half = 0.5 * (1.0 + bent)
    value = gate * half
    rise = half + 0.5 * gate * (1.0 - bent * bent) * slope * (1.0 + 0.134145 * square)
    return value, rise


def stack_heads(pair):
    lane = lax.broadcasted_iota(jnp.int32, pair.shape, 1)
    zero = jnp.zeros_like(pair)
    return jnp.concatenate(
        [jnp.where(lane < HEAD_DIM, pair, zero), jnp.where(lane < HEAD_DIM, zero, pair)], 0
    )


def merge_heads(stacked):
    rows = stacked.shape[0] // 2
    lane = lax.broadcasted_iota(jnp.int32, (rows, PAIR), 1)
    return jnp.where(lane < HEAD_DIM, stacked[:rows], stacked[rows:])


def soft_of(stacked_query, keys, bias):
    scores = mm_nt(stacked_query, keys) * SCALE + bias
    expon = jnp.exp(scores - jnp.max(scores, -1, keepdims=True))
    return expon / jnp.sum(expon, -1, keepdims=True)


def pair_fwd(query, keys, values, bias):
    soft = soft_of(stack_heads(query), keys, bias)
    return merge_heads(mm(soft.astype(BF), values)).astype(BF)


def pair_back(query, keys, values, grad_out, bias):
    queries = stack_heads(query)
    soft = soft_of(queries, keys, bias)
    grads = stack_heads(grad_out)
    grad_values = mm_tn(soft.astype(BF), grads)
    grad_soft = mm_nt(grads, values)
    grad_scores = (
        soft * (grad_soft - jnp.sum(soft * grad_soft, -1, keepdims=True))
    ).astype(BF)
    grad_query = merge_heads(mm(grad_scores, keys)) * SCALE
    grad_keys = mm_tn(grad_scores, queries) * SCALE
    return grad_query.astype(BF), grad_keys.astype(BF), grad_values.astype(BF)


def length_bias(count, rows, length):
    col = lax.broadcasted_iota(jnp.int32, (2 * rows, length), 1)
    return jnp.where(col < count, 0.0, NEG_LARGE).astype(F32)


def causal_bias(counts, plots, length):
    shape = (plots * length, plots * length)
    row = lax.broadcasted_iota(jnp.int32, shape, 0)
    col = lax.broadcasted_iota(jnp.int32, shape, 1)
    bias = jnp.full(shape, NEG_LARGE, F32)
    for plot in range(plots):
        low = plot * length
        inside = (row >= low) & (row < low + length) & (col >= low)
        inside = inside & (col <= row) & (col < low + counts[plot])
        bias = jnp.where(inside, 0.0, bias)
    return jnp.concatenate([bias, bias], 0)


def pairs_of(width):
    return [slice(at, at + PAIR) for at in range(0, width, PAIR)]


def put(ref, at, value):
    last = at + value.shape[1]
    ref[:, at:last] = value.astype(ref.dtype)
    ref.flush(at, last)
    return last


def put_both(send, keep, at, value):
    put(send, at, value)
    return put(keep, at, value)


def put_cut(send, keep, at, value, order):
    ordered = mm(value, order[...])
    half = ordered.shape[1] // 2
    put(send, at, ordered[:, :half])
    return put(keep, at, ordered[:, half:])


def keys_of(causal, length, rows, counts, first=0):
    plots = rows // length
    if causal:
        return [(slice(0, rows), causal_bias(counts, plots, length))]
    return [
        (slice(p * length, (p + 1) * length), length_bias(counts[first + p], length, length)) for p in range(plots)
    ]


def self_fwd_kernel(causal, length, first, counts, state, gain, stacked, outer, part, saved):
    rows, width = part.shape[0], outer.shape[0]
    normed = norm(state[first * length : first * length + rows, :].astype(F32), gain[0:1, :])
    for which in range(3):
        put(saved, which * width, mm(normed, stacked[which]))
    for span, bias in keys_of(causal, length, rows, counts, first):
        for cols in pairs_of(width):
            mixed = slice(3 * width + cols.start, 3 * width + cols.stop)
            saved[span, mixed] = pair_fwd(
                saved[span, cols],
                saved[span, width + cols.start : width + cols.stop],
                saved[span, 2 * width + cols.start : 2 * width + cols.stop],
                bias,
            )
    part[...] = mm(saved[:, 3 * width :], outer[...])


def enc_mlp_fwd_kernel(first, state, own, other, gain, inner, outer, part, state_ref, pre):
    rows, width = part.shape[0], outer.shape[0]
    full = state[first * rows : (first + 1) * rows, :].astype(F32) + own[...] + other[...]
    state_ref[...] = full
    normed = norm(full, gain[1:2, :])
    step = 256
    total = None
    for at in range(0, width, step):
        cols = slice(at, at + step)
        gate = mm(normed, inner[0, :, cols])
        up = mm(normed, inner[1, :, cols])
        value, _ = gelu_parts(gate)
        pre[:, cols] = gate
        pre[:, width + at : width + at + step] = up
        add = mm((value * up).astype(BF), outer[cols, :])
        total = add if total is None else total + add
    part[...] = total


def cross_fwd_kernel(
    length, first, counts, enc_state, enc_own, enc_other, enc_gain, dec_state, dec_own, dec_other, dec_gain, stacked,
    outer, part, states, saved,
):
    rows, width = part.shape[0], outer.shape[0]
    span = slice(first * rows, (first + 1) * rows)
    dec_full = dec_state[span, :].astype(F32) + dec_own[span, :] + dec_other[span, :]
    states[length:, :] = dec_full
    normed = norm(dec_full, dec_gain[1:2, :])
    saved[length:, :width] = mm(normed, stacked[0]).astype(BF)
    enc_full = enc_state[...] + enc_own[...] + enc_other[...]
    states[:length, :] = enc_full
    memory = norm(enc_full, enc_gain[2:3, :])
    saved[:length, :width] = mm(memory, stacked[1]).astype(BF)
    saved[:length, width:] = mm(memory, stacked[2]).astype(BF)
    bias = length_bias(counts[first], rows, length)
    for cols in pairs_of(width):
        beside = slice(width + cols.start, width + cols.stop)
        saved[length:, beside] = pair_fwd(saved[length:, cols], saved[:length, cols], saved[:length, beside], bias)
    part[...] = mm(saved[length:, width:], outer[...])


def dec_mlp_kernel(
    state, own, other, gain, cotangent, inner, outer, order, order_outer, part, state_ref, send, keep
):
    full = state[...] + own[...] + other[...]
    state_ref[...] = full
    state_ref.flush()
    normed = norm(full, gain[2:3, :])
    low = cotangent[...]
    width, half = outer.shape[0], order.shape[0] // 2
    step = 256
    for col in range(0, width, step):
        cols = slice(col, col + step)
        gate = mm(normed, inner[0, :, cols])
        up = mm(normed, inner[1, :, cols])
        value, rise = gelu_parts(gate)
        grad_hidden = mm_nt(low, outer[cols, :])
        put_both(send, keep, half + col, (grad_hidden * up * rise).astype(BF))
        put_both(send, keep, half + width + col, (grad_hidden * value).astype(BF))
        put_both(send, keep, 2 * half + 2 * width + col, (value * up).astype(BF))
    part[...] = mm_nt(keep[:, half : half + width], inner[0]) + mm_nt(
        keep[:, half + width : half + 2 * width], inner[1]
    )
    part.flush()
    put_cut(send, keep, 0, normed, order)
    put_cut(send, keep, half + 2 * width, low, order_outer)


def tail_parts_kernel(enc_part, dec_part, keep, outer, part):
    enc_rows, dec_rows = enc_part.shape[0], dec_part.shape[0]
    part[:enc_rows, :] = enc_part[...]
    part[enc_rows : enc_rows + dec_rows, :] = dec_part[...]
    part[enc_rows + dec_rows :, :] = mm(keep[:, keep.shape[1] - outer.shape[0] :], outer[...])


def tail_kernel(own, other, enc_state, enc_gain, enc_grad, dec_state, dec_gain, dec_grad, state, enc_out, dec_out, out):
    enc_rows, dec_rows = enc_out.shape[0], dec_out.shape[0]
    span = slice(0, enc_rows)
    grad_in, _ = norm_back(own[span, :] + other[span, :], enc_state[...].astype(F32), enc_gain[0:1, :])
    enc_out[...] = (enc_grad[...] + grad_in).astype(BF)
    span = slice(enc_rows, enc_rows + dec_rows)
    grad_in, _ = norm_back(own[span, :] + other[span, :], dec_state[...].astype(F32), dec_gain[0:1, :])
    dec_out[...] = (dec_grad[...] + grad_in).astype(BF)
    span = slice(enc_rows + dec_rows, enc_rows + 2 * dec_rows)
    out[...] = (state[...] + own[span, :] + other[span, :]).astype(BF)


def query_part_kernel(keep, stacked, part):
    half = stacked.shape[1] // 2
    part[...] = mm_nt(keep[:, half : half + stacked.shape[2]], stacked[0])


def cross_back_kernel(
    length, counts, own, other, state, gain, grad, outer, query, kv, stacked, order, dec_state, enc_state, enc_gain,
    part, grad_ref, gain_ref, send, keep, key_grads,
):
    grad_in, normed = norm_back(own[...] + other[...], state[...], gain[2:3, :])
    gain_ref[...] = gain_part(own[...], normed)
    full = grad[...].astype(F32) + grad_in
    grad_ref[...] = full
    flush(gain_ref, grad_ref)
    low = full.astype(BF)
    width, half = outer.shape[0], order.shape[0] // 2
    grad_mixed = mm_nt(low, outer[...]).astype(BF)
    plots = kv.shape[0] // length
    rows = low.shape[0] // plots
    for plot in range(plots):
        bias = length_bias(counts[plot], rows, length)
        q_span = slice(plot * rows, (plot + 1) * rows)
        k_span = slice(plot * length, (plot + 1) * length)
        for cols in pairs_of(width):
            values = slice(width + cols.start, width + cols.stop)
            grad_query, grad_keys, grad_values = pair_back(
                query[q_span, cols], kv[k_span, cols], kv[k_span, values], grad_mixed[q_span, cols], bias
            )
            keep[q_span, half + cols.start : half + cols.stop] = grad_query
            send[q_span, half + cols.start : half + cols.stop] = grad_query.astype(F32)
            key_grads[k_span, cols] = grad_keys
            key_grads[k_span, values] = grad_values
    send.flush(half, half + width)
    keep.flush(half, half + width)
    part[...] = mm_nt(key_grads[:, :width], stacked[1]) + mm_nt(key_grads[:, width:], stacked[2])
    part.flush()
    put_cut(send, keep, 0, norm(dec_state[...], gain[1:2, :]), order)
    at = put_cut(send, keep, half + width, low, order)
    base = put_both(send, keep, at, query[:, width : 2 * width])
    ordered = mm(norm(enc_state[...], enc_gain[2:3, :]), order[...])
    for fold in range(kv.shape[0] // low.shape[0]):
        span = slice(fold * low.shape[0], (fold + 1) * low.shape[0])
        put(send, base, ordered[span, :half])
        put(keep, base, ordered[span, half:])
        base = put_both(send, keep, base + half, key_grads[span, :])


def self_back_kernel(
    causal, length, counts, own, other, state, gain, grad, outer, qkv, stacked, order, inputs,
    part, grad_ref, gain_ref, send, keep,
):
    grad_in, normed = norm_back(own[...] + other[...], state[...], gain[1:2, :])
    gain_ref[0:1, :] = gain_part(own[...], normed)
    full = grad[...] + grad_in
    grad_ref[...] = full
    flush(gain_ref, grad_ref)
    low = full.astype(BF)
    width, half = outer.shape[0], order.shape[0] // 2
    grad_mixed = mm_nt(low, outer[...]).astype(BF)
    for span, bias in keys_of(causal, length, low.shape[0], counts):
        for cols in pairs_of(width):
            grads = pair_back(
                qkv[span, cols],
                qkv[span, width + cols.start : width + cols.stop],
                qkv[span, 2 * width + cols.start : 2 * width + cols.stop],
                grad_mixed[span, cols],
                bias,
            )
            for which, piece in enumerate(grads):
                start = half + which * width + cols.start
                keep[span, start : start + PAIR] = piece
                send[span, start : start + PAIR] = piece.astype(F32)
    send.flush(half, half + 3 * width)
    keep.flush(half, half + 3 * width)
    total = mm_nt(keep[:, half : half + width], stacked[0])
    total += mm_nt(keep[:, half + width : half + 2 * width], stacked[1])
    total += mm_nt(keep[:, half + 2 * width : half + 3 * width], stacked[2])
    part[...] = total
    normed = scaled(inputs[...].astype(F32))
    gain_ref[1:2, :] = gain_part(total, normed)
    put_cut(send, keep, 0, (normed * gain[0:1, :]).astype(BF), order)
    at = put_cut(send, keep, half + 3 * width, low, order)
    put_both(send, keep, at, qkv[:, 3 * width : 4 * width])


def enc_mlp_back_kernel(
    own, other, state, gain, outer, pre, inner, order, order_outer, middle,
    part, grad_ref, gain_ref, send, keep,
):
    full, normed = norm_back(own[...] + other[...], state[...], gain[2:3, :])
    gain_ref[...] = gain_part(own[...], normed)
    grad_ref[...] = full
    flush(gain_ref, grad_ref)
    low = full.astype(BF)
    width, half = outer.shape[0], order.shape[0] // 2
    step = 256
    for col in range(0, width, step):
        cols = slice(col, col + step)
        value, rise = gelu_parts(pre[:, cols])
        up = pre[:, width + col : width + col + step]
        grad_hidden = mm_nt(low, outer[cols, :])
        put_both(send, keep, half + col, (grad_hidden * up * rise).astype(BF))
        put_both(send, keep, half + width + col, (grad_hidden * value).astype(BF))
        put_both(send, keep, 2 * half + 2 * width + col, (value * up).astype(BF))
    part[...] = mm_nt(keep[:, half : half + width], inner[0]) + mm_nt(
        keep[:, half + width : half + 2 * width], inner[1]
    )
    part.flush()
    put_cut(send, keep, 0, norm(middle[...], gain[1:2, :]), order)
    put_cut(send, keep, half + 2 * width, low, order_outer)


def gains_kernel(enc_attn, enc_mlp, dec_self, dec_cross, order, send, keep):
    rows = [enc_attn[1:2, :], enc_attn[0:1, :], enc_mlp[...], dec_self[1:2, :], dec_self[0:1, :], dec_cross[...]]
    rest = jnp.concatenate(rows + [jnp.zeros((128 - len(rows), order.shape[0]), F32)], 0)
    total = None
    for _ in range(3):
        low = rest.astype(BF)
        rest = rest - low.astype(F32)
        moved = lax.dot_general(order[...], low, (((0,), (1,)), ((), ())), preferred_element_type=F32)
        total = moved if total is None else total + moved
    half = total.shape[0] // 2
    send[...] = total[:half]
    keep[...] = total[half:]


def gains_out_kernel(own, other, enc_out, dec_out):
    total = own[...] + other[...]
    rows, columns = total.shape
    total = jnp.concatenate([total, jnp.zeros((columns - rows, columns), F32)], 0).T
    enc_out[...] = total[0:3, :rows]
    dec_out[...] = total[3:6, :rows]


def gains_weight_kernel(segments, keep, recv, gains, other_gains, send_out, keep_out):
    weight_kernel(segments, keep, recv, send_out, keep_out)
    total = gains[...] + other_gains[...]
    half, first = send_out.shape[0], send_out.shape[1] - total.shape[1]
    send_out[:, first:] = total[:half]
    keep_out[:, first:] = total[half:]


def weight_kernel(segments, keep, recv, *outs):
    last_of = {(group, target): at for at, (_, _, _, _, group, target) in enumerate(segments)}
    started = set()
    for number, (cut, cut_width, first, columns, group, target) in enumerate(segments):
        send_out, keep_out = outs[2 * group], outs[2 * group + 1]
        left = jnp.concatenate([keep[:, cut : cut + cut_width], recv[:, cut : cut + cut_width].astype(BF)], 0)
        half = cut_width // 2
        step = 512 if columns % 512 == 0 else 384
        for at in range(0, columns, step):
            cols = slice(first + at, first + at + step)
            right = jnp.concatenate([keep[:, cols], recv[:, cols].astype(BF)], 0)
            total = mm_tn(left, right)
            into = slice(target + at, target + at + step)
            if (group, target) in started:
                total += jnp.concatenate([send_out[:, into], keep_out[:, into]], 0)
            send_out[:, into] = total[:half]
            keep_out[:, into] = total[half:]
            if last_of[group, target] == number:
                send_out.flush(into.start, into.stop)
                keep_out.flush(into.start, into.stop)
        started.add((group, target))


def halve_kernel(kept, recv, send_out, keep_out):
    rows = send_out.shape[0]
    send_out[...] = kept[:rows] + recv[:rows]
    send_out.flush()
    keep_out[...] = kept[rows:] + recv[rows:]


SMEM = pl.BlockSpec(memory_space=pltpu.SMEM)
VMEM = pl.BlockSpec(memory_space=pltpu.VMEM)
ANY = pl.BlockSpec(memory_space=pl.ANY)


COST = {
    "enc_attn_fwd": 2.3, "dec_self_fwd": 2.5, "enc_mlp_fwd": 1.7, "cross_fwd": 4.2, "dec_mlp": 2.7,
    "cross_back": 3.0, "weights_c": 0.3, "enc_mlp_back": 3.0, "enc_attn_back": 1.0, "query_part": 20.0,
    "weights_f": 8.0, "weights_a": 0.1, "dec_self_back": 3.0, "weights_s": 3.0, "tail_parts": 0.1,
    "tail": 8.0, "gains": 8.0, "gains_out": 0.1, "halve_m": 20.0, "halve_mo": 1.0,
    "halve_c": 0.1, "halve_f": 3.0, "halve_fo": 3.0, "halve_s": 0.1, "halve_a": 1.0,
    "finish_m": 3.0, "finish_mo": 1.0, "finish_c": 8.0, "finish_f": 1.0, "finish_fo": 3.0,
    "finish_s": 1.0, "finish_a": 1.0, "weights_m": 1.0,
}
VMEM_LIMIT = 8

LINE = (
    "pause", "enc_attn_0", "enc_attn_1", "dec_self", "pause", "enc_mlp_0", "enc_mlp_1", "pause",
    "cross_0", "cross_1", "pause", "dec_mlp", "tick", "w_m", "cross_back", "h_mo",
    "w_c", "enc_mlp_back", "tick", "h_m", "query_part", "w_f", "h_mo", "dec_self_back",
    "h_c", "h_fo", "enc_attn_back", "h_mo", "h_f", "w_s", "gains", "h_m",
    "w_a", "h_c", "h_f", "h_m", "h_c", "h_s", "h_a", "tail_parts",
    "h_fo", "h_f", "e_c", "h_s", "tick", "h_a", "e_f", "h_fo",
    "h_a", "tail", "e_m", "e_mo", "h_s", "e_a", "e_fo", "gains_out",
    "e_s",
)
HALVINGS = {"m": "pxme", "mo": "xpme", "c": "xpme", "f": "pxme", "fo": "xpme", "s": "pxme", "a": "xpme"}
PARTS = {"m": 1, "c": 3, "f": 1, "a": 1, "s": 1}
TICK = 0.1
GAINS_WITH = "a"


class Stored:
    def __init__(self, ref):
        self.ref = ref
        self.shape, self.dtype = ref.shape, ref.dtype

    def __getitem__(self, at):
        return self.ref[at]

    def __setitem__(self, at, value):
        self.ref[at] = value

    def flush(self, first=0, last=None):
        pass


class Columns:
    def __init__(self, refs):
        self.refs = refs
        self.shape = (refs[0].shape[0], sum(ref.shape[1] for ref in refs))
        self.dtype = refs[0].dtype

    def __getitem__(self, at):
        rows, cols = at
        first, last = cols.start or 0, self.shape[1] if cols.stop is None else cols.stop
        pieces, start = [], 0
        for ref in self.refs:
            low, high = max(first - start, 0), min(last - start, ref.shape[1])
            if low < high:
                pieces.append(ref[rows, low:high])
            start += ref.shape[1]
        return pieces[0] if len(pieces) == 1 else jnp.concatenate(pieces, 1)

    def __setitem__(self, at, value):
        rows, cols = at
        first, last = cols.start or 0, self.shape[1] if cols.stop is None else cols.stop
        start = 0
        for ref in self.refs:
            low, high = max(first - start, 0), min(last - start, ref.shape[1])
            if low < high:
                ref[rows, low:high] = value[:, low + start - first : high + start - first]
            start += ref.shape[1]

    def flush(self, first=0, last=None):
        pass


class Stack:
    def __init__(self, *parts):
        self.parts = parts


class Rows:
    def __init__(self, refs, spans):
        self.refs = [ref.at[first:last] if (first, last) != (0, ref.shape[0]) else ref
                     for ref, (first, last) in zip(refs, spans)]
        self.heights = [last - first for first, last in spans]
        self.shape = (sum(self.heights),) + tuple(refs[0].shape[1:])
        self.dtype = refs[0].dtype

    def __getitem__(self, at):
        rows, cols = (slice(None), slice(None)) if at is Ellipsis else at
        first, last, _ = rows.indices(self.shape[0])
        pieces, start = [], 0
        for ref, height in zip(self.refs, self.heights):
            low, high = max(first - start, 0), min(last - start, height)
            if low < high:
                pieces.append(ref[low:high, cols])
            start += height
        return pieces[0] if len(pieces) == 1 else jnp.concatenate(pieces, 0)


def flush(*refs):
    for ref in refs:
        ref.flush()


class Line:
    def __init__(self):
        self.last = None

    def call(self, kernel, outs, args, name, scratch=(), cost=None):
        spans = [[part[1:] for part in a.parts] if isinstance(a, Stack) else None for a in args]
        args = [[part[0] for part in a.parts] if isinstance(a, Stack) else a for a in args]
        flat_args, args_tree = jax.tree.flatten(list(args))
        widths = [out if isinstance(out, list) else [out] for out in outs]
        shapes = [jax.ShapeDtypeStruct(*out) for group in widths for out in group]
        in_specs = [VMEM if a.ndim > 1 else SMEM for a in flat_args]
        count, made = len(flat_args), len(shapes)
        operands = list(flat_args)
        if self.last is not None:
            operands.append(self.last)
            in_specs.append(ANY)
        total = len(operands)

        def run(*refs):
            ins = jax.tree.unflatten(args_tree, refs[:count])
            ins = [Rows(i, span) if span else Columns(i) if isinstance(i, list) else i for i, span in zip(ins, spans)]
            left = list(refs[total : total + made])
            results = []
            for group, out in zip(widths, outs):
                taken, left = [Stored(ref) for ref in left[: len(group)]], left[len(group) :]
                results.append(Columns(taken) if isinstance(out, list) else taken[0])
            kernel(*ins, *results, *refs[total + made :])

        cost = COST.get(name, 0.3) if cost is None else cost
        flat = pl.pallas_call(
            run,
            out_shape=shapes,
            in_specs=in_specs,
            out_specs=[VMEM] * made,
            scratch_shapes=list(scratch),
            compiler_params=pltpu.CompilerParams(vmem_limit_bytes=VMEM_LIMIT * MIB),
            cost_estimate=pl.CostEstimate(
                flops=int(cost * 1.15e9), bytes_accessed=int(cost * 3.69e6), transcendentals=0
            ),
            name=name,
        )(*operands)
        self.last = min(flat, key=lambda r: r.size)
        results, left = [], list(flat)
        for group, out in zip(widths, outs):
            results.append(left[: len(group)] if isinstance(out, list) else left[0])
            left = left[len(group) :]
        return results


def join_kernel(kept, recv, out):
    out[...] = kept[...] + recv[...]


def middle_kernel(kept, recv, send_out, keep_out):
    rows = send_out.shape[0]
    me = lax.axis_index("dp")
    inner = ((me >> 2) ^ (me >> 3)) & 1
    send_out[...] = jnp.where(inner == 1, recv[rows:], kept[:rows])
    keep_out[...] = jnp.where(inner == 1, recv[:rows], kept[rows:])


def finish_kernel(pieces, kept, recv, *outs):
    for out, (first, count) in zip(outs, pieces):
        width = out.shape[-1]
        for i in range(count):
            cols = slice(first + i * width, first + (i + 1) * width)
            total = kept[:, cols] + recv[:, cols]
            if count > 1:
                out[i] = total
            else:
                out[...] = total


def tick_kernel(source, target):
    target[...] = source[0:1, 0:128]


def pair_other(part, name):
    with jax.named_scope("pair_" + name):
        return lax.ppermute(part, "mp", [(0, 1), (1, 0)])


def swap(value, step, name):
    shards = lax.axis_size("dp")
    bit = {"x": 1, "p": 2, "e": 2}.get(step, step)
    if step == "m":
        pairs = [(i, i ^ 12) for i in range(shards) if (i >> 2 ^ i >> 3) & 1]
    else:
        pairs = [(i, i ^ (1 << bit)) for i in range(shards)]
    with jax.named_scope("swap_%s_%s" % (name, step)):
        return lax.ppermute(value, "dp", pairs)


def feature_order(features, steps):
    shards = lax.axis_size("dp")
    me = lax.axis_index("dp")
    block = features // shards
    column = jnp.arange(features, dtype=jnp.int32)
    place = column // block
    owner = jnp.zeros_like(column)
    other = {step: 1 - ((place >> (len(steps) - 1 - at)) & 1) for at, step in enumerate(steps)}
    near = (me >> 2) & 1
    for step in steps:
        if step == "p":
            owner = owner | ((near ^ other["p"]) << 3)
        elif step == "e":
            owner = owner | ((near ^ other["e"] ^ other["p"]) << 2)
        else:
            bit = 1 if step == "x" else step
            owner = owner | ((((me >> bit) & 1) ^ other[step]) << bit)
    source = owner * block + column % block
    return (jnp.arange(features, dtype=jnp.int32)[:, None] == source[None, :]).astype(BF)


class Halving:
    def __init__(self, sent, kept, steps, name):
        self.steps, self.name, self.at = steps, name, 0
        self.kept = kept
        self.flying = swap(sent, steps[0], name)

    def step(self, line):
        came, self.at = self.steps[self.at], self.at + 1
        rows, columns = self.kept.shape
        args, name = [self.kept, self.flying], "halve_" + self.name
        if self.steps[self.at] == "m":
            (self.kept,) = line.call(join_kernel, [((rows, columns), F32)], args, name)
            sent = self.kept
        else:
            shape = ((rows // 2, columns), F32)
            sent, self.kept = line.call(middle_kernel if came == "m" else halve_kernel, [shape, shape], args, name)
        self.flying = swap(sent, self.steps[self.at], self.name)

    def finish(self, line, *pieces):
        for bit in range(4, lax.axis_size("dp").bit_length() - 1):
            rows = self.kept.shape[0] // 2
            total = self.kept + self.flying
            self.kept, self.flying = total[rows:], swap(total[:rows], bit, self.name)
        rows = self.kept.shape[0]
        outs = [(((count, rows, width) if count > 1 else (rows, width)), F32) for _, count, width in pieces]
        return line.call(
            functools.partial(finish_kernel, [(first, count) for first, count, _ in pieces]),
            outs, [self.kept, self.flying], "finish_" + self.name,
        )


def body(
    enc_in, dec_in, cotangent, patch_counts, table_lengths, enc_qkv, enc_attn_out, enc_mlp_in, enc_mlp_out, enc_gains,
    dec_self_qkv, dec_self_out, dec_cross_qkv, dec_cross_out, dec_mlp_in, dec_mlp_out, dec_gains,
):
    plots, enc_len, features = enc_in.shape
    dec_len = dec_in.shape[1]
    enc_rows, dec_rows = plots * enc_len, plots * dec_len
    heads = enc_attn_out.shape[0]
    units = enc_mlp_out.shape[0]
    half = features // 2
    bits = lax.axis_size("dp").bit_length() - 1
    orders = {}

    def order_by(steps):
        cuts = (0,) + tuple(step for step in steps if step != "m") + tuple(range(4, bits))
        if cuts not in orders:
            orders[cuts] = feature_order(features, cuts)
        return orders[cuts]

    order_of = {name: order_by(steps) for name, steps in HALVINGS.items()}
    x0 = enc_in.reshape(enc_rows, features)
    y0 = dec_in.reshape(dec_rows, features)
    top = cotangent.reshape(dec_rows, features)
    enc_wide, dec_wide = ((enc_rows, features), F32), ((dec_rows, features), F32)
    enc_low, dec_low = ((enc_rows, features), BF), ((dec_rows, features), BF)
    gain_row, gain_rows = ((1, features), F32), ((2, features), F32)
    quarter = half // 2
    line = Line()

    def tick(cost=TICK):
        line.call(tick_kernel, [((1, 128), F32)], [enc_gains], "tick", cost=cost)

    def parts_of(name, rows, width):
        count, tiles = PARTS[name], width // 128
        edges = [128 * (tiles * i // count) for i in range(count + 1)]
        return [((rows, high - low), F32) for low, high in zip(edges, edges[1:])]

    def swap_cores(name, parts):
        return [swap(part, 0, name) for part in parts]

    def group(columns):
        return [((quarter, columns), F32)] * 2

    def mlp_of(name):
        apart = name + "o" in HALVINGS
        target = (1, 0) if apart else (0, 2 * units)
        segments = (
            (0, half, half, 2 * units, 0, 0),
            (half + 2 * units, half, 2 * half + 2 * units, units) + target,
        )
        return segments, group(2 * units) + group(units) if apart else group(3 * units)

    attn_segments = (
        (0, half, half, 3 * heads, 0, 0),
        (half + 3 * heads, half, 2 * half + 3 * heads, heads, 0, 3 * heads),
    )
    base, fold_width = 2 * half + 2 * heads, half + 2 * heads
    folds = enc_rows // dec_rows
    cross_segments = (
        (0, half, half, heads, 0, 0),
        (half + heads, half, 2 * half + heads, heads, 0, heads),
    ) + tuple(
        (base + f * fold_width, half, base + f * fold_width + half, 2 * heads, 0, 2 * heads) for f in range(folds)
    )
    attn_group = group(4 * heads)
    mlp_wide = 2 * half + 3 * units
    attn_wide = 2 * half + 4 * heads
    cross_wide = base + folds * fold_width
    v, sums, grad_of = {}, {}, {}

    def pause():
        tick(6.0)

    def enc_attn(p):
        v["part_e1", p], v["enc_saved", p] = line.call(
            functools.partial(self_fwd_kernel, False, enc_len, p),
            [((enc_len, features), F32), ((enc_len, 4 * heads), BF)],
            [patch_counts, x0, enc_gains, enc_qkv, enc_attn_out], "enc_attn_fwd",
        )
        v["other_e1", p] = pair_other(v["part_e1", p], "e1")

    def dec_self():
        v["part_d1"], v["dec_saved"] = line.call(
            functools.partial(self_fwd_kernel, True, dec_len, 0),
            [dec_wide, ((dec_rows, 4 * heads), BF)],
            [table_lengths, y0, dec_gains, dec_self_qkv, dec_self_out], "dec_self_fwd",
        )
        v["other_d1"] = pair_other(v["part_d1"], "d1")

    def enc_mlp(p):
        v["part_e2", p], v["x1", p], v["pre", p] = line.call(
            functools.partial(enc_mlp_fwd_kernel, p),
            [((enc_len, features), F32), ((enc_len, features), F32), ((enc_len, 2 * units), F32)],
            [x0, v["part_e1", p], v["other_e1", p], enc_gains, enc_mlp_in, enc_mlp_out], "enc_mlp_fwd",
        )
        v["other_e2", p] = pair_other(v["part_e2", p], "e2")

    def cross(p):
        v["part_d2", p], v["states", p], v["saved", p] = line.call(
            functools.partial(cross_fwd_kernel, enc_len, p),
            [((dec_len, features), F32), ((enc_len + dec_len, features), F32), ((enc_len + dec_len, 2 * heads), BF)],
            [patch_counts, v["x1", p], v["part_e2", p], v["other_e2", p], enc_gains, y0, v["part_d1"], v["other_d1"],
             dec_gains, dec_cross_qkv, dec_cross_out],
            "cross_fwd",
        )
        v["other_d2", p] = pair_other(v["part_d2", p], "d2")

    def stack(name, first, last):
        return Stack(*[(v[name, p], first, last) for p in range(plots)])

    def enc_part(name):
        return stack(name, 0, enc_len)

    def dec_part(name):
        return stack(name, enc_len, enc_len + dec_len)

    def dec_mlp():
        v["part_g3"], v["y2"], send, v["keep_m"] = line.call(
            dec_mlp_kernel,
            [dec_wide, dec_wide, parts_of("m", dec_rows, mlp_wide), ((dec_rows, mlp_wide), BF)],
            [dec_part("states"), stack("part_d2", 0, dec_len), stack("other_d2", 0, dec_len), dec_gains, top,
             dec_mlp_in, dec_mlp_out, order_of["m"], order_of.get("mo", order_of["m"])],
            "dec_mlp",
        )
        v["other_g3"] = pair_other(v["part_g3"], "g3")
        v["recv_m"] = swap_cores("m", send)

    def start_sums(name, products):
        for group_name, pair in zip((name, name + "o"), zip(products[::2], products[1::2])):
            sums[group_name] = Halving(pair[0], pair[1], HALVINGS[group_name], group_name)

    def mlp_weights(name, keep, recv):
        segments, groups = mlp_of(name)
        start_sums(
            name, line.call(functools.partial(weight_kernel, segments), groups, [keep, recv], "weights_" + name)
        )

    def dec_mlp_weights():
        mlp_weights("m", v["keep_m"], v["recv_m"])

    def cross_back():
        v["part_m"], v["g2"], v["gain_dec_cross"], send, v["keep_c"] = line.call(
            functools.partial(cross_back_kernel, enc_len),
            [enc_wide, dec_wide, gain_row, parts_of("c", dec_rows, cross_wide), ((dec_rows, cross_wide), BF)],
            [patch_counts, v["part_g3"], v["other_g3"], v["y2"], dec_gains, top, dec_cross_out, dec_part("saved"),
             enc_part("saved"), dec_cross_qkv, order_of["c"], dec_part("states"), enc_part("states"), enc_gains],
            "cross_back", scratch=[pltpu.VMEM((enc_rows, 2 * heads), BF)],
        )
        v["other_m"] = pair_other(v["part_m"], "m")
        v["recv_c"] = swap_cores("c", send)

    def cross_weights():
        start_sums("c", line.call(
            functools.partial(weight_kernel, cross_segments), attn_group, [v["keep_c"], v["recv_c"]], "weights_c"
        ))

    def enc_mlp_back():
        v["part_g1"], v["back2"], v["gain_enc_mlp"], send, v["keep_f"] = line.call(
            enc_mlp_back_kernel,
            [enc_wide, enc_wide, gain_row, parts_of("f", enc_rows, mlp_wide), ((enc_rows, mlp_wide), BF)],
            [v["part_m"], v["other_m"], enc_part("states"), enc_gains, enc_mlp_out, enc_part("pre"), enc_mlp_in,
             order_of["f"], order_of.get("fo", order_of["f"]), enc_part("x1")],
            "enc_mlp_back",
        )
        v["other_g1"] = pair_other(v["part_g1"], "g1")
        v["recv_f"] = swap_cores("f", send)

    def enc_mlp_weights():
        mlp_weights("f", v["keep_f"], v["recv_f"])

    def enc_attn_back():
        v["part_ge"], v["back1"], v["gain_enc_attn"], send, v["keep_a"] = line.call(
            functools.partial(self_back_kernel, False, enc_len),
            [enc_wide, enc_wide, gain_rows, parts_of("a", enc_rows, attn_wide), ((enc_rows, attn_wide), BF)],
            [patch_counts, v["part_g1"], v["other_g1"], enc_part("x1"), enc_gains, v["back2"], enc_attn_out,
             enc_part("enc_saved"), enc_qkv, order_of["a"], x0],
            "enc_attn_back",
        )
        v["recv_a"] = swap_cores("a", send)

    def query_part():
        (v["part_q"],) = line.call(query_part_kernel, [dec_wide], [v["keep_c"], dec_cross_qkv], "query_part")
        v["other_q"] = pair_other(v["part_q"], "q")

    def dec_self_back():
        v["part_g0"], v["g1"], v["gain_dec_self"], send, v["keep_s"] = line.call(
            functools.partial(self_back_kernel, True, dec_len),
            [dec_wide, dec_wide, gain_rows, parts_of("s", dec_rows, attn_wide), ((dec_rows, attn_wide), BF)],
            [table_lengths, v["part_q"], v["other_q"], dec_part("states"), dec_gains, v["g2"], dec_self_out,
             v["dec_saved"], dec_self_qkv, order_of["s"], y0],
            "dec_self_back",
        )
        v["recv_s"] = swap_cores("s", send)

    def tail_parts():
        (v["part_tail"],) = line.call(
            tail_parts_kernel, [((enc_rows + 2 * dec_rows, features), F32)],
            [v["part_ge"], v["part_g0"], v["keep_m"], dec_mlp_out], "tail_parts",
        )
        v["other_tail"] = pair_other(v["part_tail"], "tail")

    def tail():
        v["enc_out"], v["dec_out_grad"], v["dec_out"] = line.call(
            tail_kernel, [enc_low, dec_low, dec_low],
            [v["part_tail"], v["other_tail"], x0, enc_gains, v["back1"], y0, dec_gains, v["g1"], v["y2"]], "tail",
        )

    def gains():
        send, v["keep_g"] = line.call(
            gains_kernel, [((half, 128), F32), ((half, 128), F32)],
            [v["gain_enc_attn"], v["gain_enc_mlp"], v["gain_dec_self"], v["gain_dec_cross"], order_of[GAINS_WITH]],
            "gains",
        )
        v["recv_g"] = swap(send, 0, "g")

    def gains_sum():
        v["other_gains"] = pair_other(grad_of[GAINS_WITH][2], "gains")

    def gains_out():
        own = grad_of[GAINS_WITH][2]
        shape = ((3, own.shape[0]), F32)
        v["gains_out"] = line.call(gains_out_kernel, [shape, shape], [own, v["other_gains"]], "gains_out")

    def attn_weights(name):
        if name == GAINS_WITH:
            products = line.call(
                functools.partial(gains_weight_kernel, attn_segments), group(4 * heads + 128),
                [v["keep_" + name], v["recv_" + name], v["keep_g"], v["recv_g"]], "weights_" + name,
            )
        else:
            products = line.call(
                functools.partial(weight_kernel, attn_segments), attn_group,
                [v["keep_" + name], v["recv_" + name]], "weights_" + name,
            )
        start_sums(name, products)

    attn_pieces = ((0, 3, heads), (3 * heads, 1, heads))
    ends = {
        "m": ((0, 2, units),), "f": ((0, 2, units),), "mo": ((0, 1, units),), "fo": ((0, 1, units),),
        "c": ((0, 1, heads), (heads, 1, heads), (2 * heads, 2, heads)), "a": attn_pieces, "s": attn_pieces,
    }
    for name in ("m", "f"):
        if name + "o" not in HALVINGS:
            ends[name] += ((2 * units, 1, units),)
    ends[GAINS_WITH] += ((4 * heads, 1, 128),)
    stages = {
        "tick": tick, "pause": pause, "dec_self": dec_self, "dec_mlp": dec_mlp, "w_m": dec_mlp_weights,
        "cross_back": cross_back, "w_c": cross_weights, "enc_mlp_back": enc_mlp_back,
        "w_f": enc_mlp_weights, "enc_attn_back": enc_attn_back, "query_part": query_part, "gains": gains,
        "tail_parts": tail_parts, "tail": tail, "gains_out": gains_out,
        "w_a": functools.partial(attn_weights, "a"), "dec_self_back": dec_self_back,
        "w_s": functools.partial(attn_weights, "s"),
    }
    for name, stage in (("enc_attn", enc_attn), ("enc_mlp", enc_mlp), ("cross", cross)):
        for p in range(plots):
            stages["%s_%d" % (name, p)] = functools.partial(stage, p)
    for stage in LINE:
        kind, _, name = stage.partition("_")
        if stage in stages:
            stages[stage]()
        elif kind == "h":
            sums[name].step(line)
        else:
            grad_of[name] = sums[name].finish(line, *ends[name])
            if name == GAINS_WITH:
                gains_sum()
    mlp_grads = {
        name: grad_of[name] if name + "o" not in HALVINGS else grad_of[name] + grad_of[name + "o"] for name in ("m", "f")
    }
    grad_c = jnp.concatenate([grad_of["c"][0][None], grad_of["c"][2]], 0)
    grads = (
        grad_of["a"][0], grad_of["a"][1].T, mlp_grads["f"][0], mlp_grads["f"][1].T, v["gains_out"][0],
        grad_of["s"][0], grad_of["s"][1].T, grad_c, grad_of["c"][1].T, mlp_grads["m"][0], mlp_grads["m"][1].T,
        v["gains_out"][1],
    )
    return (
        v["dec_out"].reshape(cotangent.shape),
        v["enc_out"].reshape(enc_in.shape),
        v["dec_out_grad"].reshape(dec_in.shape),
    ) + grads


def solution(mesh):
    rows = P("dp", None, None)
    inner, outer = P(None, None, "mp"), P("mp", None)
    enc = (inner, outer, inner, outer, P())
    dec = (inner, outer, inner, outer, inner, outer, P())
    inner_grad, outer_grad, gain_grad = P(None, "dp", "mp"), P("mp", "dp"), P(None, "dp")
    return jax.shard_map(
        body,
        mesh=mesh,
        in_specs=(rows, rows, rows, P("dp"), P("dp")) + enc + dec,
        out_specs=(rows, rows, rows)
        + (inner_grad, outer_grad) * 2 + (gain_grad,)
        + (inner_grad, outer_grad) * 3 + (gain_grad,),
        check_vma=False,
    )
```

```python
import functools

import jax
import jax.numpy as jnp
from jax import lax
from jax.experimental import pallas as pl
from jax.experimental.pallas import tpu as pltpu
from jax.sharding import PartitionSpec as P

HEAD_DIM = 64
PAIR = 2 * HEAD_DIM
EPSILON = 1e-06
NEG_LARGE = -1e30
SCALE = HEAD_DIM ** (-0.5)
BF = jnp.bfloat16
F32 = jnp.float32
MIB = 1024 * 1024


def mm(left, right):
    return jnp.dot(left, right, preferred_element_type=F32)


def mm_nt(left, right):
    return lax.dot_general(left, right, (((1,), (1,)), ((), ())), preferred_element_type=F32)


def mm_tn(left, right):
    return lax.dot_general(left, right, (((0,), (0,)), ((), ())), preferred_element_type=F32)


def scaled(hidden):
    return hidden * lax.rsqrt(jnp.mean(hidden * hidden, -1, keepdims=True) + EPSILON)


def norm(hidden, gain):
    return (scaled(hidden) * gain).astype(BF)


def norm_back(grad, hidden, gain):
    scaling = lax.rsqrt(jnp.mean(hidden * hidden, -1, keepdims=True) + EPSILON)
    normed = hidden * scaling
    grad_hat = grad * gain
    return scaling * (grad_hat - normed * jnp.mean(grad_hat * normed, -1, keepdims=True)), normed


def gain_part(part, normed):
    return jnp.sum(part * normed, 0, keepdims=True)


def gelu_parts(gate):
    slope = 0.7978845608028654
    square = gate * gate
    bent = jnp.tanh(slope * gate * (1.0 + 0.044715 * square))
    half = 0.5 * (1.0 + bent)
    value = gate * half
    rise = half + 0.5 * gate * (1.0 - bent * bent) * slope * (1.0 + 0.134145 * square)
    return value, rise


def stack_heads(pair):
    lane = lax.broadcasted_iota(jnp.int32, pair.shape, 1)
    zero = jnp.zeros_like(pair)
    return jnp.concatenate(
        [jnp.where(lane < HEAD_DIM, pair, zero), jnp.where(lane < HEAD_DIM, zero, pair)], 0
    )


def merge_heads(stacked):
    rows = stacked.shape[0] // 2
    lane = lax.broadcasted_iota(jnp.int32, (rows, PAIR), 1)
    return jnp.where(lane < HEAD_DIM, stacked[:rows], stacked[rows:])


def soft_of(stacked_query, keys, bias):
    scores = mm_nt(stacked_query, keys) * SCALE + bias
    expon = jnp.exp(scores - jnp.max(scores, -1, keepdims=True))
    return expon / jnp.sum(expon, -1, keepdims=True)


def pair_fwd(query, keys, values, bias):
    soft = soft_of(stack_heads(query), keys, bias)
    return merge_heads(mm(soft.astype(BF), values)).astype(BF)


def pair_back(query, keys, values, grad_out, bias):
    queries = stack_heads(query)
    soft = soft_of(queries, keys, bias)
    grads = stack_heads(grad_out)
    grad_values = mm_tn(soft.astype(BF), grads)
    grad_soft = mm_nt(grads, values)
    grad_scores = (
        soft * (grad_soft - jnp.sum(soft * grad_soft, -1, keepdims=True))
    ).astype(BF)
    grad_query = merge_heads(mm(grad_scores, keys)) * SCALE
    grad_keys = mm_tn(grad_scores, queries) * SCALE
    return grad_query.astype(BF), grad_keys.astype(BF), grad_values.astype(BF)


def length_bias(count, rows, length):
    col = lax.broadcasted_iota(jnp.int32, (2 * rows, length), 1)
    return jnp.where(col < count, 0.0, NEG_LARGE).astype(F32)


def causal_bias(counts, plots, length):
    shape = (plots * length, plots * length)
    row = lax.broadcasted_iota(jnp.int32, shape, 0)
    col = lax.broadcasted_iota(jnp.int32, shape, 1)
    bias = jnp.full(shape, NEG_LARGE, F32)
    for plot in range(plots):
        low = plot * length
        inside = (row >= low) & (row < low + length) & (col >= low)
        inside = inside & (col <= row) & (col < low + counts[plot])
        bias = jnp.where(inside, 0.0, bias)
    return jnp.concatenate([bias, bias], 0)


def pairs_of(width):
    return [slice(at, at + PAIR) for at in range(0, width, PAIR)]


def put(ref, at, value):
    last = at + value.shape[1]
    ref[:, at:last] = value.astype(ref.dtype)
    ref.flush(at, last)
    return last


def put_both(send, keep, at, value):
    put(send, at, value)
    return put(keep, at, value)


def put_cut(send, keep, at, value, order):
    ordered = mm(value, order[...])
    half = ordered.shape[1] // 2
    put(send, at, ordered[:, :half])
    return put(keep, at, ordered[:, half:])


def keys_of(causal, length, rows, counts, first=0):
    plots = rows // length
    if causal:
        return [(slice(0, rows), causal_bias(counts, plots, length))]
    return [
        (slice(p * length, (p + 1) * length), length_bias(counts[first + p], length, length)) for p in range(plots)
    ]


def self_fwd_kernel(causal, length, first, counts, state, gain, stacked, outer, part, saved):
    rows, width = part.shape[0], outer.shape[0]
    normed = norm(state[first * length : first * length + rows, :].astype(F32), gain[0:1, :])
    for which in range(3):
        put(saved, which * width, mm(normed, stacked[which]))
    for span, bias in keys_of(causal, length, rows, counts, first):
        for cols in pairs_of(width):
            mixed = slice(3 * width + cols.start, 3 * width + cols.stop)
            saved[span, mixed] = pair_fwd(
                saved[span, cols],
                saved[span, width + cols.start : width + cols.stop],
                saved[span, 2 * width + cols.start : 2 * width + cols.stop],
                bias,
            )
    part[...] = mm(saved[:, 3 * width :], outer[...])


def enc_mlp_fwd_kernel(first, state, own, other, gain, inner, outer, part, state_ref, pre):
    rows, width = part.shape[0], outer.shape[0]
    full = state[first * rows : (first + 1) * rows, :].astype(F32) + own[...] + other[...]
    state_ref[...] = full
    normed = norm(full, gain[1:2, :])
    step = 256
    total = None
    for at in range(0, width, step):
        cols = slice(at, at + step)
        gate = mm(normed, inner[0, :, cols])
        up = mm(normed, inner[1, :, cols])
        value, _ = gelu_parts(gate)
        pre[:, cols] = gate
        pre[:, width + at : width + at + step] = up
        add = mm((value * up).astype(BF), outer[cols, :])
        total = add if total is None else total + add
    part[...] = total


def cross_fwd_kernel(
    length, first, counts, enc_state, enc_own, enc_other, enc_gain, dec_state, dec_own, dec_other, dec_gain, stacked,
    outer, part, states, saved,
):
    rows, width = part.shape[0], outer.shape[0]
    span = slice(first * rows, (first + 1) * rows)
    dec_full = dec_state[span, :].astype(F32) + dec_own[span, :] + dec_other[span, :]
    states[length:, :] = dec_full
    normed = norm(dec_full, dec_gain[1:2, :])
    saved[length:, :width] = mm(normed, stacked[0]).astype(BF)
    enc_full = enc_state[...] + enc_own[...] + enc_other[...]
    states[:length, :] = enc_full
    memory = norm(enc_full, enc_gain[2:3, :])
    saved[:length, :width] = mm(memory, stacked[1]).astype(BF)
    saved[:length, width:] = mm(memory, stacked[2]).astype(BF)
    bias = length_bias(counts[first], rows, length)
    for cols in pairs_of(width):
        beside = slice(width + cols.start, width + cols.stop)
        saved[length:, beside] = pair_fwd(saved[length:, cols], saved[:length, cols], saved[:length, beside], bias)
    part[...] = mm(saved[length:, width:], outer[...])


def dec_mlp_kernel(
    state, own, other, gain, cotangent, inner, outer, order, order_outer, part, state_ref, send, keep
):
    full = state[...] + own[...] + other[...]
    state_ref[...] = full
    state_ref.flush()
    normed = norm(full, gain[2:3, :])
    low = cotangent[...]
    width, half = outer.shape[0], order.shape[0] // 2
    step = 256
    for col in range(0, width, step):
        cols = slice(col, col + step)
        gate = mm(normed, inner[0, :, cols])
        up = mm(normed, inner[1, :, cols])
        value, rise = gelu_parts(gate)
        grad_hidden = mm_nt(low, outer[cols, :])
        put_both(send, keep, half + col, (grad_hidden * up * rise).astype(BF))
        put_both(send, keep, half + width + col, (grad_hidden * value).astype(BF))
        put_both(send, keep, 2 * half + 2 * width + col, (value * up).astype(BF))
    part[...] = mm_nt(keep[:, half : half + width], inner[0]) + mm_nt(
        keep[:, half + width : half + 2 * width], inner[1]
    )
    part.flush()
    put_cut(send, keep, 0, normed, order)
    put_cut(send, keep, half + 2 * width, low, order_outer)


def tail_parts_kernel(enc_part, dec_part, keep, outer, part):
    enc_rows, dec_rows = enc_part.shape[0], dec_part.shape[0]
    part[:enc_rows, :] = enc_part[...]
    part[enc_rows : enc_rows + dec_rows, :] = dec_part[...]
    part[enc_rows + dec_rows :, :] = mm(keep[:, keep.shape[1] - outer.shape[0] :], outer[...])


def tail_kernel(own, other, enc_state, enc_gain, enc_grad, dec_state, dec_gain, dec_grad, state, enc_out, dec_out, out):
    enc_rows, dec_rows = enc_out.shape[0], dec_out.shape[0]
    span = slice(0, enc_rows)
    grad_in, _ = norm_back(own[span, :] + other[span, :], enc_state[...].astype(F32), enc_gain[0:1, :])
    enc_out[...] = (enc_grad[...] + grad_in).astype(BF)
    span = slice(enc_rows, enc_rows + dec_rows)
    grad_in, _ = norm_back(own[span, :] + other[span, :], dec_state[...].astype(F32), dec_gain[0:1, :])
    dec_out[...] = (dec_grad[...] + grad_in).astype(BF)
    span = slice(enc_rows + dec_rows, enc_rows + 2 * dec_rows)
    out[...] = (state[...] + own[span, :] + other[span, :]).astype(BF)


def query_part_kernel(keep, stacked, part):
    half = stacked.shape[1] // 2
    part[...] = mm_nt(keep[:, half : half + stacked.shape[2]], stacked[0])


def cross_back_kernel(
    length, counts, own, other, state, gain, grad, outer, query, kv, stacked, order, dec_state, enc_state, enc_gain,
    part, grad_ref, gain_ref, send, keep, key_grads,
):
    grad_in, normed = norm_back(own[...] + other[...], state[...], gain[2:3, :])
    gain_ref[...] = gain_part(own[...], normed)
    full = grad[...].astype(F32) + grad_in
    grad_ref[...] = full
    flush(gain_ref, grad_ref)
    low = full.astype(BF)
    width, half = outer.shape[0], order.shape[0] // 2
    grad_mixed = mm_nt(low, outer[...]).astype(BF)
    plots = kv.shape[0] // length
    rows = low.shape[0] // plots
    for plot in range(plots):
        bias = length_bias(counts[plot], rows, length)
        q_span = slice(plot * rows, (plot + 1) * rows)
        k_span = slice(plot * length, (plot + 1) * length)
        for cols in pairs_of(width):
            values = slice(width + cols.start, width + cols.stop)
            grad_query, grad_keys, grad_values = pair_back(
                query[q_span, cols], kv[k_span, cols], kv[k_span, values], grad_mixed[q_span, cols], bias
            )
            keep[q_span, half + cols.start : half + cols.stop] = grad_query
            send[q_span, half + cols.start : half + cols.stop] = grad_query.astype(F32)
            key_grads[k_span, cols] = grad_keys
            key_grads[k_span, values] = grad_values
    send.flush(half, half + width)
    keep.flush(half, half + width)
    part[...] = mm_nt(key_grads[:, :width], stacked[1]) + mm_nt(key_grads[:, width:], stacked[2])
    part.flush()
    put_cut(send, keep, 0, norm(dec_state[...], gain[1:2, :]), order)
    at = put_cut(send, keep, half + width, low, order)
    base = put_both(send, keep, at, query[:, width : 2 * width])
    ordered = mm(norm(enc_state[...], enc_gain[2:3, :]), order[...])
    for fold in range(kv.shape[0] // low.shape[0]):
        span = slice(fold * low.shape[0], (fold + 1) * low.shape[0])
        put(send, base, ordered[span, :half])
        put(keep, base, ordered[span, half:])
        base = put_both(send, keep, base + half, key_grads[span, :])


def self_back_kernel(
    causal, length, counts, own, other, state, gain, grad, outer, qkv, stacked, order, inputs,
    part, grad_ref, gain_ref, send, keep,
):
    grad_in, normed = norm_back(own[...] + other[...], state[...], gain[1:2, :])
    gain_ref[0:1, :] = gain_part(own[...], normed)
    full = grad[...] + grad_in
    grad_ref[...] = full
    flush(gain_ref, grad_ref)
    low = full.astype(BF)
    width, half = outer.shape[0], order.shape[0] // 2
    grad_mixed = mm_nt(low, outer[...]).astype(BF)
    for span, bias in keys_of(causal, length, low.shape[0], counts):
        for cols in pairs_of(width):
            grads = pair_back(
                qkv[span, cols],
                qkv[span, width + cols.start : width + cols.stop],
                qkv[span, 2 * width + cols.start : 2 * width + cols.stop],
                grad_mixed[span, cols],
                bias,
            )
            for which, piece in enumerate(grads):
                start = half + which * width + cols.start
                keep[span, start : start + PAIR] = piece
                send[span, start : start + PAIR] = piece.astype(F32)
    send.flush(half, half + 3 * width)
    keep.flush(half, half + 3 * width)
    total = mm_nt(keep[:, half : half + width], stacked[0])
    total += mm_nt(keep[:, half + width : half + 2 * width], stacked[1])
    total += mm_nt(keep[:, half + 2 * width : half + 3 * width], stacked[2])
    part[...] = total
    normed = scaled(inputs[...].astype(F32))
    gain_ref[1:2, :] = gain_part(total, normed)
    put_cut(send, keep, 0, (normed * gain[0:1, :]).astype(BF), order)
    at = put_cut(send, keep, half + 3 * width, low, order)
    put_both(send, keep, at, qkv[:, 3 * width : 4 * width])


def enc_mlp_back_kernel(
    own, other, state, gain, outer, pre, inner, order, order_outer, middle,
    part, grad_ref, gain_ref, send, keep,
):
    full, normed = norm_back(own[...] + other[...], state[...], gain[2:3, :])
    gain_ref[...] = gain_part(own[...], normed)
    grad_ref[...] = full
    flush(gain_ref, grad_ref)
    low = full.astype(BF)
    width, half = outer.shape[0], order.shape[0] // 2
    step = 256
    for col in range(0, width, step):
        cols = slice(col, col + step)
        value, rise = gelu_parts(pre[:, cols])
        up = pre[:, width + col : width + col + step]
        grad_hidden = mm_nt(low, outer[cols, :])
        put_both(send, keep, half + col, (grad_hidden * up * rise).astype(BF))
        put_both(send, keep, half + width + col, (grad_hidden * value).astype(BF))
        put_both(send, keep, 2 * half + 2 * width + col, (value * up).astype(BF))
    part[...] = mm_nt(keep[:, half : half + width], inner[0]) + mm_nt(
        keep[:, half + width : half + 2 * width], inner[1]
    )
    part.flush()
    put_cut(send, keep, 0, norm(middle[...], gain[1:2, :]), order)
    put_cut(send, keep, half + 2 * width, low, order_outer)


def gain_rows_kernel(enc_attn, enc_mlp, dec_self, dec_cross, out):
    for at, row in enumerate((enc_attn[1:2, :], enc_attn[0:1, :], enc_mlp[...], dec_self[1:2, :], dec_self[0:1, :],
                              dec_cross[...])):
        out[at : at + 1, :] = row
    out[6:8, :] = jnp.zeros((2, out.shape[1]), F32)


def gains_kernel(own, other, order, send, keep):
    rest = own[...] + other[...]
    rest = jnp.concatenate([rest, jnp.zeros((128 - rest.shape[0], rest.shape[1]), F32)], 0)
    total = None
    for _ in range(3):
        low = rest.astype(BF)
        rest = rest - low.astype(F32)
        moved = lax.dot_general(order[...], low, (((0,), (1,)), ((), ())), preferred_element_type=F32)
        total = moved if total is None else total + moved
    half = total.shape[0] // 2
    send[...] = total[:half]
    keep[...] = total[half:]


def gains_weight_kernel(segments, keep, recv, gains, other_gains, send_out, keep_out):
    weight_kernel(segments, keep, recv, send_out, keep_out)
    total = gains[...] + other_gains[...]
    half, first = send_out.shape[0], send_out.shape[1] - total.shape[1]
    send_out[:, first:] = total[:half]
    keep_out[:, first:] = total[half:]


def weight_kernel(segments, keep, recv, *outs):
    last_of = {(group, target): at for at, (_, _, _, _, group, target) in enumerate(segments)}
    started = set()
    for number, (cut, cut_width, first, columns, group, target) in enumerate(segments):
        send_out, keep_out = outs[2 * group], outs[2 * group + 1]
        left = jnp.concatenate([keep[:, cut : cut + cut_width], recv[:, cut : cut + cut_width].astype(BF)], 0)
        half = cut_width // 2
        step = 512 if columns % 512 == 0 else 384
        for at in range(0, columns, step):
            cols = slice(first + at, first + at + step)
            right = jnp.concatenate([keep[:, cols], recv[:, cols].astype(BF)], 0)
            total = mm_tn(left, right)
            into = slice(target + at, target + at + step)
            if (group, target) in started:
                total += jnp.concatenate([send_out[:, into], keep_out[:, into]], 0)
            send_out[:, into] = total[:half]
            keep_out[:, into] = total[half:]
            if last_of[group, target] == number:
                send_out.flush(into.start, into.stop)
                keep_out.flush(into.start, into.stop)
        started.add((group, target))


def halve_kernel(kept, recv, send_out, keep_out):
    rows = send_out.shape[0]
    send_out[...] = kept[:rows] + recv[:rows]
    send_out.flush()
    keep_out[...] = kept[rows:] + recv[rows:]


SMEM = pl.BlockSpec(memory_space=pltpu.SMEM)
VMEM = pl.BlockSpec(memory_space=pltpu.VMEM)
ANY = pl.BlockSpec(memory_space=pl.ANY)


COST = {
    "enc_attn_fwd": 2.3, "dec_self_fwd": 2.5, "enc_mlp_fwd": 1.7, "cross_fwd": 4.2, "dec_mlp": 2.7,
    "cross_back": 20.0, "weights_c": 0.1, "enc_mlp_back": 3.0, "enc_attn_back": 0.3, "query_part": 20.0,
    "weights_f": 3.0, "weights_a": 0.1, "dec_self_back": 0.3, "weights_s": 1.0, "tail_parts": 3.0,
    "tail": 20.0, "gains": 1.0, "gain_rows": 1.0, "halve_m": 20.0, "halve_mo": 0.3,
    "halve_c": 0.1, "halve_f": 0.1, "halve_fo": 3.0, "halve_s": 8.0, "halve_a": 0.1,
    "finish_m": 0.3, "finish_mo": 3.0, "finish_c": 0.1, "finish_f": 0.1, "finish_fo": 1.0,
    "finish_s": 0.1, "finish_a": 8.0, "weights_m": 0.1,
}
VMEM_LIMIT = 8

LINE = (
    "pause", "enc_attn_0", "enc_attn_1", "dec_self", "pause", "enc_mlp_0", "enc_mlp_1", "pause",
    "cross_0", "cross_1", "pause", "dec_mlp", "tick", "w_m", "cross_back", "h_mo",
    "w_c", "enc_mlp_back", "h_m", "query_part", "tick", "w_f", "h_mo", "enc_attn_back",
    "h_c", "dec_self_back", "h_fo", "w_s", "gain_rows", "gains", "h_f", "h_mo",
    "h_m", "w_a", "h_c", "h_fo", "h_f", "h_m", "h_s", "h_c",
    "h_a", "h_f", "e_m", "tick", "tail_parts", "h_s", "h_a", "h_fo",
    "e_c", "h_s", "h_a", "e_f", "tail", "e_s", "e_a",
)
HALVINGS = {"m": "pxme", "mo": "xpme", "c": "xpme", "f": "pxme", "fo": "xpme", "s": "pxme", "a": "xpme"}
PARTS = {"m": 1, "c": 3, "f": 1, "a": 1, "s": 2}
TICK = 0.1
GAINS_WITH = "a"


class Stored:
    def __init__(self, ref):
        self.ref = ref
        self.shape, self.dtype = ref.shape, ref.dtype

    def __getitem__(self, at):
        return self.ref[at]

    def __setitem__(self, at, value):
        self.ref[at] = value

    def flush(self, first=0, last=None):
        pass


class Columns:
    def __init__(self, refs):
        self.refs = refs
        self.shape = (refs[0].shape[0], sum(ref.shape[1] for ref in refs))
        self.dtype = refs[0].dtype

    def __getitem__(self, at):
        rows, cols = at
        first, last = cols.start or 0, self.shape[1] if cols.stop is None else cols.stop
        pieces, start = [], 0
        for ref in self.refs:
            low, high = max(first - start, 0), min(last - start, ref.shape[1])
            if low < high:
                pieces.append(ref[rows, low:high])
            start += ref.shape[1]
        return pieces[0] if len(pieces) == 1 else jnp.concatenate(pieces, 1)

    def __setitem__(self, at, value):
        rows, cols = at
        first, last = cols.start or 0, self.shape[1] if cols.stop is None else cols.stop
        start = 0
        for ref in self.refs:
            low, high = max(first - start, 0), min(last - start, ref.shape[1])
            if low < high:
                ref[rows, low:high] = value[:, low + start - first : high + start - first]
            start += ref.shape[1]

    def flush(self, first=0, last=None):
        pass


class Stack:
    def __init__(self, *parts):
        self.parts = parts


class Rows:
    def __init__(self, refs, spans):
        self.refs = [ref.at[first:last] if (first, last) != (0, ref.shape[0]) else ref
                     for ref, (first, last) in zip(refs, spans)]
        self.heights = [last - first for first, last in spans]
        self.shape = (sum(self.heights),) + tuple(refs[0].shape[1:])
        self.dtype = refs[0].dtype

    def __getitem__(self, at):
        rows, cols = (slice(None), slice(None)) if at is Ellipsis else at
        first, last, _ = rows.indices(self.shape[0])
        pieces, start = [], 0
        for ref, height in zip(self.refs, self.heights):
            low, high = max(first - start, 0), min(last - start, height)
            if low < high:
                pieces.append(ref[low:high, cols])
            start += height
        return pieces[0] if len(pieces) == 1 else jnp.concatenate(pieces, 0)


def flush(*refs):
    for ref in refs:
        ref.flush()


class Line:
    def __init__(self):
        self.last = None

    def call(self, kernel, outs, args, name, scratch=(), cost=None):
        spans = [[part[1:] for part in a.parts] if isinstance(a, Stack) else None for a in args]
        args = [[part[0] for part in a.parts] if isinstance(a, Stack) else a for a in args]
        flat_args, args_tree = jax.tree.flatten(list(args))
        widths = [out if isinstance(out, list) else [out] for out in outs]
        shapes = [jax.ShapeDtypeStruct(*out) for group in widths for out in group]
        in_specs = [VMEM if a.ndim > 1 else SMEM for a in flat_args]
        count, made = len(flat_args), len(shapes)
        operands = list(flat_args)
        if self.last is not None:
            operands.append(self.last)
            in_specs.append(ANY)
        total = len(operands)

        def run(*refs):
            ins = jax.tree.unflatten(args_tree, refs[:count])
            ins = [Rows(i, span) if span else Columns(i) if isinstance(i, list) else i for i, span in zip(ins, spans)]
            left = list(refs[total : total + made])
            results = []
            for group, out in zip(widths, outs):
                taken, left = [Stored(ref) for ref in left[: len(group)]], left[len(group) :]
                results.append(Columns(taken) if isinstance(out, list) else taken[0])
            kernel(*ins, *results, *refs[total + made :])

        cost = COST.get(name, 0.3) if cost is None else cost
        flat = pl.pallas_call(
            run,
            out_shape=shapes,
            in_specs=in_specs,
            out_specs=[VMEM] * made,
            scratch_shapes=list(scratch),
            compiler_params=pltpu.CompilerParams(vmem_limit_bytes=VMEM_LIMIT * MIB),
            cost_estimate=pl.CostEstimate(
                flops=int(cost * 1.15e9), bytes_accessed=int(cost * 3.69e6), transcendentals=0
            ),
            name=name,
        )(*operands)
        self.last = min(flat, key=lambda r: r.size)
        results, left = [], list(flat)
        for group, out in zip(widths, outs):
            results.append(left[: len(group)] if isinstance(out, list) else left[0])
            left = left[len(group) :]
        return results


def join_kernel(kept, recv, out):
    out[...] = kept[...] + recv[...]


def middle_kernel(kept, recv, send_out, keep_out):
    rows = send_out.shape[0]
    me = lax.axis_index("dp")
    inner = ((me >> 2) ^ (me >> 3)) & 1
    send_out[...] = jnp.where(inner == 1, recv[rows:], kept[:rows])
    keep_out[...] = jnp.where(inner == 1, recv[:rows], kept[rows:])


def finish_kernel(pieces, *refs):
    groups = 1 + max(group for group, _ in pieces)
    outs = refs[2 * groups :]
    at = 0
    for group, firsts in pieces:
        kept, recv = refs[2 * group], refs[2 * group + 1]
        if firsts is None:
            total = kept[:, -128:] + recv[:, -128:]
            rows = total.shape[0]
            total = jnp.concatenate([total, jnp.zeros((128 - rows, 128), F32)], 0).T
            outs[at][...] = total[0:3, :rows]
            outs[at + 1][...] = total[3:6, :rows]
            at += 2
            continue
        out = outs[at]
        at += 1
        for i, first in enumerate(firsts):
            cols = slice(first, first + out.shape[-1])
            total = kept[:, cols] + recv[:, cols]
            if len(firsts) > 1:
                out[i] = total
            else:
                out[...] = total


def tick_kernel(source, target):
    target[...] = source[0:1, 0:128]


def pair_other(part, name):
    with jax.named_scope("pair_" + name):
        return lax.ppermute(part, "mp", [(0, 1), (1, 0)])


def swap(value, step, name):
    shards = lax.axis_size("dp")
    bit = {"x": 1, "p": 2, "e": 2}.get(step, step)
    if step == "m":
        pairs = [(i, i ^ 12) for i in range(shards) if (i >> 2 ^ i >> 3) & 1]
    else:
        pairs = [(i, i ^ (1 << bit)) for i in range(shards)]
    with jax.named_scope("swap_%s_%s" % (name, step)):
        return lax.ppermute(value, "dp", pairs)


def feature_order(features, steps):
    shards = lax.axis_size("dp")
    me = lax.axis_index("dp")
    block = features // shards
    column = jnp.arange(features, dtype=jnp.int32)
    place = column // block
    owner = jnp.zeros_like(column)
    other = {step: 1 - ((place >> (len(steps) - 1 - at)) & 1) for at, step in enumerate(steps)}
    near = (me >> 2) & 1
    for step in steps:
        if step == "p":
            owner = owner | ((near ^ other["p"]) << 3)
        elif step == "e":
            owner = owner | ((near ^ other["e"] ^ other["p"]) << 2)
        else:
            bit = 1 if step == "x" else step
            owner = owner | ((((me >> bit) & 1) ^ other[step]) << bit)
    source = owner * block + column % block
    return (jnp.arange(features, dtype=jnp.int32)[:, None] == source[None, :]).astype(BF)


class Halving:
    def __init__(self, sent, kept, steps, name):
        self.steps, self.name, self.at = steps, name, 0
        self.kept = kept
        self.flying = swap(sent, steps[0], name)

    def step(self, line):
        came, self.at = self.steps[self.at], self.at + 1
        rows, columns = self.kept.shape
        args, name = [self.kept, self.flying], "halve_" + self.name
        if self.steps[self.at] == "m":
            (self.kept,) = line.call(join_kernel, [((rows, columns), F32)], args, name)
            sent = self.kept
        else:
            shape = ((rows // 2, columns), F32)
            sent, self.kept = line.call(middle_kernel if came == "m" else halve_kernel, [shape, shape], args, name)
        self.flying = swap(sent, self.steps[self.at], self.name)

    def last(self):
        for bit in range(4, lax.axis_size("dp").bit_length() - 1):
            rows = self.kept.shape[0] // 2
            total = self.kept + self.flying
            self.kept, self.flying = total[rows:], swap(total[:rows], bit, self.name)
        return [self.kept, self.flying]


def finish(line, groups, pieces, name):
    args = [array for group in groups for array in group.last()]
    rows = args[0].shape[0]
    outs = []
    for _, firsts, width in pieces:
        if firsts is None:
            outs += [((3, rows), F32)] * 2
        else:
            outs.append((((len(firsts), rows, width) if len(firsts) > 1 else (rows, width)), F32))
    kernel = functools.partial(finish_kernel, [(group, firsts) for group, firsts, _ in pieces])
    return line.call(kernel, outs, args, "finish_" + name)


def body(
    enc_in, dec_in, cotangent, patch_counts, table_lengths, enc_qkv, enc_attn_out, enc_mlp_in, enc_mlp_out, enc_gains,
    dec_self_qkv, dec_self_out, dec_cross_qkv, dec_cross_out, dec_mlp_in, dec_mlp_out, dec_gains,
):
    plots, enc_len, features = enc_in.shape
    dec_len = dec_in.shape[1]
    enc_rows, dec_rows = plots * enc_len, plots * dec_len
    heads = enc_attn_out.shape[0]
    units = enc_mlp_out.shape[0]
    half = features // 2
    bits = lax.axis_size("dp").bit_length() - 1
    orders = {}

    def order_by(steps):
        cuts = (0,) + tuple(step for step in steps if step != "m") + tuple(range(4, bits))
        if cuts not in orders:
            orders[cuts] = feature_order(features, cuts)
        return orders[cuts]

    order_of = {name: order_by(steps) for name, steps in HALVINGS.items()}
    x0 = enc_in.reshape(enc_rows, features)
    y0 = dec_in.reshape(dec_rows, features)
    top = cotangent.reshape(dec_rows, features)
    enc_wide, dec_wide = ((enc_rows, features), F32), ((dec_rows, features), F32)
    enc_low, dec_low = ((enc_rows, features), BF), ((dec_rows, features), BF)
    gain_row, gain_rows = ((1, features), F32), ((2, features), F32)
    quarter = half // 2
    line = Line()

    def tick(cost=TICK):
        line.call(tick_kernel, [((1, 128), F32)], [enc_gains], "tick", cost=cost)

    def parts_of(name, rows, width):
        count, tiles = PARTS[name], width // 128
        edges = [128 * (tiles * i // count) for i in range(count + 1)]
        return [((rows, high - low), F32) for low, high in zip(edges, edges[1:])]

    def swap_cores(name, parts):
        return [swap(part, 0, name) for part in parts]

    def group(columns):
        return [((quarter, columns), F32)] * 2

    def mlp_of(name):
        apart = name + "o" in HALVINGS
        target = (1, 0) if apart else (0, 2 * units)
        segments = (
            (0, half, half, 2 * units, 0, 0),
            (half + 2 * units, half, 2 * half + 2 * units, units) + target,
        )
        return segments, group(2 * units) + group(units) if apart else group(3 * units)

    attn_segments = (
        (0, half, half, 3 * heads, 0, 0),
        (half + 3 * heads, half, 2 * half + 3 * heads, heads, 0, 3 * heads),
    )
    base, fold_width = 2 * half + 2 * heads, half + 2 * heads
    folds = enc_rows // dec_rows
    cross_segments = (
        (0, half, half, heads, 0, 0),
        (half + heads, half, 2 * half + heads, heads, 0, heads),
    ) + tuple(
        (base + f * fold_width, half, base + f * fold_width + half, 2 * heads, 0, 2 * heads) for f in range(folds)
    )
    attn_group = group(4 * heads)
    mlp_wide = 2 * half + 3 * units
    attn_wide = 2 * half + 4 * heads
    cross_wide = base + folds * fold_width
    v, sums, grad_of = {}, {}, {}

    def pause():
        tick(6.0)

    def enc_attn(p):
        v["part_e1", p], v["enc_saved", p] = line.call(
            functools.partial(self_fwd_kernel, False, enc_len, p),
            [((enc_len, features), F32), ((enc_len, 4 * heads), BF)],
            [patch_counts, x0, enc_gains, enc_qkv, enc_attn_out], "enc_attn_fwd",
        )
        v["other_e1", p] = pair_other(v["part_e1", p], "e1")

    def dec_self():
        v["part_d1"], v["dec_saved"] = line.call(
            functools.partial(self_fwd_kernel, True, dec_len, 0),
            [dec_wide, ((dec_rows, 4 * heads), BF)],
            [table_lengths, y0, dec_gains, dec_self_qkv, dec_self_out], "dec_self_fwd",
        )
        v["other_d1"] = pair_other(v["part_d1"], "d1")

    def enc_mlp(p):
        v["part_e2", p], v["x1", p], v["pre", p] = line.call(
            functools.partial(enc_mlp_fwd_kernel, p),
            [((enc_len, features), F32), ((enc_len, features), F32), ((enc_len, 2 * units), F32)],
            [x0, v["part_e1", p], v["other_e1", p], enc_gains, enc_mlp_in, enc_mlp_out], "enc_mlp_fwd",
        )
        v["other_e2", p] = pair_other(v["part_e2", p], "e2")

    def cross(p):
        v["part_d2", p], v["states", p], v["saved", p] = line.call(
            functools.partial(cross_fwd_kernel, enc_len, p),
            [((dec_len, features), F32), ((enc_len + dec_len, features), F32), ((enc_len + dec_len, 2 * heads), BF)],
            [patch_counts, v["x1", p], v["part_e2", p], v["other_e2", p], enc_gains, y0, v["part_d1"], v["other_d1"],
             dec_gains, dec_cross_qkv, dec_cross_out],
            "cross_fwd",
        )
        v["other_d2", p] = pair_other(v["part_d2", p], "d2")

    def stack(name, first, last):
        return Stack(*[(v[name, p], first, last) for p in range(plots)])

    def enc_part(name):
        return stack(name, 0, enc_len)

    def dec_part(name):
        return stack(name, enc_len, enc_len + dec_len)

    def dec_mlp():
        v["part_g3"], v["y2"], send, v["keep_m"] = line.call(
            dec_mlp_kernel,
            [dec_wide, dec_wide, parts_of("m", dec_rows, mlp_wide), ((dec_rows, mlp_wide), BF)],
            [dec_part("states"), stack("part_d2", 0, dec_len), stack("other_d2", 0, dec_len), dec_gains, top,
             dec_mlp_in, dec_mlp_out, order_of["m"], order_of.get("mo", order_of["m"])],
            "dec_mlp",
        )
        v["other_g3"] = pair_other(v["part_g3"], "g3")
        v["recv_m"] = swap_cores("m", send)

    def start_sums(name, products):
        for group_name, pair in zip((name, name + "o"), zip(products[::2], products[1::2])):
            sums[group_name] = Halving(pair[0], pair[1], HALVINGS[group_name], group_name)

    def mlp_weights(name, keep, recv):
        segments, groups = mlp_of(name)
        start_sums(
            name, line.call(functools.partial(weight_kernel, segments), groups, [keep, recv], "weights_" + name)
        )

    def dec_mlp_weights():
        mlp_weights("m", v["keep_m"], v["recv_m"])

    def cross_back():
        v["part_m"], v["g2"], v["gain_dec_cross"], send, v["keep_c"] = line.call(
            functools.partial(cross_back_kernel, enc_len),
            [enc_wide, dec_wide, gain_row, parts_of("c", dec_rows, cross_wide), ((dec_rows, cross_wide), BF)],
            [patch_counts, v["part_g3"], v["other_g3"], v["y2"], dec_gains, top, dec_cross_out, dec_part("saved"),
             enc_part("saved"), dec_cross_qkv, order_of["c"], dec_part("states"), enc_part("states"), enc_gains],
            "cross_back", scratch=[pltpu.VMEM((enc_rows, 2 * heads), BF)],
        )
        v["other_m"] = pair_other(v["part_m"], "m")
        v["recv_c"] = swap_cores("c", send)

    def cross_weights():
        start_sums("c", line.call(
            functools.partial(weight_kernel, cross_segments), attn_group, [v["keep_c"], v["recv_c"]], "weights_c"
        ))

    def enc_mlp_back():
        v["part_g1"], v["back2"], v["gain_enc_mlp"], send, v["keep_f"] = line.call(
            enc_mlp_back_kernel,
            [enc_wide, enc_wide, gain_row, parts_of("f", enc_rows, mlp_wide), ((enc_rows, mlp_wide), BF)],
            [v["part_m"], v["other_m"], enc_part("states"), enc_gains, enc_mlp_out, enc_part("pre"), enc_mlp_in,
             order_of["f"], order_of.get("fo", order_of["f"]), enc_part("x1")],
            "enc_mlp_back",
        )
        v["other_g1"] = pair_other(v["part_g1"], "g1")
        v["recv_f"] = swap_cores("f", send)

    def enc_mlp_weights():
        mlp_weights("f", v["keep_f"], v["recv_f"])

    def enc_attn_back():
        v["part_ge"], v["back1"], v["gain_enc_attn"], send, v["keep_a"] = line.call(
            functools.partial(self_back_kernel, False, enc_len),
            [enc_wide, enc_wide, gain_rows, parts_of("a", enc_rows, attn_wide), ((enc_rows, attn_wide), BF)],
            [patch_counts, v["part_g1"], v["other_g1"], enc_part("x1"), enc_gains, v["back2"], enc_attn_out,
             enc_part("enc_saved"), enc_qkv, order_of["a"], x0],
            "enc_attn_back",
        )
        v["recv_a"] = swap_cores("a", send)

    def query_part():
        (v["part_q"],) = line.call(query_part_kernel, [dec_wide], [v["keep_c"], dec_cross_qkv], "query_part")
        v["other_q"] = pair_other(v["part_q"], "q")

    def dec_self_back():
        v["part_g0"], v["g1"], v["gain_dec_self"], send, v["keep_s"] = line.call(
            functools.partial(self_back_kernel, True, dec_len),
            [dec_wide, dec_wide, gain_rows, parts_of("s", dec_rows, attn_wide), ((dec_rows, attn_wide), BF)],
            [table_lengths, v["part_q"], v["other_q"], dec_part("states"), dec_gains, v["g2"], dec_self_out,
             v["dec_saved"], dec_self_qkv, order_of["s"], y0],
            "dec_self_back",
        )
        v["recv_s"] = swap_cores("s", send)

    def tail_parts():
        (v["part_tail"],) = line.call(
            tail_parts_kernel, [((enc_rows + 2 * dec_rows, features), F32)],
            [v["part_ge"], v["part_g0"], v["keep_m"], dec_mlp_out], "tail_parts",
        )
        v["other_tail"] = pair_other(v["part_tail"], "tail")

    def tail():
        v["enc_out"], v["dec_out_grad"], v["dec_out"] = line.call(
            tail_kernel, [enc_low, dec_low, dec_low],
            [v["part_tail"], v["other_tail"], x0, enc_gains, v["back1"], y0, dec_gains, v["g1"], v["y2"]], "tail",
        )

    def collect_gains():
        (v["gain_rows"],) = line.call(
            gain_rows_kernel, [((8, features), F32)],
            [v["gain_enc_attn"], v["gain_enc_mlp"], v["gain_dec_self"], v["gain_dec_cross"]], "gain_rows",
        )
        v["other_rows"] = pair_other(v["gain_rows"], "gains")

    def gains():
        send, v["keep_g"] = line.call(
            gains_kernel, [((half, 128), F32), ((half, 128), F32)],
            [v["gain_rows"], v["other_rows"], order_of[GAINS_WITH]], "gains",
        )
        v["recv_g"] = swap(send, 0, "g")

    def attn_weights(name):
        if name == GAINS_WITH:
            products = line.call(
                functools.partial(gains_weight_kernel, attn_segments), group(4 * heads + 128),
                [v["keep_" + name], v["recv_" + name], v["keep_g"], v["recv_g"]], "weights_" + name,
            )
        else:
            products = line.call(
                functools.partial(weight_kernel, attn_segments), attn_group,
                [v["keep_" + name], v["recv_" + name]], "weights_" + name,
            )
        start_sums(name, products)

    attn_pieces = ((0, (0, heads, 2 * heads), heads), (0, (3 * heads,), heads))
    ends = {"c": ((0, (0, 2 * heads, 3 * heads), heads), (0, (heads,), heads)), "a": attn_pieces, "s": attn_pieces}
    for name in ("m", "f"):
        outer = (1, (0,), units) if name + "o" in HALVINGS else (0, (2 * units,), units)
        ends[name] = ((0, (0, units), units), outer)
    ends[GAINS_WITH] += ((0, None, 0),)
    stages = {
        "tick": tick, "pause": pause, "dec_self": dec_self, "dec_mlp": dec_mlp, "w_m": dec_mlp_weights,
        "cross_back": cross_back, "w_c": cross_weights, "enc_mlp_back": enc_mlp_back,
        "w_f": enc_mlp_weights, "enc_attn_back": enc_attn_back, "query_part": query_part, "gains": gains, "gain_rows": collect_gains,
        "tail_parts": tail_parts, "tail": tail,
        "w_a": functools.partial(attn_weights, "a"), "dec_self_back": dec_self_back,
        "w_s": functools.partial(attn_weights, "s"),
    }
    for name, stage in (("enc_attn", enc_attn), ("enc_mlp", enc_mlp), ("cross", cross)):
        for p in range(plots):
            stages["%s_%d" % (name, p)] = functools.partial(stage, p)
    for stage in LINE:
        kind, _, name = stage.partition("_")
        if stage in stages:
            stages[stage]()
        elif kind == "h":
            sums[name].step(line)
        else:
            groups = [sums[part] for part in (name, name + "o") if part in sums]
            grad_of[name] = finish(line, groups, ends[name], name)
    gains_out = grad_of[GAINS_WITH][2:]
    grads = (
        grad_of["a"][0], grad_of["a"][1].T, grad_of["f"][0], grad_of["f"][1].T, gains_out[0],
        grad_of["s"][0], grad_of["s"][1].T, grad_of["c"][0], grad_of["c"][1].T, grad_of["m"][0], grad_of["m"][1].T,
        gains_out[1],
    )
    return (
        v["dec_out"].reshape(cotangent.shape),
        v["enc_out"].reshape(enc_in.shape),
        v["dec_out_grad"].reshape(dec_in.shape),
    ) + grads


def solution(mesh):
    rows = P("dp", None, None)
    inner, outer = P(None, None, "mp"), P("mp", None)
    enc = (inner, outer, inner, outer, P())
    dec = (inner, outer, inner, outer, inner, outer, P())
    inner_grad, outer_grad, gain_grad = P(None, "dp", "mp"), P("mp", "dp"), P(None, "dp")
    return jax.shard_map(
        body,
        mesh=mesh,
        in_specs=(rows, rows, rows, P("dp"), P("dp")) + enc + dec,
        out_specs=(rows, rows, rows)
        + (inner_grad, outer_grad) * 2 + (gain_grad,)
        + (inner_grad, outer_grad) * 3 + (gain_grad,),
        check_vma=False,
    )
```

```python
import functools

import jax
import jax.numpy as jnp
from jax import lax
from jax.experimental import pallas as pl
from jax.experimental.pallas import tpu as pltpu
from jax.sharding import PartitionSpec as P

HEAD_DIM = 64
PAIR = 2 * HEAD_DIM
EPSILON = 1e-06
NEG_LARGE = -1e30
SCALE = HEAD_DIM ** (-0.5)
BF = jnp.bfloat16
F32 = jnp.float32
MIB = 1024 * 1024


def mm(left, right):
    return jnp.dot(left, right, preferred_element_type=F32)


def mm_nt(left, right):
    return lax.dot_general(left, right, (((1,), (1,)), ((), ())), preferred_element_type=F32)


def mm_tn(left, right):
    return lax.dot_general(left, right, (((0,), (0,)), ((), ())), preferred_element_type=F32)


def scaled(hidden):
    return hidden * lax.rsqrt(jnp.mean(hidden * hidden, -1, keepdims=True) + EPSILON)


def norm(hidden, gain):
    return (scaled(hidden) * gain).astype(BF)


def norm_back(grad, hidden, gain):
    scaling = lax.rsqrt(jnp.mean(hidden * hidden, -1, keepdims=True) + EPSILON)
    normed = hidden * scaling
    grad_hat = grad * gain
    return scaling * (grad_hat - normed * jnp.mean(grad_hat * normed, -1, keepdims=True)), normed


def gain_part(part, normed):
    return jnp.sum(part * normed, 0, keepdims=True)


def gelu_parts(gate):
    slope = 0.7978845608028654
    square = gate * gate
    bent = jnp.tanh(slope * gate * (1.0 + 0.044715 * square))
    half = 0.5 * (1.0 + bent)
    value = gate * half
    rise = half + 0.5 * gate * (1.0 - bent * bent) * slope * (1.0 + 0.134145 * square)
    return value, rise


def stack_heads(pair):
    lane = lax.broadcasted_iota(jnp.int32, pair.shape, 1)
    zero = jnp.zeros_like(pair)
    return jnp.concatenate(
        [jnp.where(lane < HEAD_DIM, pair, zero), jnp.where(lane < HEAD_DIM, zero, pair)], 0
    )


def merge_heads(stacked):
    rows = stacked.shape[0] // 2
    lane = lax.broadcasted_iota(jnp.int32, (rows, PAIR), 1)
    return jnp.where(lane < HEAD_DIM, stacked[:rows], stacked[rows:])


def soft_of(stacked_query, keys, bias):
    scores = mm_nt(stacked_query, keys) * SCALE + bias
    expon = jnp.exp(scores - jnp.max(scores, -1, keepdims=True))
    return expon / jnp.sum(expon, -1, keepdims=True)


def pair_fwd(query, keys, values, bias):
    soft = soft_of(stack_heads(query), keys, bias)
    return merge_heads(mm(soft.astype(BF), values)).astype(BF)


def pair_back(query, keys, values, grad_out, bias):
    queries = stack_heads(query)
    soft = soft_of(queries, keys, bias)
    grads = stack_heads(grad_out)
    grad_values = mm_tn(soft.astype(BF), grads)
    grad_soft = mm_nt(grads, values)
    grad_scores = (
        soft * (grad_soft - jnp.sum(soft * grad_soft, -1, keepdims=True))
    ).astype(BF)
    grad_query = merge_heads(mm(grad_scores, keys)) * SCALE
    grad_keys = mm_tn(grad_scores, queries) * SCALE
    return grad_query.astype(BF), grad_keys.astype(BF), grad_values.astype(BF)


def length_bias(count, rows, length):
    col = lax.broadcasted_iota(jnp.int32, (2 * rows, length), 1)
    return jnp.where(col < count, 0.0, NEG_LARGE).astype(F32)


def causal_bias(counts, plots, length):
    shape = (plots * length, plots * length)
    row = lax.broadcasted_iota(jnp.int32, shape, 0)
    col = lax.broadcasted_iota(jnp.int32, shape, 1)
    bias = jnp.full(shape, NEG_LARGE, F32)
    for plot in range(plots):
        low = plot * length
        inside = (row >= low) & (row < low + length) & (col >= low)
        inside = inside & (col <= row) & (col < low + counts[plot])
        bias = jnp.where(inside, 0.0, bias)
    return jnp.concatenate([bias, bias], 0)


def pairs_of(width):
    return [slice(at, at + PAIR) for at in range(0, width, PAIR)]


def put(ref, at, value):
    last = at + value.shape[1]
    ref[:, at:last] = value.astype(ref.dtype)
    ref.flush(at, last)
    return last


def put_both(send, keep, at, value):
    put(send, at, value)
    return put(keep, at, value)


def put_cut(send, keep, at, value, order):
    ordered = mm(value, order[...])
    half = ordered.shape[1] // 2
    put(send, at, ordered[:, :half])
    return put(keep, at, ordered[:, half:])


def keys_of(causal, length, rows, counts, first=0):
    plots = rows // length
    if causal:
        return [(slice(0, rows), causal_bias(counts, plots, length))]
    return [
        (slice(p * length, (p + 1) * length), length_bias(counts[first + p], length, length)) for p in range(plots)
    ]


def self_fwd_kernel(causal, length, first, counts, state, gain, stacked, outer, part, saved):
    rows, width = part.shape[0], outer.shape[0]
    normed = norm(state[first * length : first * length + rows, :].astype(F32), gain[0:1, :])
    for which in range(3):
        put(saved, which * width, mm(normed, stacked[which]))
    for span, bias in keys_of(causal, length, rows, counts, first):
        for cols in pairs_of(width):
            mixed = slice(3 * width + cols.start, 3 * width + cols.stop)
            saved[span, mixed] = pair_fwd(
                saved[span, cols],
                saved[span, width + cols.start : width + cols.stop],
                saved[span, 2 * width + cols.start : 2 * width + cols.stop],
                bias,
            )
    part[...] = mm(saved[:, 3 * width :], outer[...])


def enc_mlp_fwd_kernel(first, state, own, other, gain, inner, outer, part, state_ref, pre):
    rows, width = part.shape[0], outer.shape[0]
    full = state[first * rows : (first + 1) * rows, :].astype(F32) + own[...] + other[...]
    state_ref[...] = full
    normed = norm(full, gain[1:2, :])
    step = 256
    total = None
    for at in range(0, width, step):
        cols = slice(at, at + step)
        gate = mm(normed, inner[0, :, cols])
        up = mm(normed, inner[1, :, cols])
        value, _ = gelu_parts(gate)
        pre[:, cols] = gate
        pre[:, width + at : width + at + step] = up
        add = mm((value * up).astype(BF), outer[cols, :])
        total = add if total is None else total + add
    part[...] = total


def cross_fwd_kernel(
    length, first, counts, enc_state, enc_own, enc_other, enc_gain, dec_state, dec_own, dec_other, dec_gain, stacked,
    outer, part, states, saved,
):
    rows, width = part.shape[0], outer.shape[0]
    span = slice(first * rows, (first + 1) * rows)
    dec_full = dec_state[span, :].astype(F32) + dec_own[span, :] + dec_other[span, :]
    states[length:, :] = dec_full
    normed = norm(dec_full, dec_gain[1:2, :])
    saved[length:, :width] = mm(normed, stacked[0]).astype(BF)
    enc_full = enc_state[...] + enc_own[...] + enc_other[...]
    states[:length, :] = enc_full
    memory = norm(enc_full, enc_gain[2:3, :])
    saved[:length, :width] = mm(memory, stacked[1]).astype(BF)
    saved[:length, width:] = mm(memory, stacked[2]).astype(BF)
    bias = length_bias(counts[first], rows, length)
    for cols in pairs_of(width):
        beside = slice(width + cols.start, width + cols.stop)
        saved[length:, beside] = pair_fwd(saved[length:, cols], saved[:length, cols], saved[:length, beside], bias)
    part[...] = mm(saved[length:, width:], outer[...])


def dec_mlp_kernel(
    state, own, other, gain, cotangent, inner, outer, order, order_outer, part, state_ref, send, keep
):
    full = state[...] + own[...] + other[...]
    state_ref[...] = full
    state_ref.flush()
    normed = norm(full, gain[2:3, :])
    low = cotangent[...]
    width, half = outer.shape[0], order.shape[0] // 2
    step = 256
    for col in range(0, width, step):
        cols = slice(col, col + step)
        gate = mm(normed, inner[0, :, cols])
        up = mm(normed, inner[1, :, cols])
        value, rise = gelu_parts(gate)
        grad_hidden = mm_nt(low, outer[cols, :])
        put_both(send, keep, half + col, (grad_hidden * up * rise).astype(BF))
        put_both(send, keep, half + width + col, (grad_hidden * value).astype(BF))
        put_both(send, keep, 2 * half + 2 * width + col, (value * up).astype(BF))
    part[...] = mm_nt(keep[:, half : half + width], inner[0]) + mm_nt(
        keep[:, half + width : half + 2 * width], inner[1]
    )
    part.flush()
    put_cut(send, keep, 0, normed, order)
    put_cut(send, keep, half + 2 * width, low, order_outer)


def tail_parts_kernel(enc_part, dec_part, keep, outer, part):
    enc_rows, dec_rows = enc_part.shape[0], dec_part.shape[0]
    part[:enc_rows, :] = enc_part[...]
    part[enc_rows : enc_rows + dec_rows, :] = dec_part[...]
    part[enc_rows + dec_rows :, :] = mm(keep[:, keep.shape[1] - outer.shape[0] :], outer[...])


def tail_kernel(own, other, enc_state, enc_gain, enc_grad, dec_state, dec_gain, dec_grad, state, enc_out, dec_out, out):
    enc_rows, dec_rows = enc_out.shape[0], dec_out.shape[0]
    span = slice(0, enc_rows)
    grad_in, _ = norm_back(own[span, :] + other[span, :], enc_state[...].astype(F32), enc_gain[0:1, :])
    enc_out[...] = (enc_grad[...] + grad_in).astype(BF)
    span = slice(enc_rows, enc_rows + dec_rows)
    grad_in, _ = norm_back(own[span, :] + other[span, :], dec_state[...].astype(F32), dec_gain[0:1, :])
    dec_out[...] = (dec_grad[...] + grad_in).astype(BF)
    span = slice(enc_rows + dec_rows, enc_rows + 2 * dec_rows)
    out[...] = (state[...] + own[span, :] + other[span, :]).astype(BF)


def query_part_kernel(keep, stacked, part):
    half = stacked.shape[1] // 2
    part[...] = mm_nt(keep[:, half : half + stacked.shape[2]], stacked[0])


def cross_back_kernel(
    length, counts, own, other, state, gain, grad, outer, query, kv, stacked, order, dec_state, enc_state, enc_gain,
    part, grad_ref, gain_ref, send, keep, key_grads,
):
    grad_in, normed = norm_back(own[...] + other[...], state[...], gain[2:3, :])
    gain_ref[...] = gain_part(own[...], normed)
    full = grad[...].astype(F32) + grad_in
    grad_ref[...] = full
    flush(gain_ref, grad_ref)
    low = full.astype(BF)
    width, half = outer.shape[0], order.shape[0] // 2
    grad_mixed = mm_nt(low, outer[...]).astype(BF)
    plots = kv.shape[0] // length
    rows = low.shape[0] // plots
    for plot in range(plots):
        bias = length_bias(counts[plot], rows, length)
        q_span = slice(plot * rows, (plot + 1) * rows)
        k_span = slice(plot * length, (plot + 1) * length)
        for cols in pairs_of(width):
            values = slice(width + cols.start, width + cols.stop)
            grad_query, grad_keys, grad_values = pair_back(
                query[q_span, cols], kv[k_span, cols], kv[k_span, values], grad_mixed[q_span, cols], bias
            )
            keep[q_span, half + cols.start : half + cols.stop] = grad_query
            send[q_span, half + cols.start : half + cols.stop] = grad_query.astype(F32)
            key_grads[k_span, cols] = grad_keys
            key_grads[k_span, values] = grad_values
    send.flush(half, half + width)
    keep.flush(half, half + width)
    part[...] = mm_nt(key_grads[:, :width], stacked[1]) + mm_nt(key_grads[:, width:], stacked[2])
    part.flush()
    put_cut(send, keep, 0, norm(dec_state[...], gain[1:2, :]), order)
    at = put_cut(send, keep, half + width, low, order)
    base = put_both(send, keep, at, query[:, width : 2 * width])
    ordered = mm(norm(enc_state[...], enc_gain[2:3, :]), order[...])
    for fold in range(kv.shape[0] // low.shape[0]):
        span = slice(fold * low.shape[0], (fold + 1) * low.shape[0])
        put(send, base, ordered[span, :half])
        put(keep, base, ordered[span, half:])
        base = put_both(send, keep, base + half, key_grads[span, :])


def self_back_kernel(
    causal, length, counts, own, other, state, gain, grad, outer, qkv, stacked, order, inputs,
    part, grad_ref, gain_ref, send, keep,
):
    grad_in, normed = norm_back(own[...] + other[...], state[...], gain[1:2, :])
    gain_ref[0:1, :] = gain_part(own[...], normed)
    full = grad[...] + grad_in
    grad_ref[...] = full
    flush(gain_ref, grad_ref)
    low = full.astype(BF)
    width, half = outer.shape[0], order.shape[0] // 2
    grad_mixed = mm_nt(low, outer[...]).astype(BF)
    for span, bias in keys_of(causal, length, low.shape[0], counts):
        for cols in pairs_of(width):
            grads = pair_back(
                qkv[span, cols],
                qkv[span, width + cols.start : width + cols.stop],
                qkv[span, 2 * width + cols.start : 2 * width + cols.stop],
                grad_mixed[span, cols],
                bias,
            )
            for which, piece in enumerate(grads):
                start = half + which * width + cols.start
                keep[span, start : start + PAIR] = piece
                send[span, start : start + PAIR] = piece.astype(F32)
    send.flush(half, half + 3 * width)
    keep.flush(half, half + 3 * width)
    total = mm_nt(keep[:, half : half + width], stacked[0])
    total += mm_nt(keep[:, half + width : half + 2 * width], stacked[1])
    total += mm_nt(keep[:, half + 2 * width : half + 3 * width], stacked[2])
    part[...] = total
    normed = scaled(inputs[...].astype(F32))
    gain_ref[1:2, :] = gain_part(total, normed)
    put_cut(send, keep, 0, (normed * gain[0:1, :]).astype(BF), order)
    at = put_cut(send, keep, half + 3 * width, low, order)
    put_both(send, keep, at, qkv[:, 3 * width : 4 * width])


def enc_mlp_back_kernel(
    own, other, state, gain, outer, pre, inner, order, order_outer, middle,
    part, grad_ref, gain_ref, send, keep,
):
    full, normed = norm_back(own[...] + other[...], state[...], gain[2:3, :])
    gain_ref[...] = gain_part(own[...], normed)
    grad_ref[...] = full
    flush(gain_ref, grad_ref)
    low = full.astype(BF)
    width, half = outer.shape[0], order.shape[0] // 2
    step = 256
    for col in range(0, width, step):
        cols = slice(col, col + step)
        value, rise = gelu_parts(pre[:, cols])
        up = pre[:, width + col : width + col + step]
        grad_hidden = mm_nt(low, outer[cols, :])
        put_both(send, keep, half + col, (grad_hidden * up * rise).astype(BF))
        put_both(send, keep, half + width + col, (grad_hidden * value).astype(BF))
        put_both(send, keep, 2 * half + 2 * width + col, (value * up).astype(BF))
    part[...] = mm_nt(keep[:, half : half + width], inner[0]) + mm_nt(
        keep[:, half + width : half + 2 * width], inner[1]
    )
    part.flush()
    put_cut(send, keep, 0, norm(middle[...], gain[1:2, :]), order)
    put_cut(send, keep, half + 2 * width, low, order_outer)


def gain_rows_kernel(enc_attn, enc_mlp, dec_self, dec_cross, out):
    for at, row in enumerate((enc_attn[1:2, :], enc_attn[0:1, :], enc_mlp[...], dec_self[1:2, :], dec_self[0:1, :],
                              dec_cross[...])):
        out[at : at + 1, :] = row
    out[6:8, :] = jnp.zeros((2, out.shape[1]), F32)


def gains_kernel(own, other, order, send, keep):
    rest = own[...] + other[...]
    rest = jnp.concatenate([rest, jnp.zeros((128 - rest.shape[0], rest.shape[1]), F32)], 0)
    total = None
    for _ in range(3):
        low = rest.astype(BF)
        rest = rest - low.astype(F32)
        moved = lax.dot_general(order[...], low, (((0,), (1,)), ((), ())), preferred_element_type=F32)
        total = moved if total is None else total + moved
    half = total.shape[0] // 2
    send[...] = total[:half]
    keep[...] = total[half:]


def gains_weight_kernel(segments, keep, recv, gains, other_gains, send_out, keep_out):
    weight_kernel(segments, keep, recv, send_out, keep_out)
    total = gains[...] + other_gains[...]
    half, first = send_out.shape[0], send_out.shape[1] - total.shape[1]
    send_out[:, first:] = total[:half]
    keep_out[:, first:] = total[half:]


def weight_kernel(segments, keep, recv, *outs):
    last_of = {(group, target): at for at, (_, _, _, _, group, target) in enumerate(segments)}
    started = set()
    for number, (cut, cut_width, first, columns, group, target) in enumerate(segments):
        send_out, keep_out = outs[2 * group], outs[2 * group + 1]
        left = jnp.concatenate([keep[:, cut : cut + cut_width], recv[:, cut : cut + cut_width].astype(BF)], 0)
        half = cut_width // 2
        step = 512 if columns % 512 == 0 else 384
        for at in range(0, columns, step):
            cols = slice(first + at, first + at + step)
            right = jnp.concatenate([keep[:, cols], recv[:, cols].astype(BF)], 0)
            total = mm_tn(left, right)
            into = slice(target + at, target + at + step)
            if (group, target) in started:
                total += jnp.concatenate([send_out[:, into], keep_out[:, into]], 0)
            send_out[:, into] = total[:half]
            keep_out[:, into] = total[half:]
            if last_of[group, target] == number:
                send_out.flush(into.start, into.stop)
                keep_out.flush(into.start, into.stop)
        started.add((group, target))


def halve_kernel(kept, recv, send_out, keep_out):
    rows = send_out.shape[0]
    send_out[...] = kept[:rows] + recv[:rows]
    send_out.flush()
    keep_out[...] = kept[rows:] + recv[rows:]


SMEM = pl.BlockSpec(memory_space=pltpu.SMEM)
VMEM = pl.BlockSpec(memory_space=pltpu.VMEM)
ANY = pl.BlockSpec(memory_space=pl.ANY)


COST = {
    "enc_attn_fwd": 2.3, "dec_self_fwd": 2.5, "enc_mlp_fwd": 1.7, "cross_fwd": 4.2, "dec_mlp": 2.7,
    "cross_back": 20.0, "weights_c": 0.1, "enc_mlp_back": 3.0, "enc_attn_back": 0.3, "query_part": 20.0,
    "weights_f": 3.0, "weights_a": 0.1, "dec_self_back": 0.3, "weights_s": 1.0, "tail_parts": 3.0,
    "tail": 20.0, "gains": 1.0, "gain_rows": 1.0, "halve_m": 20.0, "halve_mo": 0.3,
    "halve_c": 0.1, "halve_f": 0.1, "halve_fo": 3.0, "halve_s": 8.0, "halve_a": 0.1,
    "finish_m": 0.3, "finish_mo": 3.0, "finish_c": 0.1, "finish_f": 0.1, "finish_fo": 1.0,
    "finish_s": 0.1, "finish_a": 8.0, "weights_m": 0.1,
}
VMEM_LIMIT = 8

LINE = (
    "pause", "enc_attn_0", "enc_attn_1", "dec_self", "pause", "enc_mlp_0", "enc_mlp_1", "pause",
    "cross_0", "cross_1", "pause", "dec_mlp", "tick", "w_m", "cross_back", "h_mo",
    "w_c", "enc_mlp_back", "h_m", "query_part", "tick", "w_f", "h_mo", "enc_attn_back",
    "h_c", "dec_self_back", "h_fo", "w_s", "gain_rows", "gains", "h_f", "h_mo",
    "h_m", "w_a", "h_c", "h_fo", "h_f", "h_m", "h_s", "h_c",
    "h_a", "h_f", "e_m", "tick", "tail_parts", "h_s", "h_a", "h_fo",
    "e_c", "h_s", "h_a", "e_f", "tail", "e_s", "pause", "e_a",
)
HALVINGS = {"m": "pxme", "mo": "xpme", "c": "xpme", "f": "pxme", "fo": "xpme", "s": "pxme", "a": "xpme"}
PARTS = {"m": 1, "c": 3, "f": 1, "a": 1, "s": 2}
TICK = 0.1
GAINS_WITH = "a"


class Stored:
    def __init__(self, ref):
        self.ref = ref
        self.shape, self.dtype = ref.shape, ref.dtype

    def __getitem__(self, at):
        return self.ref[at]

    def __setitem__(self, at, value):
        self.ref[at] = value

    def flush(self, first=0, last=None):
        pass


class Columns:
    def __init__(self, refs):
        self.refs = refs
        self.shape = (refs[0].shape[0], sum(ref.shape[1] for ref in refs))
        self.dtype = refs[0].dtype

    def __getitem__(self, at):
        rows, cols = at
        first, last = cols.start or 0, self.shape[1] if cols.stop is None else cols.stop
        pieces, start = [], 0
        for ref in self.refs:
            low, high = max(first - start, 0), min(last - start, ref.shape[1])
            if low < high:
                pieces.append(ref[rows, low:high])
            start += ref.shape[1]
        return pieces[0] if len(pieces) == 1 else jnp.concatenate(pieces, 1)

    def __setitem__(self, at, value):
        rows, cols = at
        first, last = cols.start or 0, self.shape[1] if cols.stop is None else cols.stop
        start = 0
        for ref in self.refs:
            low, high = max(first - start, 0), min(last - start, ref.shape[1])
            if low < high:
                ref[rows, low:high] = value[:, low + start - first : high + start - first]
            start += ref.shape[1]

    def flush(self, first=0, last=None):
        pass


class Stack:
    def __init__(self, *parts):
        self.parts = parts


class Rows:
    def __init__(self, refs, spans):
        self.refs = [ref.at[first:last] if (first, last) != (0, ref.shape[0]) else ref
                     for ref, (first, last) in zip(refs, spans)]
        self.heights = [last - first for first, last in spans]
        self.shape = (sum(self.heights),) + tuple(refs[0].shape[1:])
        self.dtype = refs[0].dtype

    def __getitem__(self, at):
        rows, cols = (slice(None), slice(None)) if at is Ellipsis else at
        first, last, _ = rows.indices(self.shape[0])
        pieces, start = [], 0
        for ref, height in zip(self.refs, self.heights):
            low, high = max(first - start, 0), min(last - start, height)
            if low < high:
                pieces.append(ref[low:high, cols])
            start += height
        return pieces[0] if len(pieces) == 1 else jnp.concatenate(pieces, 0)


def flush(*refs):
    for ref in refs:
        ref.flush()


class Line:
    def __init__(self):
        self.last = None

    def call(self, kernel, outs, args, name, scratch=(), cost=None):
        spans = [[part[1:] for part in a.parts] if isinstance(a, Stack) else None for a in args]
        args = [[part[0] for part in a.parts] if isinstance(a, Stack) else a for a in args]
        flat_args, args_tree = jax.tree.flatten(list(args))
        widths = [out if isinstance(out, list) else [out] for out in outs]
        shapes = [jax.ShapeDtypeStruct(*out) for group in widths for out in group]
        in_specs = [VMEM if a.ndim > 1 else SMEM for a in flat_args]
        count, made = len(flat_args), len(shapes)
        operands = list(flat_args)
        if self.last is not None:
            operands.append(self.last)
            in_specs.append(ANY)
        total = len(operands)

        def run(*refs):
            ins = jax.tree.unflatten(args_tree, refs[:count])
            ins = [Rows(i, span) if span else Columns(i) if isinstance(i, list) else i for i, span in zip(ins, spans)]
            left = list(refs[total : total + made])
            results = []
            for group, out in zip(widths, outs):
                taken, left = [Stored(ref) for ref in left[: len(group)]], left[len(group) :]
                results.append(Columns(taken) if isinstance(out, list) else taken[0])
            kernel(*ins, *results, *refs[total + made :])

        cost = COST.get(name, 0.3) if cost is None else cost
        flat = pl.pallas_call(
            run,
            out_shape=shapes,
            in_specs=in_specs,
            out_specs=[VMEM] * made,
            scratch_shapes=list(scratch),
            compiler_params=pltpu.CompilerParams(vmem_limit_bytes=VMEM_LIMIT * MIB),
            cost_estimate=pl.CostEstimate(
                flops=int(cost * 1.15e9), bytes_accessed=int(cost * 3.69e6), transcendentals=0
            ),
            name=name,
        )(*operands)
        self.last = min(flat, key=lambda r: r.size)
        results, left = [], list(flat)
        for group, out in zip(widths, outs):
            results.append(left[: len(group)] if isinstance(out, list) else left[0])
            left = left[len(group) :]
        return results


def join_kernel(kept, recv, out):
    out[...] = kept[...] + recv[...]


def middle_kernel(kept, recv, send_out, keep_out):
    rows = send_out.shape[0]
    me = lax.axis_index("dp")
    inner = ((me >> 2) ^ (me >> 3)) & 1
    send_out[...] = jnp.where(inner == 1, recv[rows:], kept[:rows])
    keep_out[...] = jnp.where(inner == 1, recv[:rows], kept[rows:])


def finish_kernel(pieces, *refs):
    groups = 1 + max(group for group, _ in pieces)
    outs = refs[2 * groups :]
    at = 0
    for group, firsts in pieces:
        kept, recv = refs[2 * group], refs[2 * group + 1]
        if firsts is None:
            total = kept[:, -128:] + recv[:, -128:]
            rows = total.shape[0]
            total = jnp.concatenate([total, jnp.zeros((128 - rows, 128), F32)], 0).T
            outs[at][...] = total[0:3, :rows]
            outs[at + 1][...] = total[3:6, :rows]
            at += 2
            continue
        out = outs[at]
        at += 1
        for i, first in enumerate(firsts):
            cols = slice(first, first + out.shape[-1])
            total = kept[:, cols] + recv[:, cols]
            if len(firsts) > 1:
                out[i] = total
            else:
                out[...] = total


def tick_kernel(source, target):
    target[...] = source[0:1, 0:128]


def pair_other(part, name):
    with jax.named_scope("pair_" + name):
        return lax.ppermute(part, "mp", [(0, 1), (1, 0)])


def swap(value, step, name):
    shards = lax.axis_size("dp")
    bit = {"x": 1, "p": 2, "e": 2}.get(step, step)
    if step == "m":
        pairs = [(i, i ^ 12) for i in range(shards) if (i >> 2 ^ i >> 3) & 1]
    else:
        pairs = [(i, i ^ (1 << bit)) for i in range(shards)]
    with jax.named_scope("swap_%s_%s" % (name, step)):
        return lax.ppermute(value, "dp", pairs)


def feature_order(features, steps):
    shards = lax.axis_size("dp")
    me = lax.axis_index("dp")
    block = features // shards
    column = jnp.arange(features, dtype=jnp.int32)
    place = column // block
    owner = jnp.zeros_like(column)
    other = {step: 1 - ((place >> (len(steps) - 1 - at)) & 1) for at, step in enumerate(steps)}
    near = (me >> 2) & 1
    for step in steps:
        if step == "p":
            owner = owner | ((near ^ other["p"]) << 3)
        elif step == "e":
            owner = owner | ((near ^ other["e"] ^ other["p"]) << 2)
        else:
            bit = 1 if step == "x" else step
            owner = owner | ((((me >> bit) & 1) ^ other[step]) << bit)
    source = owner * block + column % block
    return (jnp.arange(features, dtype=jnp.int32)[:, None] == source[None, :]).astype(BF)


class Halving:
    def __init__(self, sent, kept, steps, name):
        self.steps, self.name, self.at = steps, name, 0
        self.kept = kept
        self.flying = swap(sent, steps[0], name)

    def step(self, line):
        came, self.at = self.steps[self.at], self.at + 1
        rows, columns = self.kept.shape
        args, name = [self.kept, self.flying], "halve_" + self.name
        if self.steps[self.at] == "m":
            (self.kept,) = line.call(join_kernel, [((rows, columns), F32)], args, name)
            sent = self.kept
        else:
            shape = ((rows // 2, columns), F32)
            sent, self.kept = line.call(middle_kernel if came == "m" else halve_kernel, [shape, shape], args, name)
        self.flying = swap(sent, self.steps[self.at], self.name)

    def last(self):
        for bit in range(4, lax.axis_size("dp").bit_length() - 1):
            rows = self.kept.shape[0] // 2
            total = self.kept + self.flying
            self.kept, self.flying = total[rows:], swap(total[:rows], bit, self.name)
        return [self.kept, self.flying]


def finish(line, groups, pieces, name):
    args = [array for group in groups for array in group.last()]
    rows = args[0].shape[0]
    outs = []
    for _, firsts, width in pieces:
        if firsts is None:
            outs += [((3, rows), F32)] * 2
        else:
            outs.append((((len(firsts), rows, width) if len(firsts) > 1 else (rows, width)), F32))
    kernel = functools.partial(finish_kernel, [(group, firsts) for group, firsts, _ in pieces])
    return line.call(kernel, outs, args, "finish_" + name)


def body(
    enc_in, dec_in, cotangent, patch_counts, table_lengths, enc_qkv, enc_attn_out, enc_mlp_in, enc_mlp_out, enc_gains,
    dec_self_qkv, dec_self_out, dec_cross_qkv, dec_cross_out, dec_mlp_in, dec_mlp_out, dec_gains,
):
    plots, enc_len, features = enc_in.shape
    dec_len = dec_in.shape[1]
    enc_rows, dec_rows = plots * enc_len, plots * dec_len
    heads = enc_attn_out.shape[0]
    units = enc_mlp_out.shape[0]
    half = features // 2
    bits = lax.axis_size("dp").bit_length() - 1
    orders = {}

    def order_by(steps):
        cuts = (0,) + tuple(step for step in steps if step != "m") + tuple(range(4, bits))
        if cuts not in orders:
            orders[cuts] = feature_order(features, cuts)
        return orders[cuts]

    order_of = {name: order_by(steps) for name, steps in HALVINGS.items()}
    x0 = enc_in.reshape(enc_rows, features)
    y0 = dec_in.reshape(dec_rows, features)
    top = cotangent.reshape(dec_rows, features)
    enc_wide, dec_wide = ((enc_rows, features), F32), ((dec_rows, features), F32)
    enc_low, dec_low = ((enc_rows, features), BF), ((dec_rows, features), BF)
    gain_row, gain_rows = ((1, features), F32), ((2, features), F32)
    quarter = half // 2
    line = Line()

    def tick(cost=TICK):
        line.call(tick_kernel, [((1, 128), F32)], [enc_gains], "tick", cost=cost)

    def parts_of(name, rows, width):
        count, tiles = PARTS[name], width // 128
        edges = [128 * (tiles * i // count) for i in range(count + 1)]
        return [((rows, high - low), F32) for low, high in zip(edges, edges[1:])]

    def swap_cores(name, parts):
        return [swap(part, 0, name) for part in parts]

    def group(columns):
        return [((quarter, columns), F32)] * 2

    def mlp_of(name):
        apart = name + "o" in HALVINGS
        target = (1, 0) if apart else (0, 2 * units)
        segments = (
            (0, half, half, 2 * units, 0, 0),
            (half + 2 * units, half, 2 * half + 2 * units, units) + target,
        )
        return segments, group(2 * units) + group(units) if apart else group(3 * units)

    attn_segments = (
        (0, half, half, 3 * heads, 0, 0),
        (half + 3 * heads, half, 2 * half + 3 * heads, heads, 0, 3 * heads),
    )
    base, fold_width = 2 * half + 2 * heads, half + 2 * heads
    folds = enc_rows // dec_rows
    cross_segments = (
        (0, half, half, heads, 0, 0),
        (half + heads, half, 2 * half + heads, heads, 0, heads),
    ) + tuple(
        (base + f * fold_width, half, base + f * fold_width + half, 2 * heads, 0, 2 * heads) for f in range(folds)
    )
    attn_group = group(4 * heads)
    mlp_wide = 2 * half + 3 * units
    attn_wide = 2 * half + 4 * heads
    cross_wide = base + folds * fold_width
    v, sums, grad_of = {}, {}, {}

    def pause():
        tick(6.0)

    def enc_attn(p):
        v["part_e1", p], v["enc_saved", p] = line.call(
            functools.partial(self_fwd_kernel, False, enc_len, p),
            [((enc_len, features), F32), ((enc_len, 4 * heads), BF)],
            [patch_counts, x0, enc_gains, enc_qkv, enc_attn_out], "enc_attn_fwd",
        )
        v["other_e1", p] = pair_other(v["part_e1", p], "e1")

    def dec_self():
        v["part_d1"], v["dec_saved"] = line.call(
            functools.partial(self_fwd_kernel, True, dec_len, 0),
            [dec_wide, ((dec_rows, 4 * heads), BF)],
            [table_lengths, y0, dec_gains, dec_self_qkv, dec_self_out], "dec_self_fwd",
        )
        v["other_d1"] = pair_other(v["part_d1"], "d1")

    def enc_mlp(p):
        v["part_e2", p], v["x1", p], v["pre", p] = line.call(
            functools.partial(enc_mlp_fwd_kernel, p),
            [((enc_len, features), F32), ((enc_len, features), F32), ((enc_len, 2 * units), F32)],
            [x0, v["part_e1", p], v["other_e1", p], enc_gains, enc_mlp_in, enc_mlp_out], "enc_mlp_fwd",
        )
        v["other_e2", p] = pair_other(v["part_e2", p], "e2")

    def cross(p):
        v["part_d2", p], v["states", p], v["saved", p] = line.call(
            functools.partial(cross_fwd_kernel, enc_len, p),
            [((dec_len, features), F32), ((enc_len + dec_len, features), F32), ((enc_len + dec_len, 2 * heads), BF)],
            [patch_counts, v["x1", p], v["part_e2", p], v["other_e2", p], enc_gains, y0, v["part_d1"], v["other_d1"],
             dec_gains, dec_cross_qkv, dec_cross_out],
            "cross_fwd",
        )
        v["other_d2", p] = pair_other(v["part_d2", p], "d2")

    def stack(name, first, last):
        return Stack(*[(v[name, p], first, last) for p in range(plots)])

    def enc_part(name):
        return stack(name, 0, enc_len)

    def dec_part(name):
        return stack(name, enc_len, enc_len + dec_len)

    def dec_mlp():
        v["part_g3"], v["y2"], send, v["keep_m"] = line.call(
            dec_mlp_kernel,
            [dec_wide, dec_wide, parts_of("m", dec_rows, mlp_wide), ((dec_rows, mlp_wide), BF)],
            [dec_part("states"), stack("part_d2", 0, dec_len), stack("other_d2", 0, dec_len), dec_gains, top,
             dec_mlp_in, dec_mlp_out, order_of["m"], order_of.get("mo", order_of["m"])],
            "dec_mlp",
        )
        v["other_g3"] = pair_other(v["part_g3"], "g3")
        v["recv_m"] = swap_cores("m", send)

    def start_sums(name, products):
        for group_name, pair in zip((name, name + "o"), zip(products[::2], products[1::2])):
            sums[group_name] = Halving(pair[0], pair[1], HALVINGS[group_name], group_name)

    def mlp_weights(name, keep, recv):
        segments, groups = mlp_of(name)
        start_sums(
            name, line.call(functools.partial(weight_kernel, segments), groups, [keep, recv], "weights_" + name)
        )

    def dec_mlp_weights():
        mlp_weights("m", v["keep_m"], v["recv_m"])

    def cross_back():
        v["part_m"], v["g2"], v["gain_dec_cross"], send, v["keep_c"] = line.call(
            functools.partial(cross_back_kernel, enc_len),
            [enc_wide, dec_wide, gain_row, parts_of("c", dec_rows, cross_wide), ((dec_rows, cross_wide), BF)],
            [patch_counts, v["part_g3"], v["other_g3"], v["y2"], dec_gains, top, dec_cross_out, dec_part("saved"),
             enc_part("saved"), dec_cross_qkv, order_of["c"], dec_part("states"), enc_part("states"), enc_gains],
            "cross_back", scratch=[pltpu.VMEM((enc_rows, 2 * heads), BF)],
        )
        v["other_m"] = pair_other(v["part_m"], "m")
        v["recv_c"] = swap_cores("c", send)

    def cross_weights():
        start_sums("c", line.call(
            functools.partial(weight_kernel, cross_segments), attn_group, [v["keep_c"], v["recv_c"]], "weights_c"
        ))

    def enc_mlp_back():
        v["part_g1"], v["back2"], v["gain_enc_mlp"], send, v["keep_f"] = line.call(
            enc_mlp_back_kernel,
            [enc_wide, enc_wide, gain_row, parts_of("f", enc_rows, mlp_wide), ((enc_rows, mlp_wide), BF)],
            [v["part_m"], v["other_m"], enc_part("states"), enc_gains, enc_mlp_out, enc_part("pre"), enc_mlp_in,
             order_of["f"], order_of.get("fo", order_of["f"]), enc_part("x1")],
            "enc_mlp_back",
        )
        v["other_g1"] = pair_other(v["part_g1"], "g1")
        v["recv_f"] = swap_cores("f", send)

    def enc_mlp_weights():
        mlp_weights("f", v["keep_f"], v["recv_f"])

    def enc_attn_back():
        v["part_ge"], v["back1"], v["gain_enc_attn"], send, v["keep_a"] = line.call(
            functools.partial(self_back_kernel, False, enc_len),
            [enc_wide, enc_wide, gain_rows, parts_of("a", enc_rows, attn_wide), ((enc_rows, attn_wide), BF)],
            [patch_counts, v["part_g1"], v["other_g1"], enc_part("x1"), enc_gains, v["back2"], enc_attn_out,
             enc_part("enc_saved"), enc_qkv, order_of["a"], x0],
            "enc_attn_back",
        )
        v["recv_a"] = swap_cores("a", send)

    def query_part():
        (v["part_q"],) = line.call(query_part_kernel, [dec_wide], [v["keep_c"], dec_cross_qkv], "query_part")
        v["other_q"] = pair_other(v["part_q"], "q")

    def dec_self_back():
        v["part_g0"], v["g1"], v["gain_dec_self"], send, v["keep_s"] = line.call(
            functools.partial(self_back_kernel, True, dec_len),
            [dec_wide, dec_wide, gain_rows, parts_of("s", dec_rows, attn_wide), ((dec_rows, attn_wide), BF)],
            [table_lengths, v["part_q"], v["other_q"], dec_part("states"), dec_gains, v["g2"], dec_self_out,
             v["dec_saved"], dec_self_qkv, order_of["s"], y0],
            "dec_self_back",
        )
        v["recv_s"] = swap_cores("s", send)

    def tail_parts():
        (v["part_tail"],) = line.call(
            tail_parts_kernel, [((enc_rows + 2 * dec_rows, features), F32)],
            [v["part_ge"], v["part_g0"], v["keep_m"], dec_mlp_out], "tail_parts",
        )
        v["other_tail"] = pair_other(v["part_tail"], "tail")

    def tail():
        v["enc_out"], v["dec_out_grad"], v["dec_out"] = line.call(
            tail_kernel, [enc_low, dec_low, dec_low],
            [v["part_tail"], v["other_tail"], x0, enc_gains, v["back1"], y0, dec_gains, v["g1"], v["y2"]], "tail",
        )

    def collect_gains():
        (v["gain_rows"],) = line.call(
            gain_rows_kernel, [((8, features), F32)],
            [v["gain_enc_attn"], v["gain_enc_mlp"], v["gain_dec_self"], v["gain_dec_cross"]], "gain_rows",
        )
        v["other_rows"] = pair_other(v["gain_rows"], "gains")

    def gains():
        send, v["keep_g"] = line.call(
            gains_kernel, [((half, 128), F32), ((half, 128), F32)],
            [v["gain_rows"], v["other_rows"], order_of[GAINS_WITH]], "gains",
        )
        v["recv_g"] = swap(send, 0, "g")

    def attn_weights(name):
        if name == GAINS_WITH:
            products = line.call(
                functools.partial(gains_weight_kernel, attn_segments), group(4 * heads + 128),
                [v["keep_" + name], v["recv_" + name], v["keep_g"], v["recv_g"]], "weights_" + name,
            )
        else:
            products = line.call(
                functools.partial(weight_kernel, attn_segments), attn_group,
                [v["keep_" + name], v["recv_" + name]], "weights_" + name,
            )
        start_sums(name, products)

    attn_pieces = ((0, (0, heads, 2 * heads), heads), (0, (3 * heads,), heads))
    ends = {"c": ((0, (0, 2 * heads, 3 * heads), heads), (0, (heads,), heads)), "a": attn_pieces, "s": attn_pieces}
    for name in ("m", "f"):
        outer = (1, (0,), units) if name + "o" in HALVINGS else (0, (2 * units,), units)
        ends[name] = ((0, (0, units), units), outer)
    ends[GAINS_WITH] += ((0, None, 0),)
    stages = {
        "tick": tick, "pause": pause, "dec_self": dec_self, "dec_mlp": dec_mlp, "w_m": dec_mlp_weights,
        "cross_back": cross_back, "w_c": cross_weights, "enc_mlp_back": enc_mlp_back,
        "w_f": enc_mlp_weights, "enc_attn_back": enc_attn_back, "query_part": query_part, "gains": gains, "gain_rows": collect_gains,
        "tail_parts": tail_parts, "tail": tail,
        "w_a": functools.partial(attn_weights, "a"), "dec_self_back": dec_self_back,
        "w_s": functools.partial(attn_weights, "s"),
    }
    for name, stage in (("enc_attn", enc_attn), ("enc_mlp", enc_mlp), ("cross", cross)):
        for p in range(plots):
            stages["%s_%d" % (name, p)] = functools.partial(stage, p)
    for stage in LINE:
        kind, _, name = stage.partition("_")
        if stage in stages:
            stages[stage]()
        elif kind == "h":
            sums[name].step(line)
        else:
            groups = [sums[part] for part in (name, name + "o") if part in sums]
            grad_of[name] = finish(line, groups, ends[name], name)
    gains_out = grad_of[GAINS_WITH][2:]
    grads = (
        grad_of["a"][0], grad_of["a"][1].T, grad_of["f"][0], grad_of["f"][1].T, gains_out[0],
        grad_of["s"][0], grad_of["s"][1].T, grad_of["c"][0], grad_of["c"][1].T, grad_of["m"][0], grad_of["m"][1].T,
        gains_out[1],
    )
    return (
        v["dec_out"].reshape(cotangent.shape),
        v["enc_out"].reshape(enc_in.shape),
        v["dec_out_grad"].reshape(dec_in.shape),
    ) + grads


def solution(mesh):
    rows = P("dp", None, None)
    inner, outer = P(None, None, "mp"), P("mp", None)
    enc = (inner, outer, inner, outer, P())
    dec = (inner, outer, inner, outer, inner, outer, P())
    inner_grad, outer_grad, gain_grad = P(None, "dp", "mp"), P("mp", "dp"), P(None, "dp")
    return jax.shard_map(
        body,
        mesh=mesh,
        in_specs=(rows, rows, rows, P("dp"), P("dp")) + enc + dec,
        out_specs=(rows, rows, rows)
        + (inner_grad, outer_grad) * 2 + (gain_grad,)
        + (inner_grad, outer_grad) * 3 + (gain_grad,),
        check_vma=False,
    )
```

```python
import functools

import jax
import jax.numpy as jnp
from jax import lax
from jax.experimental import pallas as pl
from jax.experimental.pallas import tpu as pltpu
from jax.sharding import PartitionSpec as P

HEAD_DIM = 64
PAIR = 2 * HEAD_DIM
EPSILON = 1e-06
NEG_LARGE = -1e30
SCALE = HEAD_DIM ** (-0.5)
BF = jnp.bfloat16
F32 = jnp.float32
MIB = 1024 * 1024


def mm(left, right):
    return jnp.dot(left, right, preferred_element_type=F32)


def mm_nt(left, right):
    return lax.dot_general(left, right, (((1,), (1,)), ((), ())), preferred_element_type=F32)


def mm_tn(left, right):
    return lax.dot_general(left, right, (((0,), (0,)), ((), ())), preferred_element_type=F32)


def scaled(hidden):
    return hidden * lax.rsqrt(jnp.mean(hidden * hidden, -1, keepdims=True) + EPSILON)


def norm(hidden, gain):
    return (scaled(hidden) * gain).astype(BF)


def norm_back(grad, hidden, gain):
    scaling = lax.rsqrt(jnp.mean(hidden * hidden, -1, keepdims=True) + EPSILON)
    normed = hidden * scaling
    grad_hat = grad * gain
    return scaling * (grad_hat - normed * jnp.mean(grad_hat * normed, -1, keepdims=True)), normed


def gain_part(part, normed):
    return jnp.sum(part * normed, 0, keepdims=True)


def gelu_parts(gate):
    slope = 0.7978845608028654
    square = gate * gate
    bent = jnp.tanh(slope * gate * (1.0 + 0.044715 * square))
    half = 0.5 * (1.0 + bent)
    value = gate * half
    rise = half + 0.5 * gate * (1.0 - bent * bent) * slope * (1.0 + 0.134145 * square)
    return value, rise


def stack_heads(pair):
    lane = lax.broadcasted_iota(jnp.int32, pair.shape, 1)
    zero = jnp.zeros_like(pair)
    return jnp.concatenate(
        [jnp.where(lane < HEAD_DIM, pair, zero), jnp.where(lane < HEAD_DIM, zero, pair)], 0
    )


def merge_heads(stacked):
    rows = stacked.shape[0] // 2
    lane = lax.broadcasted_iota(jnp.int32, (rows, PAIR), 1)
    return jnp.where(lane < HEAD_DIM, stacked[:rows], stacked[rows:])


def soft_of(stacked_query, keys, bias):
    scores = mm_nt(stacked_query, keys) * SCALE + bias
    expon = jnp.exp(scores - jnp.max(scores, -1, keepdims=True))
    return expon / jnp.sum(expon, -1, keepdims=True)


def pair_fwd(query, keys, values, bias):
    soft = soft_of(stack_heads(query), keys, bias)
    return merge_heads(mm(soft.astype(BF), values)).astype(BF)


def pair_back(query, keys, values, grad_out, bias):
    queries = stack_heads(query)
    soft = soft_of(queries, keys, bias)
    grads = stack_heads(grad_out)
    grad_values = mm_tn(soft.astype(BF), grads)
    grad_soft = mm_nt(grads, values)
    grad_scores = (
        soft * (grad_soft - jnp.sum(soft * grad_soft, -1, keepdims=True))
    ).astype(BF)
    grad_query = merge_heads(mm(grad_scores, keys)) * SCALE
    grad_keys = mm_tn(grad_scores, queries) * SCALE
    return grad_query.astype(BF), grad_keys.astype(BF), grad_values.astype(BF)


def length_bias(count, rows, length):
    col = lax.broadcasted_iota(jnp.int32, (2 * rows, length), 1)
    return jnp.where(col < count, 0.0, NEG_LARGE).astype(F32)


def causal_bias(counts, plots, length):
    shape = (plots * length, plots * length)
    row = lax.broadcasted_iota(jnp.int32, shape, 0)
    col = lax.broadcasted_iota(jnp.int32, shape, 1)
    bias = jnp.full(shape, NEG_LARGE, F32)
    for plot in range(plots):
        low = plot * length
        inside = (row >= low) & (row < low + length) & (col >= low)
        inside = inside & (col <= row) & (col < low + counts[plot])
        bias = jnp.where(inside, 0.0, bias)
    return jnp.concatenate([bias, bias], 0)


def pairs_of(width):
    return [slice(at, at + PAIR) for at in range(0, width, PAIR)]


def put(ref, at, value):
    last = at + value.shape[1]
    ref[:, at:last] = value.astype(ref.dtype)
    ref.flush(at, last)
    return last


def put_both(send, keep, at, value):
    put(send, at, value)
    return put(keep, at, value)


def put_cut(send, keep, at, value, order):
    ordered = mm(value, order[...])
    half = ordered.shape[1] // 2
    put(send, at, ordered[:, :half])
    return put(keep, at, ordered[:, half:])


def keys_of(causal, length, rows, counts, first=0):
    plots = rows // length
    if causal:
        return [(slice(0, rows), causal_bias(counts, plots, length))]
    return [
        (slice(p * length, (p + 1) * length), length_bias(counts[first + p], length, length)) for p in range(plots)
    ]


def self_fwd_kernel(causal, length, first, counts, state, gain, stacked, outer, part, saved):
    rows, width = part.shape[0], outer.shape[0]
    normed = norm(state[first * length : first * length + rows, :].astype(F32), gain[0:1, :])
    for which in range(3):
        put(saved, which * width, mm(normed, stacked[which]))
    for span, bias in keys_of(causal, length, rows, counts, first):
        for cols in pairs_of(width):
            mixed = slice(3 * width + cols.start, 3 * width + cols.stop)
            saved[span, mixed] = pair_fwd(
                saved[span, cols],
                saved[span, width + cols.start : width + cols.stop],
                saved[span, 2 * width + cols.start : 2 * width + cols.stop],
                bias,
            )
    part[...] = mm(saved[:, 3 * width :], outer[...])


def enc_mlp_fwd_kernel(first, state, own, other, gain, inner, outer, part, state_ref, pre):
    rows, width = part.shape[0], outer.shape[0]
    full = state[first * rows : (first + 1) * rows, :].astype(F32) + own[...] + other[...]
    state_ref[...] = full
    normed = norm(full, gain[1:2, :])
    step = 256
    total = None
    for at in range(0, width, step):
        cols = slice(at, at + step)
        gate = mm(normed, inner[0, :, cols])
        up = mm(normed, inner[1, :, cols])
        value, _ = gelu_parts(gate)
        pre[:, cols] = gate
        pre[:, width + at : width + at + step] = up
        add = mm((value * up).astype(BF), outer[cols, :])
        total = add if total is None else total + add
    part[...] = total


def cross_fwd_kernel(
    length, first, counts, enc_state, enc_own, enc_other, enc_gain, dec_state, dec_own, dec_other, dec_gain, stacked,
    outer, part, states, saved,
):
    rows, width = part.shape[0], outer.shape[0]
    span = slice(first * rows, (first + 1) * rows)
    dec_full = dec_state[span, :].astype(F32) + dec_own[span, :] + dec_other[span, :]
    states[length:, :] = dec_full
    normed = norm(dec_full, dec_gain[1:2, :])
    saved[length:, :width] = mm(normed, stacked[0]).astype(BF)
    enc_full = enc_state[...] + enc_own[...] + enc_other[...]
    states[:length, :] = enc_full
    memory = norm(enc_full, enc_gain[2:3, :])
    saved[:length, :width] = mm(memory, stacked[1]).astype(BF)
    saved[:length, width:] = mm(memory, stacked[2]).astype(BF)
    bias = length_bias(counts[first], rows, length)
    for cols in pairs_of(width):
        beside = slice(width + cols.start, width + cols.stop)
        saved[length:, beside] = pair_fwd(saved[length:, cols], saved[:length, cols], saved[:length, beside], bias)
    part[...] = mm(saved[length:, width:], outer[...])


def dec_mlp_kernel(
    state, own, other, gain, cotangent, inner, outer, order, order_outer, part, state_ref, send, keep
):
    full = state[...] + own[...] + other[...]
    state_ref[...] = full
    state_ref.flush()
    normed = norm(full, gain[2:3, :])
    low = cotangent[...]
    width, half = outer.shape[0], order.shape[0] // 2
    step = 256
    for col in range(0, width, step):
        cols = slice(col, col + step)
        gate = mm(normed, inner[0, :, cols])
        up = mm(normed, inner[1, :, cols])
        value, rise = gelu_parts(gate)
        grad_hidden = mm_nt(low, outer[cols, :])
        put_both(send, keep, half + col, (grad_hidden * up * rise).astype(BF))
        put_both(send, keep, half + width + col, (grad_hidden * value).astype(BF))
        put_both(send, keep, 2 * half + 2 * width + col, (value * up).astype(BF))
    part[...] = mm_nt(keep[:, half : half + width], inner[0]) + mm_nt(
        keep[:, half + width : half + 2 * width], inner[1]
    )
    part.flush()
    put_cut(send, keep, 0, normed, order)
    put_cut(send, keep, half + 2 * width, low, order_outer)


def tail_parts_kernel(enc_part, dec_part, keep, outer, part):
    enc_rows, dec_rows = enc_part.shape[0], dec_part.shape[0]
    part[:enc_rows, :] = enc_part[...]
    part[enc_rows : enc_rows + dec_rows, :] = dec_part[...]
    part[enc_rows + dec_rows :, :] = mm(keep[:, keep.shape[1] - outer.shape[0] :], outer[...])


def tail_kernel(own, other, enc_state, enc_gain, enc_grad, dec_state, dec_gain, dec_grad, state, enc_out, dec_out, out):
    enc_rows, dec_rows = enc_out.shape[0], dec_out.shape[0]
    span = slice(0, enc_rows)
    grad_in, _ = norm_back(own[span, :] + other[span, :], enc_state[...].astype(F32), enc_gain[0:1, :])
    enc_out[...] = (enc_grad[...] + grad_in).astype(BF)
    span = slice(enc_rows, enc_rows + dec_rows)
    grad_in, _ = norm_back(own[span, :] + other[span, :], dec_state[...].astype(F32), dec_gain[0:1, :])
    dec_out[...] = (dec_grad[...] + grad_in).astype(BF)
    span = slice(enc_rows + dec_rows, enc_rows + 2 * dec_rows)
    out[...] = (state[...] + own[span, :] + other[span, :]).astype(BF)


def query_part_kernel(keep, stacked, part):
    half = stacked.shape[1] // 2
    part[...] = mm_nt(keep[:, half : half + stacked.shape[2]], stacked[0])


def cross_back_kernel(
    length, counts, own, other, state, gain, grad, outer, query, kv, stacked, order, dec_state, enc_state, enc_gain,
    part, grad_ref, gain_ref, send, keep, key_grads,
):
    grad_in, normed = norm_back(own[...] + other[...], state[...], gain[2:3, :])
    gain_ref[...] = gain_part(own[...], normed)
    full = grad[...].astype(F32) + grad_in
    grad_ref[...] = full
    flush(gain_ref, grad_ref)
    low = full.astype(BF)
    width, half = outer.shape[0], order.shape[0] // 2
    grad_mixed = mm_nt(low, outer[...]).astype(BF)
    plots = kv.shape[0] // length
    rows = low.shape[0] // plots
    for plot in range(plots):
        bias = length_bias(counts[plot], rows, length)
        q_span = slice(plot * rows, (plot + 1) * rows)
        k_span = slice(plot * length, (plot + 1) * length)
        for cols in pairs_of(width):
            values = slice(width + cols.start, width + cols.stop)
            grad_query, grad_keys, grad_values = pair_back(
                query[q_span, cols], kv[k_span, cols], kv[k_span, values], grad_mixed[q_span, cols], bias
            )
            keep[q_span, half + cols.start : half + cols.stop] = grad_query
            send[q_span, half + cols.start : half + cols.stop] = grad_query.astype(F32)
            key_grads[k_span, cols] = grad_keys
            key_grads[k_span, values] = grad_values
    send.flush(half, half + width)
    keep.flush(half, half + width)
    part[...] = mm_nt(key_grads[:, :width], stacked[1]) + mm_nt(key_grads[:, width:], stacked[2])
    part.flush()
    put_cut(send, keep, 0, norm(dec_state[...], gain[1:2, :]), order)
    at = put_cut(send, keep, half + width, low, order)
    base = put_both(send, keep, at, query[:, width : 2 * width])
    ordered = mm(norm(enc_state[...], enc_gain[2:3, :]), order[...])
    for fold in range(kv.shape[0] // low.shape[0]):
        span = slice(fold * low.shape[0], (fold + 1) * low.shape[0])
        put(send, base, ordered[span, :half])
        put(keep, base, ordered[span, half:])
        base = put_both(send, keep, base + half, key_grads[span, :])


def self_back_kernel(
    causal, length, counts, own, other, state, gain, grad, outer, qkv, stacked, order, inputs,
    part, grad_ref, gain_ref, send, keep,
):
    grad_in, normed = norm_back(own[...] + other[...], state[...], gain[1:2, :])
    gain_ref[0:1, :] = gain_part(own[...], normed)
    full = grad[...] + grad_in
    grad_ref[...] = full
    flush(gain_ref, grad_ref)
    low = full.astype(BF)
    width, half = outer.shape[0], order.shape[0] // 2
    grad_mixed = mm_nt(low, outer[...]).astype(BF)
    for span, bias in keys_of(causal, length, low.shape[0], counts):
        for cols in pairs_of(width):
            grads = pair_back(
                qkv[span, cols],
                qkv[span, width + cols.start : width + cols.stop],
                qkv[span, 2 * width + cols.start : 2 * width + cols.stop],
                grad_mixed[span, cols],
                bias,
            )
            for which, piece in enumerate(grads):
                start = half + which * width + cols.start
                keep[span, start : start + PAIR] = piece
                send[span, start : start + PAIR] = piece.astype(F32)
    send.flush(half, half + 3 * width)
    keep.flush(half, half + 3 * width)
    total = mm_nt(keep[:, half : half + width], stacked[0])
    total += mm_nt(keep[:, half + width : half + 2 * width], stacked[1])
    total += mm_nt(keep[:, half + 2 * width : half + 3 * width], stacked[2])
    part[...] = total
    normed = scaled(inputs[...].astype(F32))
    gain_ref[1:2, :] = gain_part(total, normed)
    put_cut(send, keep, 0, (normed * gain[0:1, :]).astype(BF), order)
    at = put_cut(send, keep, half + 3 * width, low, order)
    put_both(send, keep, at, qkv[:, 3 * width : 4 * width])


def enc_mlp_back_kernel(
    own, other, state, gain, outer, pre, inner, order, order_outer, middle,
    part, grad_ref, gain_ref, send, keep,
):
    full, normed = norm_back(own[...] + other[...], state[...], gain[2:3, :])
    gain_ref[...] = gain_part(own[...], normed)
    grad_ref[...] = full
    flush(gain_ref, grad_ref)
    low = full.astype(BF)
    width, half = outer.shape[0], order.shape[0] // 2
    step = 256
    for col in range(0, width, step):
        cols = slice(col, col + step)
        value, rise = gelu_parts(pre[:, cols])
        up = pre[:, width + col : width + col + step]
        grad_hidden = mm_nt(low, outer[cols, :])
        put_both(send, keep, half + col, (grad_hidden * up * rise).astype(BF))
        put_both(send, keep, half + width + col, (grad_hidden * value).astype(BF))
        put_both(send, keep, 2 * half + 2 * width + col, (value * up).astype(BF))
    part[...] = mm_nt(keep[:, half : half + width], inner[0]) + mm_nt(
        keep[:, half + width : half + 2 * width], inner[1]
    )
    part.flush()
    put_cut(send, keep, 0, norm(middle[...], gain[1:2, :]), order)
    put_cut(send, keep, half + 2 * width, low, order_outer)


def gain_rows_kernel(enc_attn, enc_mlp, dec_self, dec_cross, out):
    for at, row in enumerate((enc_attn[1:2, :], enc_attn[0:1, :], enc_mlp[...], dec_self[1:2, :], dec_self[0:1, :],
                              dec_cross[...])):
        out[at : at + 1, :] = row
    out[6:8, :] = jnp.zeros((2, out.shape[1]), F32)


def gains_kernel(own, other, order, send, keep):
    rest = own[...] + other[...]
    rest = jnp.concatenate([rest, jnp.zeros((128 - rest.shape[0], rest.shape[1]), F32)], 0)
    total = None
    for _ in range(3):
        low = rest.astype(BF)
        rest = rest - low.astype(F32)
        moved = lax.dot_general(order[...], low, (((0,), (1,)), ((), ())), preferred_element_type=F32)
        total = moved if total is None else total + moved
    half = total.shape[0] // 2
    send[...] = total[:half]
    keep[...] = total[half:]


def gains_weight_kernel(segments, keep, recv, gains, other_gains, send_out, keep_out):
    weight_kernel(segments, keep, recv, send_out, keep_out)
    total = gains[...] + other_gains[...]
    half, first = send_out.shape[0], send_out.shape[1] - total.shape[1]
    send_out[:, first:] = total[:half]
    keep_out[:, first:] = total[half:]


def weight_kernel(segments, keep, recv, *outs):
    last_of = {(group, target): at for at, (_, _, _, _, group, target) in enumerate(segments)}
    started = set()
    for number, (cut, cut_width, first, columns, group, target) in enumerate(segments):
        send_out, keep_out = outs[2 * group], outs[2 * group + 1]
        left = jnp.concatenate([keep[:, cut : cut + cut_width], recv[:, cut : cut + cut_width].astype(BF)], 0)
        half = cut_width // 2
        step = 512 if columns % 512 == 0 else 384
        for at in range(0, columns, step):
            cols = slice(first + at, first + at + step)
            right = jnp.concatenate([keep[:, cols], recv[:, cols].astype(BF)], 0)
            total = mm_tn(left, right)
            into = slice(target + at, target + at + step)
            if (group, target) in started:
                total += jnp.concatenate([send_out[:, into], keep_out[:, into]], 0)
            send_out[:, into] = total[:half]
            keep_out[:, into] = total[half:]
            if last_of[group, target] == number:
                send_out.flush(into.start, into.stop)
                keep_out.flush(into.start, into.stop)
        started.add((group, target))


def halve_kernel(kept, recv, send_out, keep_out):
    rows = send_out.shape[0]
    send_out[...] = kept[:rows] + recv[:rows]
    send_out.flush()
    keep_out[...] = kept[rows:] + recv[rows:]


SMEM = pl.BlockSpec(memory_space=pltpu.SMEM)
VMEM = pl.BlockSpec(memory_space=pltpu.VMEM)
ANY = pl.BlockSpec(memory_space=pl.ANY)


COST = {
    "enc_attn_fwd": 2.3, "dec_self_fwd": 2.5, "enc_mlp_fwd": 1.7, "cross_fwd": 4.2, "dec_mlp": 2.7,
    "cross_back": 20.0, "weights_c": 1.0, "enc_mlp_back": 0.1, "enc_attn_back": 0.3, "query_part": 20.0,
    "weights_f": 1.0, "weights_a": 0.3, "dec_self_back": 3.0, "weights_s": 1.0, "tail_parts": 0.1,
    "tail": 1.0, "gains": 20.0, "gain_rows": 1.0, "halve_m": 20.0, "halve_mo": 0.3,
    "halve_c": 0.3, "halve_f": 3.0, "halve_fo": 0.3, "halve_s": 3.0, "halve_a": 8.0,
    "finish_m": 3.0, "finish_mo": 0.3, "finish_c": 3.0, "finish_f": 1.0, "finish_fo": 3.0,
    "finish_s": 1.0, "finish_a": 8.0, "weights_m": 0.1,
}
VMEM_LIMIT = 8

LINE = (
    "pause", "enc_attn_0", "enc_attn_1", "dec_self", "pause", "enc_mlp_0", "enc_mlp_1", "pause",
    "cross_0", "cross_1", "pause", "dec_mlp", "tick", "w_m", "cross_back", "h_mo",
    "w_c", "enc_mlp_back", "h_m", "query_part", "w_f", "h_mo", "h_mo", "h_c",
    "enc_attn_back", "dec_self_back", "h_fo", "gain_rows", "h_f", "gains", "w_s", "h_m",
    "h_c", "w_a", "h_fo", "h_f", "h_m", "tick", "tick", "h_c",
    "h_s", "h_fo", "h_a", "tail_parts", "e_c", "h_s", "h_f", "h_a",
    "e_f", "h_s", "tail", "h_a", "e_m", "e_s", "pause", "e_a",
)
HALVINGS = {"m": "pxme", "mo": "xpme", "c": "xpme", "f": "pxme", "fo": "xpme", "s": "pxme", "a": "xpme"}
PARTS = {"m": 1, "c": 3, "f": 1, "a": 1, "s": 1}
TICK = 0.1
GAINS_WITH = "a"


class Stored:
    def __init__(self, ref):
        self.ref = ref
        self.shape, self.dtype = ref.shape, ref.dtype

    def __getitem__(self, at):
        return self.ref[at]

    def __setitem__(self, at, value):
        self.ref[at] = value

    def flush(self, first=0, last=None):
        pass


class Columns:
    def __init__(self, refs):
        self.refs = refs
        self.shape = (refs[0].shape[0], sum(ref.shape[1] for ref in refs))
        self.dtype = refs[0].dtype

    def __getitem__(self, at):
        rows, cols = at
        first, last = cols.start or 0, self.shape[1] if cols.stop is None else cols.stop
        pieces, start = [], 0
        for ref in self.refs:
            low, high = max(first - start, 0), min(last - start, ref.shape[1])
            if low < high:
                pieces.append(ref[rows, low:high])
            start += ref.shape[1]
        return pieces[0] if len(pieces) == 1 else jnp.concatenate(pieces, 1)

    def __setitem__(self, at, value):
        rows, cols = at
        first, last = cols.start or 0, self.shape[1] if cols.stop is None else cols.stop
        start = 0
        for ref in self.refs:
            low, high = max(first - start, 0), min(last - start, ref.shape[1])
            if low < high:
                ref[rows, low:high] = value[:, low + start - first : high + start - first]
            start += ref.shape[1]

    def flush(self, first=0, last=None):
        pass


class Stack:
    def __init__(self, *parts):
        self.parts = parts


class Rows:
    def __init__(self, refs, spans):
        self.refs = [ref.at[first:last] if (first, last) != (0, ref.shape[0]) else ref
                     for ref, (first, last) in zip(refs, spans)]
        self.heights = [last - first for first, last in spans]
        self.shape = (sum(self.heights),) + tuple(refs[0].shape[1:])
        self.dtype = refs[0].dtype

    def __getitem__(self, at):
        rows, cols = (slice(None), slice(None)) if at is Ellipsis else at
        first, last, _ = rows.indices(self.shape[0])
        pieces, start = [], 0
        for ref, height in zip(self.refs, self.heights):
            low, high = max(first - start, 0), min(last - start, height)
            if low < high:
                pieces.append(ref[low:high, cols])
            start += height
        return pieces[0] if len(pieces) == 1 else jnp.concatenate(pieces, 0)


def flush(*refs):
    for ref in refs:
        ref.flush()


class Line:
    def __init__(self):
        self.last = None

    def call(self, kernel, outs, args, name, scratch=(), cost=None):
        spans = [[part[1:] for part in a.parts] if isinstance(a, Stack) else None for a in args]
        args = [[part[0] for part in a.parts] if isinstance(a, Stack) else a for a in args]
        flat_args, args_tree = jax.tree.flatten(list(args))
        widths = [out if isinstance(out, list) else [out] for out in outs]
        shapes = [jax.ShapeDtypeStruct(*out) for group in widths for out in group]
        in_specs = [VMEM if a.ndim > 1 else SMEM for a in flat_args]
        count, made = len(flat_args), len(shapes)
        operands = list(flat_args)
        if self.last is not None:
            operands.append(self.last)
            in_specs.append(ANY)
        total = len(operands)

        def run(*refs):
            ins = jax.tree.unflatten(args_tree, refs[:count])
            ins = [Rows(i, span) if span else Columns(i) if isinstance(i, list) else i for i, span in zip(ins, spans)]
            left = list(refs[total : total + made])
            results = []
            for group, out in zip(widths, outs):
                taken, left = [Stored(ref) for ref in left[: len(group)]], left[len(group) :]
                results.append(Columns(taken) if isinstance(out, list) else taken[0])
            kernel(*ins, *results, *refs[total + made :])

        cost = COST.get(name, 0.3) if cost is None else cost
        flat = pl.pallas_call(
            run,
            out_shape=shapes,
            in_specs=in_specs,
            out_specs=[VMEM] * made,
            scratch_shapes=list(scratch),
            compiler_params=pltpu.CompilerParams(vmem_limit_bytes=VMEM_LIMIT * MIB),
            cost_estimate=pl.CostEstimate(
                flops=int(cost * 1.15e9), bytes_accessed=int(cost * 3.69e6), transcendentals=0
            ),
            name=name,
        )(*operands)
        self.last = min(flat, key=lambda r: r.size)
        results, left = [], list(flat)
        for group, out in zip(widths, outs):
            results.append(left[: len(group)] if isinstance(out, list) else left[0])
            left = left[len(group) :]
        return results


def join_kernel(kept, recv, out):
    out[...] = kept[...] + recv[...]


def middle_kernel(kept, recv, send_out, keep_out):
    rows = send_out.shape[0]
    me = lax.axis_index("dp")
    inner = ((me >> 2) ^ (me >> 3)) & 1
    send_out[...] = jnp.where(inner == 1, recv[rows:], kept[:rows])
    keep_out[...] = jnp.where(inner == 1, recv[:rows], kept[rows:])


def finish_kernel(pieces, *refs):
    groups = 1 + max(group for group, _ in pieces)
    outs = refs[2 * groups :]
    at = 0
    for group, firsts in pieces:
        kept, recv = refs[2 * group], refs[2 * group + 1]
        if firsts is None:
            total = kept[:, -128:] + recv[:, -128:]
            rows = total.shape[0]
            total = jnp.concatenate([total, jnp.zeros((128 - rows, 128), F32)], 0).T
            outs[at][...] = total[0:3, :rows]
            outs[at + 1][...] = total[3:6, :rows]
            at += 2
            continue
        out = outs[at]
        at += 1
        for i, first in enumerate(firsts):
            cols = slice(first, first + out.shape[-1])
            total = kept[:, cols] + recv[:, cols]
            if len(firsts) > 1:
                out[i] = total
            else:
                out[...] = total


def tick_kernel(source, target):
    target[...] = source[0:1, 0:128]


def pair_other(part, name):
    with jax.named_scope("pair_" + name):
        return lax.ppermute(part, "mp", [(0, 1), (1, 0)])


def swap(value, step, name):
    shards = lax.axis_size("dp")
    bit = {"x": 1, "p": 2, "e": 2}.get(step, step)
    if step == "m":
        pairs = [(i, i ^ 12) for i in range(shards) if (i >> 2 ^ i >> 3) & 1]
    else:
        pairs = [(i, i ^ (1 << bit)) for i in range(shards)]
    with jax.named_scope("swap_%s_%s" % (name, step)):
        return lax.ppermute(value, "dp", pairs)


def feature_order(features, steps):
    shards = lax.axis_size("dp")
    me = lax.axis_index("dp")
    block = features // shards
    column = jnp.arange(features, dtype=jnp.int32)
    place = column // block
    owner = jnp.zeros_like(column)
    other = {step: 1 - ((place >> (len(steps) - 1 - at)) & 1) for at, step in enumerate(steps)}
    near = (me >> 2) & 1
    for step in steps:
        if step == "p":
            owner = owner | ((near ^ other["p"]) << 3)
        elif step == "e":
            owner = owner | ((near ^ other["e"] ^ other["p"]) << 2)
        else:
            bit = 1 if step == "x" else step
            owner = owner | ((((me >> bit) & 1) ^ other[step]) << bit)
    source = owner * block + column % block
    return (jnp.arange(features, dtype=jnp.int32)[:, None] == source[None, :]).astype(BF)


class Halving:
    def __init__(self, sent, kept, steps, name):
        self.steps, self.name, self.at = steps, name, 0
        self.kept = kept
        self.flying = swap(sent, steps[0], name)

    def step(self, line):
        came, self.at = self.steps[self.at], self.at + 1
        rows, columns = self.kept.shape
        args, name = [self.kept, self.flying], "halve_" + self.name
        if self.steps[self.at] == "m":
            (self.kept,) = line.call(join_kernel, [((rows, columns), F32)], args, name)
            sent = self.kept
        else:
            shape = ((rows // 2, columns), F32)
            sent, self.kept = line.call(middle_kernel if came == "m" else halve_kernel, [shape, shape], args, name)
        self.flying = swap(sent, self.steps[self.at], self.name)

    def last(self):
        for bit in range(4, lax.axis_size("dp").bit_length() - 1):
            rows = self.kept.shape[0] // 2
            total = self.kept + self.flying
            self.kept, self.flying = total[rows:], swap(total[:rows], bit, self.name)
        return [self.kept, self.flying]


def finish(line, groups, pieces, name):
    args = [array for group in groups for array in group.last()]
    rows = args[0].shape[0]
    outs = []
    for _, firsts, width in pieces:
        if firsts is None:
            outs += [((3, rows), F32)] * 2
        else:
            outs.append((((len(firsts), rows, width) if len(firsts) > 1 else (rows, width)), F32))
    kernel = functools.partial(finish_kernel, [(group, firsts) for group, firsts, _ in pieces])
    return line.call(kernel, outs, args, "finish_" + name)


def body(
    enc_in, dec_in, cotangent, patch_counts, table_lengths, enc_qkv, enc_attn_out, enc_mlp_in, enc_mlp_out, enc_gains,
    dec_self_qkv, dec_self_out, dec_cross_qkv, dec_cross_out, dec_mlp_in, dec_mlp_out, dec_gains,
):
    plots, enc_len, features = enc_in.shape
    dec_len = dec_in.shape[1]
    enc_rows, dec_rows = plots * enc_len, plots * dec_len
    heads = enc_attn_out.shape[0]
    units = enc_mlp_out.shape[0]
    half = features // 2
    bits = lax.axis_size("dp").bit_length() - 1
    orders = {}

    def order_by(steps):
        cuts = (0,) + tuple(step for step in steps if step != "m") + tuple(range(4, bits))
        if cuts not in orders:
            orders[cuts] = feature_order(features, cuts)
        return orders[cuts]

    order_of = {name: order_by(steps) for name, steps in HALVINGS.items()}
    x0 = enc_in.reshape(enc_rows, features)
    y0 = dec_in.reshape(dec_rows, features)
    top = cotangent.reshape(dec_rows, features)
    enc_wide, dec_wide = ((enc_rows, features), F32), ((dec_rows, features), F32)
    enc_low, dec_low = ((enc_rows, features), BF), ((dec_rows, features), BF)
    gain_row, gain_rows = ((1, features), F32), ((2, features), F32)
    quarter = half // 2
    line = Line()

    def tick(cost=TICK):
        line.call(tick_kernel, [((1, 128), F32)], [enc_gains], "tick", cost=cost)

    def parts_of(name, rows, width):
        count, tiles = PARTS[name], width // 128
        edges = [128 * (tiles * i // count) for i in range(count + 1)]
        return [((rows, high - low), F32) for low, high in zip(edges, edges[1:])]

    def swap_cores(name, parts):
        return [swap(part, 0, name) for part in parts]

    def group(columns):
        return [((quarter, columns), F32)] * 2

    def mlp_of(name):
        apart = name + "o" in HALVINGS
        target = (1, 0) if apart else (0, 2 * units)
        segments = (
            (0, half, half, 2 * units, 0, 0),
            (half + 2 * units, half, 2 * half + 2 * units, units) + target,
        )
        return segments, group(2 * units) + group(units) if apart else group(3 * units)

    attn_segments = (
        (0, half, half, 3 * heads, 0, 0),
        (half + 3 * heads, half, 2 * half + 3 * heads, heads, 0, 3 * heads),
    )
    base, fold_width = 2 * half + 2 * heads, half + 2 * heads
    folds = enc_rows // dec_rows
    cross_segments = (
        (0, half, half, heads, 0, 0),
        (half + heads, half, 2 * half + heads, heads, 0, heads),
    ) + tuple(
        (base + f * fold_width, half, base + f * fold_width + half, 2 * heads, 0, 2 * heads) for f in range(folds)
    )
    attn_group = group(4 * heads)
    mlp_wide = 2 * half + 3 * units
    attn_wide = 2 * half + 4 * heads
    cross_wide = base + folds * fold_width
    v, sums, grad_of = {}, {}, {}

    def pause():
        tick(6.0)

    def enc_attn(p):
        v["part_e1", p], v["enc_saved", p] = line.call(
            functools.partial(self_fwd_kernel, False, enc_len, p),
            [((enc_len, features), F32), ((enc_len, 4 * heads), BF)],
            [patch_counts, x0, enc_gains, enc_qkv, enc_attn_out], "enc_attn_fwd",
        )
        v["other_e1", p] = pair_other(v["part_e1", p], "e1")

    def dec_self():
        v["part_d1"], v["dec_saved"] = line.call(
            functools.partial(self_fwd_kernel, True, dec_len, 0),
            [dec_wide, ((dec_rows, 4 * heads), BF)],
            [table_lengths, y0, dec_gains, dec_self_qkv, dec_self_out], "dec_self_fwd",
        )
        v["other_d1"] = pair_other(v["part_d1"], "d1")

    def enc_mlp(p):
        v["part_e2", p], v["x1", p], v["pre", p] = line.call(
            functools.partial(enc_mlp_fwd_kernel, p),
            [((enc_len, features), F32), ((enc_len, features), F32), ((enc_len, 2 * units), F32)],
            [x0, v["part_e1", p], v["other_e1", p], enc_gains, enc_mlp_in, enc_mlp_out], "enc_mlp_fwd",
        )
        v["other_e2", p] = pair_other(v["part_e2", p], "e2")

    def cross(p):
        v["part_d2", p], v["states", p], v["saved", p] = line.call(
            functools.partial(cross_fwd_kernel, enc_len, p),
            [((dec_len, features), F32), ((enc_len + dec_len, features), F32), ((enc_len + dec_len, 2 * heads), BF)],
            [patch_counts, v["x1", p], v["part_e2", p], v["other_e2", p], enc_gains, y0, v["part_d1"], v["other_d1"],
             dec_gains, dec_cross_qkv, dec_cross_out],
            "cross_fwd",
        )
        v["other_d2", p] = pair_other(v["part_d2", p], "d2")

    def stack(name, first, last):
        return Stack(*[(v[name, p], first, last) for p in range(plots)])

    def enc_part(name):
        return stack(name, 0, enc_len)

    def dec_part(name):
        return stack(name, enc_len, enc_len + dec_len)

    def dec_mlp():
        v["part_g3"], v["y2"], send, v["keep_m"] = line.call(
            dec_mlp_kernel,
            [dec_wide, dec_wide, parts_of("m", dec_rows, mlp_wide), ((dec_rows, mlp_wide), BF)],
            [dec_part("states"), stack("part_d2", 0, dec_len), stack("other_d2", 0, dec_len), dec_gains, top,
             dec_mlp_in, dec_mlp_out, order_of["m"], order_of.get("mo", order_of["m"])],
            "dec_mlp",
        )
        v["other_g3"] = pair_other(v["part_g3"], "g3")
        v["recv_m"] = swap_cores("m", send)

    def start_sums(name, products):
        for group_name, pair in zip((name, name + "o"), zip(products[::2], products[1::2])):
            sums[group_name] = Halving(pair[0], pair[1], HALVINGS[group_name], group_name)

    def mlp_weights(name, keep, recv):
        segments, groups = mlp_of(name)
        start_sums(
            name, line.call(functools.partial(weight_kernel, segments), groups, [keep, recv], "weights_" + name)
        )

    def dec_mlp_weights():
        mlp_weights("m", v["keep_m"], v["recv_m"])

    def cross_back():
        v["part_m"], v["g2"], v["gain_dec_cross"], send, v["keep_c"] = line.call(
            functools.partial(cross_back_kernel, enc_len),
            [enc_wide, dec_wide, gain_row, parts_of("c", dec_rows, cross_wide), ((dec_rows, cross_wide), BF)],
            [patch_counts, v["part_g3"], v["other_g3"], v["y2"], dec_gains, top, dec_cross_out, dec_part("saved"),
             enc_part("saved"), dec_cross_qkv, order_of["c"], dec_part("states"), enc_part("states"), enc_gains],
            "cross_back", scratch=[pltpu.VMEM((enc_rows, 2 * heads), BF)],
        )
        v["other_m"] = pair_other(v["part_m"], "m")
        v["recv_c"] = swap_cores("c", send)

    def cross_weights():
        start_sums("c", line.call(
            functools.partial(weight_kernel, cross_segments), attn_group, [v["keep_c"], v["recv_c"]], "weights_c"
        ))

    def enc_mlp_back():
        v["part_g1"], v["back2"], v["gain_enc_mlp"], send, v["keep_f"] = line.call(
            enc_mlp_back_kernel,
            [enc_wide, enc_wide, gain_row, parts_of("f", enc_rows, mlp_wide), ((enc_rows, mlp_wide), BF)],
            [v["part_m"], v["other_m"], enc_part("states"), enc_gains, enc_mlp_out, enc_part("pre"), enc_mlp_in,
             order_of["f"], order_of.get("fo", order_of["f"]), enc_part("x1")],
            "enc_mlp_back",
        )
        v["other_g1"] = pair_other(v["part_g1"], "g1")
        v["recv_f"] = swap_cores("f", send)

    def enc_mlp_weights():
        mlp_weights("f", v["keep_f"], v["recv_f"])

    def enc_attn_back():
        v["part_ge"], v["back1"], v["gain_enc_attn"], send, v["keep_a"] = line.call(
            functools.partial(self_back_kernel, False, enc_len),
            [enc_wide, enc_wide, gain_rows, parts_of("a", enc_rows, attn_wide), ((enc_rows, attn_wide), BF)],
            [patch_counts, v["part_g1"], v["other_g1"], enc_part("x1"), enc_gains, v["back2"], enc_attn_out,
             enc_part("enc_saved"), enc_qkv, order_of["a"], x0],
            "enc_attn_back",
        )
        v["recv_a"] = swap_cores("a", send)

    def query_part():
        (v["part_q"],) = line.call(query_part_kernel, [dec_wide], [v["keep_c"], dec_cross_qkv], "query_part")
        v["other_q"] = pair_other(v["part_q"], "q")

    def dec_self_back():
        v["part_g0"], v["g1"], v["gain_dec_self"], send, v["keep_s"] = line.call(
            functools.partial(self_back_kernel, True, dec_len),
            [dec_wide, dec_wide, gain_rows, parts_of("s", dec_rows, attn_wide), ((dec_rows, attn_wide), BF)],
            [table_lengths, v["part_q"], v["other_q"], dec_part("states"), dec_gains, v["g2"], dec_self_out,
             v["dec_saved"], dec_self_qkv, order_of["s"], y0],
            "dec_self_back",
        )
        v["recv_s"] = swap_cores("s", send)

    def tail_parts():
        (v["part_tail"],) = line.call(
            tail_parts_kernel, [((enc_rows + 2 * dec_rows, features), F32)],
            [v["part_ge"], v["part_g0"], v["keep_m"], dec_mlp_out], "tail_parts",
        )
        v["other_tail"] = pair_other(v["part_tail"], "tail")

    def tail():
        v["enc_out"], v["dec_out_grad"], v["dec_out"] = line.call(
            tail_kernel, [enc_low, dec_low, dec_low],
            [v["part_tail"], v["other_tail"], x0, enc_gains, v["back1"], y0, dec_gains, v["g1"], v["y2"]], "tail",
        )

    def collect_gains():
        (v["gain_rows"],) = line.call(
            gain_rows_kernel, [((8, features), F32)],
            [v["gain_enc_attn"], v["gain_enc_mlp"], v["gain_dec_self"], v["gain_dec_cross"]], "gain_rows",
        )
        v["other_rows"] = pair_other(v["gain_rows"], "gains")

    def gains():
        send, v["keep_g"] = line.call(
            gains_kernel, [((half, 128), F32), ((half, 128), F32)],
            [v["gain_rows"], v["other_rows"], order_of[GAINS_WITH]], "gains",
        )
        v["recv_g"] = swap(send, 0, "g")

    def attn_weights(name):
        if name == GAINS_WITH:
            products = line.call(
                functools.partial(gains_weight_kernel, attn_segments), group(4 * heads + 128),
                [v["keep_" + name], v["recv_" + name], v["keep_g"], v["recv_g"]], "weights_" + name,
            )
        else:
            products = line.call(
                functools.partial(weight_kernel, attn_segments), attn_group,
                [v["keep_" + name], v["recv_" + name]], "weights_" + name,
            )
        start_sums(name, products)

    attn_pieces = ((0, (0, heads, 2 * heads), heads), (0, (3 * heads,), heads))
    ends = {"c": ((0, (0, 2 * heads, 3 * heads), heads), (0, (heads,), heads)), "a": attn_pieces, "s": attn_pieces}
    for name in ("m", "f"):
        outer = (1, (0,), units) if name + "o" in HALVINGS else (0, (2 * units,), units)
        ends[name] = ((0, (0, units), units), outer)
    ends[GAINS_WITH] += ((0, None, 0),)
    stages = {
        "tick": tick, "pause": pause, "dec_self": dec_self, "dec_mlp": dec_mlp, "w_m": dec_mlp_weights,
        "cross_back": cross_back, "w_c": cross_weights, "enc_mlp_back": enc_mlp_back,
        "w_f": enc_mlp_weights, "enc_attn_back": enc_attn_back, "query_part": query_part, "gains": gains, "gain_rows": collect_gains,
        "tail_parts": tail_parts, "tail": tail,
        "w_a": functools.partial(attn_weights, "a"), "dec_self_back": dec_self_back,
        "w_s": functools.partial(attn_weights, "s"),
    }
    for name, stage in (("enc_attn", enc_attn), ("enc_mlp", enc_mlp), ("cross", cross)):
        for p in range(plots):
            stages["%s_%d" % (name, p)] = functools.partial(stage, p)
    for stage in LINE:
        kind, _, name = stage.partition("_")
        if stage in stages:
            stages[stage]()
        elif kind == "h":
            sums[name].step(line)
        else:
            groups = [sums[part] for part in (name, name + "o") if part in sums]
            grad_of[name] = finish(line, groups, ends[name], name)
    gains_out = grad_of[GAINS_WITH][2:]
    grads = (
        grad_of["a"][0], grad_of["a"][1].T, grad_of["f"][0], grad_of["f"][1].T, gains_out[0],
        grad_of["s"][0], grad_of["s"][1].T, grad_of["c"][0], grad_of["c"][1].T, grad_of["m"][0], grad_of["m"][1].T,
        gains_out[1],
    )
    return (
        v["dec_out"].reshape(cotangent.shape),
        v["enc_out"].reshape(enc_in.shape),
        v["dec_out_grad"].reshape(dec_in.shape),
    ) + grads


def solution(mesh):
    rows = P("dp", None, None)
    inner, outer = P(None, None, "mp"), P("mp", None)
    enc = (inner, outer, inner, outer, P())
    dec = (inner, outer, inner, outer, inner, outer, P())
    inner_grad, outer_grad, gain_grad = P(None, "dp", "mp"), P("mp", "dp"), P(None, "dp")
    return jax.shard_map(
        body,
        mesh=mesh,
        in_specs=(rows, rows, rows, P("dp"), P("dp")) + enc + dec,
        out_specs=(rows, rows, rows)
        + (inner_grad, outer_grad) * 2 + (gain_grad,)
        + (inner_grad, outer_grad) * 3 + (gain_grad,),
        check_vma=False,
    )
```
